32 devices in a mesh: groups: 2 (over y), tp: 4 (over x, core), req: 4 (over z).
Axes of the slice: x: 2, y: 2, z: 4, core: 2. Of those that a mesh axis runs over, the one named last changes fastest.
Arguments:
- queries: bfloat16 [32, 8192], P(('groups', 'tp', 'req')), parts along dimension 0, may hold values from -6 to 6
- new_kv: bfloat16 [32, 1024], P(('groups', 'tp', 'req')), parts along dimension 0, may hold values from -8 to 8
- cache_pool: bfloat16 [8, 4, 6, 4, 128, 256], P(('groups', 'tp'), 'req'), parts along dimension 0, may hold values from -210 to 210
- page_slot: int32 [8, 4, 7], P(('groups', 'tp')), parts along dimension 0, may hold values from 0 to 5, as said below
- page_owner: int32 [8, 4, 7], P(('groups', 'tp')), parts along dimension 0, may hold values from 0 to 3, as said below
- context_len: int32 [8, 4], P(('groups', 'tp')), parts along dimension 0, may hold values from 1 to 896, as said below
- out_weight: bfloat16 [8192, 16384], P('tp', 'req'), may hold values from -0.0625 to 0.0625
Outputs:
- mixed: bfloat16 [32, 16384], P(('groups', 'tp'), 'req'), parts along dimension 0
The draws below stay inside these ranges and needn't reach their ends.
There are 2 independent parts, one for each index of `groups`. The reference program is written for one: setup_inputs(seed, part) draws one part's arguments, and reference() takes and returns one part's arrays. A program takes and returns all parts, laid end to end along the dimension named above; an argument that names none is the same for every part. Nothing has to cross between parts.
Inputs may be any that keep to these rules, and one draw needn't show every extreme that they name: `page_owner`: the pool holding page j: a request's first pages are held by its own device, each later live page by a different other device; entries past the live pages name the request's own device; in each column some request has a page on every other device. `page_slot`: the page's slot in that pool; no slot holds two live pages. `context_len`: a request has ceil(length / 128) live pages; in each column some request is exactly 896 tokens long.
All inputs are finite; a program needn't handle non-finite values.
Results may differ from the reference program's by a relative error of at most 0.0051.
Values may be sent and summed in bfloat16 or wider, within the bound.
No kernel may reach another device: no remote copies, remote signals or barrier semaphores. Data moves between devices by JAX's collectives and lax.ppermute only.
A program may use at most 64 MiB of HBM per device.

```python
import math
import jax
import jax.numpy as jnp
from jax import lax

D = 16384
HQ = 64
KVH = 4
HD = 128
PAGE = 128
RESIDENT = 4
SWAP_PEERS = 1
POOL = 6
MAXP = 7
ROWS = 16
N_TP = 4
N_REQ = 4


def layout_tables(key):

    def one_column(column_key):
        subkeys = jax.random.split(column_key, 5)
        offsets = jax.random.permutation(subkeys[0], N_REQ - 1)[:SWAP_PEERS] + 1
        hub_index = jax.random.randint(subkeys[1], (), 0, N_REQ)
        source_ids = jnp.arange(N_REQ, dtype=jnp.int32)[:, None]
        target_ids = jnp.arange(N_REQ, dtype=jnp.int32)[None, :]
        offset_gap = (source_ids - target_ids) % N_REQ
        regular = jnp.any(offset_gap[..., None] == offsets[None, None, :], axis=-1)
        send_table = jnp.where(target_ids == hub_index, source_ids != hub_index, regular).astype(jnp.int32)
        request_ids = jnp.arange(N_REQ, dtype=jnp.int32)
        resident = jnp.where(request_ids == hub_index, RESIDENT, jax.random.randint(subkeys[2], (N_REQ,), 1, RESIDENT + 1))
        incoming = jnp.sum(send_table, axis=0)
        page_count = resident + incoming
        slot_order = jax.vmap(lambda one_key: jax.random.permutation(one_key, POOL))(jax.random.split(subkeys[3], N_REQ)).astype(jnp.int32)
        send_rank = jnp.cumsum(send_table, axis=1) - send_table
        seen_count = jnp.cumsum(send_table, axis=0)
        entry_ids = jnp.arange(MAXP, dtype=jnp.int32)[None, :]
        swapped = entry_ids - resident[:, None]
        owner_swap = jnp.sum((seen_count.T[:, None, :] <= swapped[:, :, None]).astype(jnp.int32), axis=-1)
        owner_swap = jnp.minimum(owner_swap, N_REQ - 1)
        is_resident = entry_ids < resident[:, None]
        is_swapped = jnp.logical_not(is_resident) & (entry_ids < page_count[:, None])
        mine = request_ids[:, None]
        owner = jnp.where(is_swapped, owner_swap, mine)
        rank_at = send_rank[owner_swap, mine]
        slot_swap = slot_order[owner_swap, jnp.minimum(RESIDENT + rank_at, POOL - 1)]
        slot_home = slot_order[mine, jnp.minimum(entry_ids, POOL - 1)]
        slot = jnp.where(is_swapped, slot_swap, jnp.where(is_resident, slot_home, slot_order[mine, 0]))
        last_fill = jax.random.randint(subkeys[4], (N_REQ,), 1, PAGE + 1)
        length = jnp.where(request_ids == hub_index, page_count * PAGE, (page_count - 1) * PAGE + last_fill)
        return (owner.astype(jnp.int32), slot.astype(jnp.int32), length.astype(jnp.int32))
    column_keys = jax.random.split(key, N_TP)
    return jax.vmap(one_column)(column_keys)


def draw_page_owner(key, part):
    return layout_tables(key)[0]


def draw_page_slot(key, part):
    return layout_tables(key)[1]


def draw_context_len(key, part):
    return layout_tables(key)[2]


def draw_cache_pool(key, part):
    key = jax.random.fold_in(key, 7)
    subkeys = jax.random.split(key, 1)
    pool_shape = (N_TP, N_REQ, POOL, KVH, PAGE, 2 * HD)
    base_draw = jax.random.normal(subkeys[0], pool_shape, jnp.float32) * 2.0
    return jnp.clip(base_draw, -8.0, 8.0).astype(jnp.bfloat16)


def levels(stream_key, dims, shards, least, high):
    loudness, own = 1.0, jax.random.fold_in(stream_key, 6)
    for axis_at, parts in shards:
        draws = jnp.exp(jax.random.uniform(jax.random.fold_in(own, axis_at), (parts,), jnp.float32, least / len(shards), high / len(shards)))
        loudness = loudness * jnp.repeat(draws, dims[axis_at] // parts).reshape([-1 if axis == axis_at else 1 for axis in range(len(dims))])
    return loudness


def bell_draw(rng, dims, deviation, most, shards=(), kind=jnp.bfloat16):
    result = deviation * jax.random.normal(rng, dims, jnp.float32)
    if shards:
        result = result * levels(rng, dims, shards, -0.22, 0.18)
    return jnp.clip(result, -most, most).astype(kind)


def setup_inputs(seed: int = 0, part: int = 0) -> dict:
    streams_of = jax.random.split(jax.random.key(seed), 8)
    own_keys = jax.random.split(jax.random.fold_in(streams_of[7], part), 8)
    queries = bell_draw(own_keys[0], (ROWS, HQ * HD), 1.0, 6.0, ((0, 16),))
    new_kv = bell_draw(own_keys[1], (ROWS, 2 * KVH * HD), 2.0, 8.0, ((0, 16),))
    cache_pool = draw_cache_pool(jax.random.fold_in(jax.random.fold_in(streams_of[7], part), 71), part)
    page_slot = draw_page_slot(jax.random.fold_in(jax.random.fold_in(streams_of[7], part), 71), part)
    page_owner = draw_page_owner(jax.random.fold_in(jax.random.fold_in(streams_of[7], part), 71), part)
    context_len = draw_context_len(jax.random.fold_in(jax.random.fold_in(streams_of[7], part), 71), part)
    out_weight = bell_draw(streams_of[6], (HQ * HD, D), (HQ * HD) ** -0.5, 0.0625, ((0, 4), (1, 4)))
    return {"queries": queries, "new_kv": new_kv, "cache_pool": cache_pool, "page_slot": page_slot, "page_owner": page_owner, "context_len": context_len, "out_weight": out_weight}


very_negative = -1e+30

def page_parts(grouped, page_data, valid_mask):
    head_dim = grouped.shape[-1]
    key_part = page_data[..., :head_dim].astype(jnp.float32)
    values = page_data[..., head_dim:].astype(jnp.float32)
    scores = jnp.einsum('phgd,phid->phgi', grouped.astype(jnp.float32), key_part, precision=lax.Precision.HIGHEST) / math.sqrt(head_dim)
    token_mask = valid_mask[:, None, None, :]
    masked = jnp.where(token_mask, scores, very_negative)
    page_max = lax.optimization_barrier(jnp.max(masked, axis=-1))
    weights = jnp.where(token_mask, jnp.exp(masked - page_max[..., None]), 0.0)
    page_total = lax.optimization_barrier(jnp.sum(weights, axis=-1))
    rounded = lax.optimization_barrier(weights.astype(jnp.bfloat16)).astype(jnp.float32)
    page_sum = jnp.einsum('phgi,phid->phgd', rounded, values, precision=lax.Precision.HIGHEST)
    return (page_max, page_total, page_sum)

def combine(page_max, page_total, page_sum, self_score, self_value):
    top_score = jnp.maximum(lax.optimization_barrier(jnp.max(page_max, axis=0)), self_score)
    factor = jnp.exp(page_max - top_score)
    own_factor = jnp.exp(self_score - top_score)
    numerator = lax.optimization_barrier(jnp.sum(factor[..., None] * page_sum, axis=0)) + own_factor[..., None] * self_value[:, None, :]
    denominator = lax.optimization_barrier(jnp.sum(factor * page_total, axis=0)) + own_factor
    return numerator / denominator[..., None]

def reference(queries, new_kv, cache_pool, page_slot, page_owner, context_len, out_weight):
    row_count = queries.shape[0]
    flat_pool = cache_pool.reshape((-1,) + cache_pool.shape[3:])
    slot_rows = page_slot.reshape(row_count, MAXP).astype(jnp.int32)
    owner_rows = page_owner.reshape(row_count, MAXP).astype(jnp.int32)
    length_rows = context_len.reshape(row_count).astype(jnp.int32)
    position = jnp.arange(MAXP * PAGE, dtype=jnp.int32).reshape(MAXP, PAGE)

    def attend_row(row_index):
        column = row_index // N_REQ
        flat_index = (column * N_REQ + owner_rows[row_index]) * POOL + slot_rows[row_index]
        page_data = flat_pool[flat_index]
        valid_mask = position < length_rows[row_index]
        grouped = queries[row_index].reshape(KVH, HQ // KVH, HD)
        fresh_kv = new_kv[row_index].astype(jnp.float32).reshape(2, KVH, HD)
        spread = jnp.broadcast_to(grouped, (MAXP,) + grouped.shape)
        page_max, page_total, page_sum = page_parts(spread, page_data, valid_mask)
        self_score = jnp.einsum('hgd,hd->hg', grouped.astype(jnp.float32), fresh_kv[0], precision=lax.Precision.HIGHEST) / math.sqrt(HD)
        attention = combine(page_max, page_total, page_sum, self_score, fresh_kv[1])
        return attention.astype(jnp.bfloat16)
    attention = lax.map(attend_row, jnp.arange(row_count, dtype=jnp.int32))
    attention = attention.reshape(row_count, HQ * HD)
    return jnp.dot(attention, out_weight, preferred_element_type=jnp.float32).astype(jnp.bfloat16)
```

```python
import functools
import math

import jax
import jax.numpy as jnp
from jax import lax
from jax.experimental import pallas as pl
from jax.experimental.pallas import tpu as pltpu
from jax.sharding import PartitionSpec as P

very_negative = -1e30
MIB = 1 << 20


def swap(x, axis, offset):
    count = lax.axis_size(axis)
    return lax.ppermute(x, axis, [(i, i ^ offset) for i in range(count)])


def round_up(value, step):
    return -(-value // step) * step


def attend_kernel(n_req, n_tp, *refs):
    q_refs = refs[:n_req]
    kv_ref, slot_ref, owner_ref, len_ref, pool_ref = refs[n_req : n_req + 5]
    out_refs = refs[n_req + 5 : n_req + 5 + n_tp]
    q_all, request_of, page_of, acc_all = refs[n_req + 5 + n_tp :]
    pool, kv_heads, page_len, width = pool_ref.shape
    head_dim = width // 2
    heads = q_refs[0].shape[0]
    group = heads // kv_heads
    chunk = heads // n_tp
    entries = slot_ref.shape[2]
    me = lax.axis_index("req")
    my_tp = lax.axis_index("tp")
    scale = 1.0 / math.sqrt(head_dim)

    for s in range(pool + 1):
        request_of[s] = -1
        page_of[s] = 0

    def enter(n, carry):
        length = len_ref[0, n]
        for j in range(entries):
            held = (owner_ref[0, n, j] == me) & (j * page_len < length)
            s = jnp.where(held, slot_ref[0, n, j], pool)
            request_of[s] = n
            page_of[s] = j
        return carry

    lax.fori_loop(0, n_req, enter, 0)

    for d in range(n_req):
        q_all[d] = q_refs[d][...]
    acc_all[...] = jnp.zeros_like(acc_all)
    token = lax.broadcasted_iota(jnp.int32, (group, page_len), 1)
    lane = lax.broadcasted_iota(jnp.int32, (heads, 128), 1)
    stat = jnp.full((heads, 128), very_negative, jnp.float32)

    own_q = q_all[0].astype(jnp.float32)
    new_k = jnp.concatenate(
        [jnp.broadcast_to(kv_ref[0:1, h * head_dim : (h + 1) * head_dim], (group, head_dim)) for h in range(kv_heads)], axis=0
    ).astype(jnp.float32)
    base = kv_heads * head_dim
    new_v = jnp.concatenate(
        [
            jnp.broadcast_to(kv_ref[0:1, base + h * head_dim : base + (h + 1) * head_dim], (group, head_dim))
            for h in range(kv_heads)
        ],
        axis=0,
    ).astype(jnp.float32)
    self_score = jnp.sum(own_q * new_k, axis=1, keepdims=True) * scale

    own_max, own_total, own_sum = [], [], []
    for s in range(pool):
        n = request_of[s]
        live = (n >= 0) & (s >= 0)
        nn = jnp.maximum(n, 0)
        valid = jnp.where(live, len_ref[0, nn] - page_of[s] * page_len, 0)
        mask = token < valid
        q = q_all[jnp.where(live, nn ^ me, 0)]
        maxes, totals, sums = [], [], []
        for h in range(kv_heads):
            scores = lax.dot_general(
                q[h * group : (h + 1) * group],
                pool_ref[s, h, :, :head_dim],
                (((1,), (1,)), ((), ())),
                preferred_element_type=jnp.float32,
            )
            masked = jnp.where(mask, scores * scale, very_negative)
            top = jnp.max(masked, axis=1, keepdims=True)
            weights = jnp.where(mask, jnp.exp(masked - top), 0.0)
            maxes.append(top)
            totals.append(jnp.sum(weights, axis=1, keepdims=True))
            sums.append(
                jnp.dot(
                    weights.astype(jnp.bfloat16), pool_ref[s, h, :, head_dim:], preferred_element_type=jnp.float32
                )
            )
        page_max = jnp.concatenate(maxes, axis=0)
        page_total = jnp.concatenate(totals, axis=0)
        page_sum = jnp.concatenate(sums, axis=0)
        other = live & (n != me)
        target = jnp.where(other, nn, me)
        safe_total = jnp.where(page_total > 0.0, page_total, 1.0)
        result = page_sum / safe_total
        logsum = page_max + jnp.log(safe_total)
        for c in range(n_tp):
            acc_all[c, target] = result[c * chunk : (c + 1) * chunk]
        stat = jnp.where(lane == target, logsum, stat)
        mine = live & (n == me)
        own_max.append(jnp.where(mine, page_max, very_negative))
        own_total.append(jnp.where(mine, page_total, 0.0))
        own_sum.append(page_sum)

    top = self_score
    for page_max in own_max:
        top = jnp.maximum(top, page_max)
    factor = jnp.exp(self_score - top)
    total = factor
    numerator = factor * new_v
    for page_max, page_total, page_sum in zip(own_max, own_total, own_sum):
        factor = jnp.exp(page_max - top)
        total = total + factor * page_total
        factor = jnp.where(page_total > 0.0, factor, 0.0)
        numerator = numerator + factor * page_sum
    result = numerator / total
    logsum = top + jnp.log(total)
    for c in range(n_tp):
        acc_all[c, me] = result[c * chunk : (c + 1) * chunk]
    stat = jnp.where(lane == me, logsum, stat)

    padded = stat
    if heads < 128:
        padded = jnp.concatenate([stat, jnp.zeros((128 - heads, 128), jnp.float32)], axis=0)
    turned = padded.T[: round_up(n_req, 8)]
    rows = n_req * chunk
    stat_rows = out_refs[0].shape[0] - rows
    high = turned.astype(jnp.bfloat16).astype(jnp.float32)
    rest = turned - high
    middle = rest.astype(jnp.bfloat16).astype(jnp.float32)
    low = rest - middle
    split = jnp.concatenate([high, middle, low], axis=0)
    if split.shape[0] < stat_rows:
        split = jnp.concatenate([split, jnp.zeros((stat_rows - split.shape[0], 128), jnp.float32)], axis=0)
    for d in range(n_tp):
        c = my_tp ^ d
        out_refs[d][:rows] = acc_all[c].reshape(rows, 128).astype(jnp.bfloat16)
        turned_to = pltpu.roll(split, (128 - c * chunk) % 128, 1)
        out_refs[d][rows:] = turned_to.astype(jnp.bfloat16)


def attend(q_list, new_kv, page_slot, page_owner, context_len, pool, n_req, n_tp):
    heads, head_dim = q_list[0].shape
    chunk = heads // n_tp
    rows = n_req * chunk
    stat_rows = round_up(3 * round_up(n_req, 8), 16)
    smem = pl.BlockSpec(memory_space=pltpu.SMEM)
    vmem = pl.BlockSpec(memory_space=pltpu.VMEM)
    slots = pool.shape[0]
    flops = 4 * pool.size // 2 * heads // pool.shape[1]
    return pl.pallas_call(
        functools.partial(attend_kernel, n_req, n_tp),
        out_shape=[jax.ShapeDtypeStruct((rows + stat_rows, head_dim), jnp.bfloat16)] * n_tp,
        in_specs=[vmem] * (n_req + 1) + [smem] * 3 + [vmem],
        out_specs=[vmem] * n_tp,
        scratch_shapes=[
            pltpu.VMEM((n_req, heads, head_dim), jnp.bfloat16),
            pltpu.SMEM((slots + 1,), jnp.int32),
            pltpu.SMEM((slots + 1,), jnp.int32),
            pltpu.VMEM((n_tp, n_req, chunk, head_dim), jnp.float32),
        ],
        compiler_params=pltpu.CompilerParams(vmem_limit_bytes=16 * MIB),
        cost_estimate=pl.CostEstimate(flops=flops, bytes_accessed=pool.size * 2, transcendentals=0),
        name="attend",
    )(*q_list, new_kv, page_slot, page_owner, context_len, pool)


def project_kernel(n_req, n_tp, chunk, *refs):
    part_refs = refs[:n_req]
    weight_ref = refs[n_req]
    out_refs = refs[n_req + 1 : n_req + 1 + n_tp]
    wide, logs, attention, sums = refs[n_req + 1 + n_tp :]
    rows = n_req * chunk
    step = round_up(n_req, 8)
    total_rows = n_tp * n_req
    depth, columns = weight_ref.shape
    my_tp = lax.axis_index("tp")
    for r in range(n_req):
        for c in range(n_tp):
            col = my_tp ^ c
            wide[r, pl.ds(pl.multiple_of(col * rows, 8), rows)] = part_refs[r][c, :rows].astype(jnp.float32)
            tail = part_refs[r][c, rows:].astype(jnp.float32)
            value = tail[:step] + tail[step : 2 * step] + tail[2 * step : 3 * step]
            logs[r, pl.ds(col * n_req, n_req)] = value[:n_req]
    values = [logs[r] for r in range(n_req)]
    top = functools.reduce(jnp.maximum, values)
    factors = [jnp.exp(v - top) for v in values]
    total = functools.reduce(jnp.add, factors)
    factors = [f / total for f in factors]
    for h in range(chunk):
        block = None
        for r in range(n_req):
            term = wide[r, pl.ds(h, total_rows, stride=chunk)] * factors[r][:, h : h + 1]
            block = term if block is None else block + term
        attention[:, h * 128 : (h + 1) * 128] = block.astype(jnp.bfloat16)
    tile = min(columns, 512)

    @pl.loop(0, columns // tile)
    def _(t):
        at = pl.ds(pl.multiple_of(t * tile, tile), tile)
        product = jnp.dot(attention[...], weight_ref[:, at], preferred_element_type=jnp.float32)
        for c in range(n_tp):
            sums[c, :, at] = product[c * n_req : (c + 1) * n_req]

    for d in range(n_tp):
        out_refs[d][...] = sums[my_tp ^ d].astype(out_refs[d].dtype)


def project(parts, out_weight, n_req, n_tp, chunk):
    depth, columns = out_weight.shape
    rows = n_req * chunk
    vmem = pl.BlockSpec(memory_space=pltpu.VMEM)
    own = jax.ShapeDtypeStruct((n_req, columns), jnp.float32)
    sent = jax.ShapeDtypeStruct((n_req, columns), jnp.bfloat16)
    total_rows = n_tp * n_req
    return pl.pallas_call(
        functools.partial(project_kernel, n_req, n_tp, chunk),
        out_shape=[own] + [sent] * (n_tp - 1),
        in_specs=[vmem] * (n_req + 1),
        out_specs=[vmem] * n_tp,
        scratch_shapes=[
            pltpu.VMEM((n_req, n_tp * rows, 128), jnp.float32),
            pltpu.VMEM((n_req, total_rows, 128), jnp.float32),
            pltpu.VMEM((total_rows, depth), jnp.bfloat16),
            pltpu.VMEM((n_tp, n_req, columns), jnp.float32),
        ],
        compiler_params=pltpu.CompilerParams(vmem_limit_bytes=32 * MIB),
        cost_estimate=pl.CostEstimate(
            flops=2 * total_rows * depth * columns, bytes_accessed=out_weight.size * 2, transcendentals=0
        ),
        name="project",
    )(*parts, out_weight)


def on_device(queries, new_kv, cache_pool, page_slot, page_owner, context_len, out_weight):
    n_req = lax.axis_size("req")
    n_tp = lax.axis_size("tp")
    pool = cache_pool[0, 0]
    head_dim = pool.shape[3] // 2
    q = queries.reshape(-1, head_dim)
    chunk = q.shape[0] // n_tp
    q_list = [q] + [swap(q, "req", d) for d in range(1, n_req)]
    pieces = attend(q_list, new_kv, page_slot, page_owner, context_len, pool, n_req, n_tp)
    arrived = jnp.stack([pieces[0]] + [swap(pieces[d], "tp", d) for d in range(1, n_tp)])
    parts = [arrived] + [swap(arrived, "req", d) for d in range(1, n_req)]
    sums = project(parts, out_weight, n_req, n_tp, chunk)
    total = sums[0]
    for d in range(1, n_tp):
        total = total + swap(sums[d], "tp", d).astype(jnp.float32)
    return total.astype(jnp.bfloat16)


def solution(mesh):
    placed = (
        P(("groups", "tp", "req"), None),
        P(("groups", "tp", "req"), None),
        P(("groups", "tp"), "req", None, None, None, None),
        P(("groups", "tp"), None, None),
        P(("groups", "tp"), None, None),
        P(("groups", "tp"), None),
        P("tp", "req"),
    )
    return jax.shard_map(
        on_device, mesh=mesh, in_specs=placed, out_specs=P(("groups", "tp"), "req"), check_vma=False
    )
```

```python
import functools
import math

import jax
import jax.numpy as jnp
from jax import lax
from jax.experimental import pallas as pl
from jax.experimental.pallas import tpu as pltpu
from jax.sharding import PartitionSpec as P

very_negative = -1e30
MIB = 1 << 20


def swap(x, axis, offset):
    count = lax.axis_size(axis)
    return lax.ppermute(x, axis, [(i, i ^ offset) for i in range(count)])


def round_up(value, step):
    return -(-value // step) * step


def halves(x):
    return pltpu.roll(x, 64, 1)


def query_tiles(stacked, kv_heads):
    turned = stacked.astype(jnp.float32).T
    lane = lax.broadcasted_iota(jnp.int32, turned.shape, 1)
    group = 64 // kv_heads
    return [
        [
            jnp.where((lane >= a * 64 + h * group) & (lane < a * 64 + (h + 1) * group), turned, 0.0).astype(jnp.bfloat16)
            for a in range(2)
        ]
        for h in range(kv_heads)
    ]


def pair_scores(page_a, page_b, tiles, head_dim):
    total = None
    for h in range(len(tiles)):
        for a, page in enumerate((page_a, page_b)):
            part = jnp.dot(page[h, :, :head_dim], tiles[h][a], preferred_element_type=jnp.float32)
            total = part if total is None else total + part
    return total


def pair_softmax(scores, limit):
    token = lax.broadcasted_iota(jnp.int32, scores.shape, 0)
    mask = token < limit
    masked = jnp.where(mask, scores, very_negative)
    top = jnp.max(masked, axis=0, keepdims=True)
    weights = jnp.where(mask, jnp.exp(masked - top), 0.0)
    return top, jnp.sum(weights, axis=0, keepdims=True), weights


def pair_values(weights, page_a, page_b, head_dim):
    turned = weights.T.astype(jnp.bfloat16)
    kv_heads = page_a.shape[0]
    group = 64 // kv_heads
    blocks = []
    for a, page in enumerate((page_a, page_b)):
        for h in range(kv_heads):
            at = a * 64 + h * group
            blocks.append(
                jnp.dot(turned[at : at + group], page[h, :, head_dim:], preferred_element_type=jnp.float32)
            )
    return jnp.concatenate(blocks, axis=0)


def to_columns(rows):
    stacked = jnp.concatenate(rows + [jnp.zeros((128 - len(rows), 128), jnp.float32)], axis=0)
    return stacked.T


def own_kernel(n_req, own_pages, *refs):
    (q_ref, kv_hbm, slot_hbm, owner_hbm, len_hbm, pool_hbm) = refs[:6]
    acc_ref, log_ref, limit_ref, pages_ref = refs[6:10]
    kv, slots, owners, lens, pool, small_sem, pool_sem, page_sem = refs[10:]
    slot_count, kv_heads, page_len, width = pool_hbm.shape
    head_dim = width // 2
    entries = slot_hbm.shape[2]
    me = lax.axis_index("req")
    scale = 1.0 / math.sqrt(head_dim)
    small = [
        pltpu.make_async_copy(src, dst, small_sem.at[i])
        for i, (src, dst) in enumerate(((slot_hbm, slots), (owner_hbm, owners), (len_hbm, lens), (kv_hbm, kv)))
    ]
    for copy in small:
        copy.start()
    whole = pltpu.make_async_copy(pool_hbm, pool, pool_sem)
    whole.start()
    stacked = jnp.concatenate([q_ref[...], q_ref[...]], axis=0)
    tiles = query_tiles(stacked, kv_heads)
    for copy in small:
        copy.wait()

    fetched = []
    lane = lax.broadcasted_iota(jnp.int32, (1, 128), 1)
    limits = []
    for d in range(1, n_req):
        n = me ^ d
        length = lens[0, n]
        slot = jnp.int32(0)
        limit = jnp.int32(0)
        for j in range(entries):
            held = (owners[0, n, j] == me) & (j * page_len < length)
            slot = jnp.where(held, slots[0, n, j], slot)
            limit = jnp.where(held, length - j * page_len, limit)
        copy = pltpu.make_async_copy(pool_hbm.at[slot], pages_ref.at[d - 1], page_sem.at[d - 1])
        copy.start()
        fetched.append(copy)
        limits.append(limit)
    if len(limits) % 2:
        limits.append(jnp.int32(0))
    for p in range(len(limits) // 2):
        limit_ref[p : p + 1] = jnp.where(lane < 64, limits[2 * p], limits[2 * p + 1])

    my_length = lens[0, me]
    pages, valid = [], []
    for i in range(own_pages):
        held = (owners[0, me, i] == me) & (i * page_len < my_length)
        pages.append(pool.at[jnp.where(held, slots[0, me, i], 0)])
        valid.append(jnp.where(held, my_length - i * page_len, 0))
    if own_pages % 2:
        pages.append(pages[0])
        valid.append(jnp.int32(0))
    pairs = len(pages) // 2

    base = kv_heads * head_dim
    new_k = [kv[0:1, h * head_dim : (h + 1) * head_dim] for h in range(kv_heads)]
    self_score = None
    for h in range(kv_heads):
        both = tiles[h][0] + tiles[h][1]
        part = jnp.dot(jnp.broadcast_to(new_k[h], (16, head_dim)), both, preferred_element_type=jnp.float32)
        self_score = part if self_score is None else self_score + part
    self_score = self_score[0:1] * scale

    whole.wait()
    scores = [pair_scores(pages[2 * p], pages[2 * p + 1], tiles, head_dim) * scale for p in range(pairs)]
    tops, totals, sums = [], [], []
    for p in range(pairs):
        limit = jnp.where(lane < 64, valid[2 * p], valid[2 * p + 1])
        top, total, weights = pair_softmax(scores[p], limit)
        tops.append(top)
        totals.append(total)
        sums.append(pair_values(weights, pages[2 * p], pages[2 * p + 1], head_dim))
    top = functools.reduce(jnp.maximum, tops)
    top = jnp.maximum(jnp.maximum(top, halves(top)), self_score)
    factors = [jnp.exp(t - top) for t in tops]
    own_factor = jnp.exp(self_score - top)
    total = functools.reduce(jnp.add, [f * t for f, t in zip(factors, totals)])
    total = total + halves(total) + own_factor
    columns = to_columns([f / total for f in factors] + [own_factor / total])
    result = None
    for p in range(pairs):
        term = sums[p] * columns[:, p : p + 1]
        result = term if result is None else result + term
    group = 64 // kv_heads
    new_v = jnp.concatenate(
        [
            jnp.broadcast_to(kv[0:1, base + h * head_dim : base + (h + 1) * head_dim].astype(jnp.float32), (group, head_dim))
            for h in range(kv_heads)
        ],
        axis=0,
    )
    acc_ref[...] = result[:64] + result[64:] + columns[:64, pairs : pairs + 1] * new_v
    log_ref[...] = jnp.broadcast_to(top + jnp.log(total), log_ref.shape)
    for copy in fetched:
        copy.wait()


def own_attention(q, new_kv, page_slot, page_owner, context_len, pool, n_req):
    heads, head_dim = q.shape
    slots, kv_heads, page_len, width = pool.shape
    own_pages = min(slots, page_slot.shape[2])
    hbm = pl.BlockSpec(memory_space=pl.ANY)
    vmem = pl.BlockSpec(memory_space=pltpu.VMEM)
    pair_count = round_up(n_req - 1, 2) // 2
    page_bytes = pool.size * 2 // slots
    return pl.pallas_call(
        functools.partial(own_kernel, n_req, own_pages),
        out_shape=[
            jax.ShapeDtypeStruct((heads, head_dim), jnp.float32),
            jax.ShapeDtypeStruct((8, 128), jnp.float32),
            jax.ShapeDtypeStruct((round_up(pair_count, 8), 128), jnp.int32),
            jax.ShapeDtypeStruct((n_req - 1, kv_heads, page_len, width), pool.dtype),
        ],
        in_specs=[vmem] + [hbm] * 5,
        out_specs=[vmem] * 4,
        scratch_shapes=[
            pltpu.VMEM(new_kv.shape, new_kv.dtype),
            pltpu.SMEM(page_slot.shape, jnp.int32),
            pltpu.SMEM(page_owner.shape, jnp.int32),
            pltpu.SMEM(context_len.shape, jnp.int32),
            pltpu.VMEM(pool.shape, pool.dtype),
            pltpu.SemaphoreType.DMA((4,)),
            pltpu.SemaphoreType.DMA,
            pltpu.SemaphoreType.DMA((n_req - 1,)),
        ],
        compiler_params=pltpu.CompilerParams(vmem_limit_bytes=16 * MIB),
        cost_estimate=pl.CostEstimate(
            flops=4 * own_pages * page_len * heads * head_dim,
            bytes_accessed=page_bytes * (slots + n_req - 1) * 2,
            transcendentals=0,
        ),
        name="own_attention",
    )(q, new_kv, page_slot, page_owner, context_len, pool)


def stat_rows_of(n_req):
    return round_up(2 * n_req, 8)


def other_kernel(n_req, n_tp, *refs):
    q_refs = refs[: n_req - 1]
    acc_ref, log_ref, limit_ref, pages_ref = refs[n_req - 1 : n_req + 3]
    out_refs = refs[n_req + 3 : n_req + 3 + n_tp]
    results, logs, stats = refs[n_req + 3 + n_tp :]
    kv_heads, width = pages_ref.shape[1], pages_ref.shape[3]
    head_dim = width // 2
    heads = q_refs[0].shape[0]
    chunk = heads // n_tp
    my_tp = lax.axis_index("tp")
    scale = 1.0 / math.sqrt(head_dim)
    others = n_req - 1
    pairs = round_up(others, 2) // 2
    results[0] = acc_ref[...]
    logs[0:1] = log_ref[0:1]
    scores, members = [], []
    for p in range(pairs):
        a, b = 2 * p, min(2 * p + 1, others - 1)
        members.append((a, b))
        tiles = query_tiles(jnp.concatenate([q_refs[a][...], q_refs[b][...]], axis=0), kv_heads)
        scores.append(pair_scores(pages_ref.at[a], pages_ref.at[b], tiles, head_dim) * scale)
    sums, inverse, log_rows = [], [], []
    for p in range(pairs):
        a, b = members[p]
        top, total, weights = pair_softmax(scores[p], limit_ref[p : p + 1])
        sums.append(pair_values(weights, pages_ref.at[a], pages_ref.at[b], head_dim))
        total = jnp.where(total > 0.0, total, 1.0)
        inverse.append(1.0 / total)
        log_rows.append(top + jnp.log(total))
    columns = to_columns(inverse)
    for p in range(pairs):
        result = sums[p] * columns[:, p : p + 1]
        results[2 * p + 1] = result[:64]
        logs[2 * p + 1 : 2 * p + 2] = log_rows[p]
        if 2 * p + 1 < others:
            results[2 * p + 2] = result[64:]
            logs[2 * p + 2 : 2 * p + 3] = halves(log_rows[p])
    lane = lax.broadcasted_iota(jnp.int32, (n_req, 128), 1)
    value = logs[0:n_req]
    high = value.astype(jnp.bfloat16).astype(jnp.float32)
    rest = value - high
    middle = rest.astype(jnp.bfloat16).astype(jnp.float32)
    stats[...] = jnp.zeros_like(stats)
    stats[0:n_req] = jnp.where(lane < 64, high, halves(middle))
    stats[n_req : 2 * n_req] = jnp.where(lane < 64, rest - middle, 0.0)
    tail = stats[...].astype(jnp.bfloat16)
    rows = n_req * chunk
    for d in range(n_tp):
        at = pl.ds(pl.multiple_of((my_tp ^ d) * chunk, chunk), chunk)
        for k in range(n_req):
            out_refs[d][k * chunk : (k + 1) * chunk] = results[k, at].astype(jnp.bfloat16)
        out_refs[d][rows:] = tail


def other_attention(q_list, own, n_req, n_tp):
    heads, head_dim = q_list[0].shape
    chunk = heads // n_tp
    rows = n_req * chunk + stat_rows_of(n_req)
    vmem = pl.BlockSpec(memory_space=pltpu.VMEM)
    return pl.pallas_call(
        functools.partial(other_kernel, n_req, n_tp),
        out_shape=[jax.ShapeDtypeStruct((rows, head_dim), jnp.bfloat16)] * n_tp,
        in_specs=[vmem] * (n_req + 3),
        out_specs=[vmem] * n_tp,
        scratch_shapes=[
            pltpu.VMEM((n_req, heads, head_dim), jnp.float32),
            pltpu.VMEM((round_up(n_req, 8), 128), jnp.float32),
            pltpu.VMEM((stat_rows_of(n_req), 128), jnp.float32),
        ],
        compiler_params=pltpu.CompilerParams(vmem_limit_bytes=16 * MIB),
        cost_estimate=pl.CostEstimate(flops=2 * own[3].size * 16, bytes_accessed=own[3].size * 2, transcendentals=0),
        name="other_attention",
    )(*q_list, *own)


def load_kernel(after_ref, weight_hbm, out_ref, sems):
    depth = weight_hbm.shape[0]
    parts = sems.shape[0]
    step = depth // parts
    copies = [
        pltpu.make_async_copy(
            weight_hbm.at[pl.ds(i * step, step)], out_ref.at[pl.ds(i * step, step)], sems.at[i]
        )
        for i in range(parts)
    ]
    for copy in copies:
        copy.start()
    for copy in copies:
        copy.wait()


def load_weight(after, out_weight):
    return pl.pallas_call(
        load_kernel,
        out_shape=jax.ShapeDtypeStruct(out_weight.shape, out_weight.dtype),
        in_specs=[pl.BlockSpec(memory_space=pl.ANY)] * 2,
        out_specs=pl.BlockSpec(memory_space=pltpu.VMEM),
        scratch_shapes=[pltpu.SemaphoreType.DMA((8,))],
        compiler_params=pltpu.CompilerParams(vmem_limit_bytes=20 * MIB),
        cost_estimate=pl.CostEstimate(flops=0, bytes_accessed=out_weight.size * 4, transcendentals=0),
        name="load_weight",
    )(after, out_weight)


def project_kernel(n_req, n_tp, chunk, *refs):
    part_refs = refs[:n_req]
    weight_ref = refs[n_req]
    out_refs = refs[n_req + 1 : n_req + 1 + n_tp]
    wide, logs, attention, sums = refs[n_req + 1 + n_tp :]
    rows = n_req * chunk
    total_rows = n_tp * n_req
    columns = weight_ref.shape[1]
    my_tp = lax.axis_index("tp")
    me = lax.axis_index("req")
    for r in range(n_req):
        for c in range(n_tp):
            col = my_tp ^ c
            block = part_refs[r][c, :rows].astype(jnp.float32)
            tail = part_refs[r][c, rows:].astype(jnp.float32)
            value = (tail[:n_req] + halves(tail[:n_req])) + tail[n_req : 2 * n_req]
            for k in range(n_req):
                row = col * n_req + (me ^ r ^ k)
                wide[r, pl.ds(pl.multiple_of(row * chunk, chunk), chunk)] = block[k * chunk : (k + 1) * chunk]
                logs[r, pl.ds(row, 1)] = value[k : k + 1]
    shift = (128 - my_tp * chunk) % 128
    values = [pltpu.roll(logs[r], shift, 1) for r in range(n_req)]
    top = functools.reduce(jnp.maximum, values)
    factors = [jnp.exp(v - top) for v in values]
    total = functools.reduce(jnp.add, factors)
    factors = [f / total for f in factors]
    for h in range(chunk):
        block = None
        for r in range(n_req):
            term = wide[r, pl.ds(h, total_rows, stride=chunk)] * factors[r][:, h : h + 1]
            block = term if block is None else block + term
        attention[:, h * 128 : (h + 1) * 128] = block.astype(jnp.bfloat16)
    tile = min(columns, 512)

    @pl.loop(0, columns // tile)
    def _(t):
        at = pl.ds(pl.multiple_of(t * tile, tile), tile)
        product = jnp.dot(attention[...], weight_ref[:, at], preferred_element_type=jnp.float32)
        for c in range(n_tp):
            sums[c, :, at] = product[c * n_req : (c + 1) * n_req]

    for d in range(n_tp):
        out_refs[d][...] = sums[my_tp ^ d].astype(out_refs[d].dtype)


def project(parts, out_weight, n_req, n_tp, chunk):
    depth, columns = out_weight.shape
    rows = n_req * chunk
    vmem = pl.BlockSpec(memory_space=pltpu.VMEM)
    own = jax.ShapeDtypeStruct((n_req, columns), jnp.float32)
    sent = jax.ShapeDtypeStruct((n_req, columns), jnp.bfloat16)
    total_rows = n_tp * n_req
    return pl.pallas_call(
        functools.partial(project_kernel, n_req, n_tp, chunk),
        out_shape=[own] + [sent] * (n_tp - 1),
        in_specs=[vmem] * (n_req + 1),
        out_specs=[vmem] * n_tp,
        scratch_shapes=[
            pltpu.VMEM((n_req, n_tp * rows, 128), jnp.float32),
            pltpu.VMEM((n_req, total_rows, 128), jnp.float32),
            pltpu.VMEM((total_rows, depth), jnp.bfloat16),
            pltpu.VMEM((n_tp, n_req, columns), jnp.float32),
        ],
        compiler_params=pltpu.CompilerParams(vmem_limit_bytes=24 * MIB),
        cost_estimate=pl.CostEstimate(
            flops=2 * total_rows * depth * columns, bytes_accessed=out_weight.size * 2, transcendentals=0
        ),
        name="project",
    )(*parts, out_weight)


def on_device(queries, new_kv, cache_pool, page_slot, page_owner, context_len, out_weight):
    n_req = lax.axis_size("req")
    n_tp = lax.axis_size("tp")
    pool = cache_pool[0, 0]
    head_dim = pool.shape[3] // 2
    q = queries.reshape(-1, head_dim)
    chunk = q.shape[0] // n_tp
    q_list = [swap(q, "req", d) for d in range(1, n_req)]
    own = own_attention(q, new_kv, page_slot, page_owner, context_len, pool, n_req)
    pieces = other_attention(q_list, own, n_req, n_tp)
    arrived = jnp.stack([pieces[0]] + [swap(pieces[d], "tp", d) for d in range(1, n_tp)])
    parts = [arrived] + [swap(arrived, "req", d) for d in range(1, n_req)]
    weight = load_weight(arrived, out_weight)
    sums = project(parts, weight, n_req, n_tp, chunk)
    total = sums[0]
    for d in range(1, n_tp):
        total = total + swap(sums[d], "tp", d).astype(jnp.float32)
    return total.astype(jnp.bfloat16)


def solution(mesh):
    placed = (
        P(("groups", "tp", "req"), None),
        P(("groups", "tp", "req"), None),
        P(("groups", "tp"), "req", None, None, None, None),
        P(("groups", "tp"), None, None),
        P(("groups", "tp"), None, None),
        P(("groups", "tp"), None),
        P("tp", "req"),
    )
    return jax.shard_map(
        on_device, mesh=mesh, in_specs=placed, out_specs=P(("groups", "tp"), "req"), check_vma=False
    )
```

```python
import functools
import math

import jax
import jax.numpy as jnp
from jax import lax
from jax.experimental import pallas as pl
from jax.experimental.pallas import tpu as pltpu
from jax.sharding import PartitionSpec as P

very_negative = -1e30
MIB = 1 << 20


def swap(x, axis, offset):
    count = lax.axis_size(axis)
    return lax.ppermute(x, axis, [(i, i ^ offset) for i in range(count)])


def in_hbm(x):
    return pltpu.with_memory_space_constraint(x, pltpu.HBM)


def round_up(value, step):
    return -(-value // step) * step


def halves(x):
    return pltpu.roll(x, 64, 1)


def lay_rows(target, start, q_ref):
    head_dim = target.shape[1]
    for h in range(64):
        target[start + h : start + h + 1] = q_ref[0:1, h * head_dim : (h + 1) * head_dim].astype(jnp.float32)


def query_tiles(stacked, kv_heads):
    turned = stacked.T
    lane = lax.broadcasted_iota(jnp.int32, turned.shape, 1)
    group = 64 // kv_heads
    return [
        [
            jnp.where((lane >= a * 64 + h * group) & (lane < a * 64 + (h + 1) * group), turned, 0.0).astype(jnp.bfloat16)
            for a in range(2)
        ]
        for h in range(kv_heads)
    ]


def pair_scores(page_a, page_b, tiles, head_dim):
    total = None
    for h in range(len(tiles)):
        for a, page in enumerate((page_a, page_b)):
            part = jnp.dot(page[h, :, :head_dim], tiles[h][a], preferred_element_type=jnp.float32)
            total = part if total is None else total + part
    return total


def pair_softmax(scores, limit):
    token = lax.broadcasted_iota(jnp.int32, scores.shape, 0)
    mask = token < limit
    masked = jnp.where(mask, scores, very_negative)
    top = jnp.max(masked, axis=0, keepdims=True)
    weights = jnp.where(mask, jnp.exp(masked - top), 0.0)
    return top, jnp.sum(weights, axis=0, keepdims=True), weights


def pair_values(weights, page_a, page_b, head_dim):
    turned = weights.T.astype(jnp.bfloat16)
    kv_heads = page_a.shape[0]
    group = 64 // kv_heads
    blocks = []
    for a, page in enumerate((page_a, page_b)):
        for h in range(kv_heads):
            at = a * 64 + h * group
            blocks.append(
                jnp.dot(turned[at : at + group], page[h, :, head_dim:], preferred_element_type=jnp.float32)
            )
    return jnp.concatenate(blocks, axis=0)


def to_columns(rows):
    stacked = jnp.concatenate(rows + [jnp.zeros((128 - len(rows), 128), jnp.float32)], axis=0)
    return stacked.T


def own_kernel(n_req, own_pages, *refs):
    (q_hbm, kv_hbm, slot_hbm, owner_hbm, len_hbm, pool_hbm) = refs[:6]
    acc_ref, log_ref, limit_ref, pages_ref = refs[6:10]
    q_row, q_heads, kv, slots, owners, lens, pool, small_sem, pool_sem, page_sem = refs[10:]
    slot_count, kv_heads, page_len, width = pool_hbm.shape
    head_dim = width // 2
    entries = slot_hbm.shape[2]
    me = lax.axis_index("req")
    scale = 1.0 / math.sqrt(head_dim)
    small = [
        pltpu.make_async_copy(src, dst, small_sem.at[i])
        for i, (src, dst) in enumerate(
            ((slot_hbm, slots), (owner_hbm, owners), (len_hbm, lens), (kv_hbm, kv), (q_hbm, q_row))
        )
    ]
    for copy in small:
        copy.start()
    whole = pltpu.make_async_copy(pool_hbm, pool, pool_sem)
    whole.start()
    for copy in small:
        copy.wait()

    fetched = []
    lane = lax.broadcasted_iota(jnp.int32, (1, 128), 1)
    limits = []
    for d in range(1, n_req):
        n = me ^ d
        length = lens[0, n]
        slot = jnp.int32(0)
        limit = jnp.int32(0)
        for j in range(entries):
            held = (owners[0, n, j] == me) & (j * page_len < length)
            slot = jnp.where(held, slots[0, n, j], slot)
            limit = jnp.where(held, length - j * page_len, limit)
        copy = pltpu.make_async_copy(pool_hbm.at[slot], pages_ref.at[d - 1], page_sem.at[d - 1])
        copy.start()
        fetched.append(copy)
        limits.append(limit)
    if len(limits) % 2:
        limits.append(jnp.int32(0))
    for p in range(len(limits) // 2):
        limit_ref[p : p + 1] = jnp.where(lane < 64, limits[2 * p], limits[2 * p + 1])

    lay_rows(q_heads, 0, q_row)
    q_heads[64:] = q_heads[:64]
    tiles = query_tiles(q_heads[...], kv_heads)
    my_length = lens[0, me]
    pages, valid = [], []
    for i in range(own_pages):
        held = (owners[0, me, i] == me) & (i * page_len < my_length)
        pages.append(pool.at[jnp.where(held, slots[0, me, i], 0)])
        valid.append(jnp.where(held, my_length - i * page_len, 0))
    if own_pages % 2:
        pages.append(pages[0])
        valid.append(jnp.int32(0))
    pairs = len(pages) // 2

    base = kv_heads * head_dim
    new_k = [kv[0:1, h * head_dim : (h + 1) * head_dim] for h in range(kv_heads)]
    self_score = None
    for h in range(kv_heads):
        both = tiles[h][0] + tiles[h][1]
        part = jnp.dot(jnp.broadcast_to(new_k[h], (16, head_dim)), both, preferred_element_type=jnp.float32)
        self_score = part if self_score is None else self_score + part
    self_score = self_score[0:1] * scale

    whole.wait()
    scores = [pair_scores(pages[2 * p], pages[2 * p + 1], tiles, head_dim) * scale for p in range(pairs)]
    tops, totals, sums = [], [], []
    for p in range(pairs):
        limit = jnp.where(lane < 64, valid[2 * p], valid[2 * p + 1])
        top, total, weights = pair_softmax(scores[p], limit)
        tops.append(top)
        totals.append(total)
        sums.append(pair_values(weights, pages[2 * p], pages[2 * p + 1], head_dim))
    top = functools.reduce(jnp.maximum, tops)
    top = jnp.maximum(jnp.maximum(top, halves(top)), self_score)
    factors = [jnp.exp(t - top) for t in tops]
    own_factor = jnp.exp(self_score - top)
    total = functools.reduce(jnp.add, [f * t for f, t in zip(factors, totals)])
    total = total + halves(total) + own_factor
    columns = to_columns([f / total for f in factors] + [own_factor / total])
    result = None
    for p in range(pairs):
        term = sums[p] * columns[:, p : p + 1]
        result = term if result is None else result + term
    group = 64 // kv_heads
    new_v = jnp.concatenate(
        [
            jnp.broadcast_to(kv[0:1, base + h * head_dim : base + (h + 1) * head_dim].astype(jnp.float32), (group, head_dim))
            for h in range(kv_heads)
        ],
        axis=0,
    )
    acc_ref[...] = result[:64] + result[64:] + columns[:64, pairs : pairs + 1] * new_v
    log_ref[...] = jnp.broadcast_to(top + jnp.log(total), log_ref.shape)
    for copy in fetched:
        copy.wait()


def own_attention(q, new_kv, page_slot, page_owner, context_len, pool, n_req):
    slots, kv_heads, page_len, width = pool.shape
    head_dim = width // 2
    heads = q.shape[1] // head_dim
    own_pages = min(slots, page_slot.shape[2])
    hbm = pl.BlockSpec(memory_space=pltpu.HBM)
    vmem = pl.BlockSpec(memory_space=pltpu.VMEM)
    pair_count = round_up(n_req - 1, 2) // 2
    page_bytes = pool.size * 2 // slots
    return pl.pallas_call(
        functools.partial(own_kernel, n_req, own_pages),
        out_shape=[
            jax.ShapeDtypeStruct((heads, head_dim), jnp.float32),
            jax.ShapeDtypeStruct((8, 128), jnp.float32),
            jax.ShapeDtypeStruct((round_up(pair_count, 8), 128), jnp.int32),
            jax.ShapeDtypeStruct((n_req - 1, kv_heads, page_len, width), pool.dtype),
        ],
        in_specs=[hbm] * 6,
        out_specs=[vmem] * 4,
        scratch_shapes=[
            pltpu.VMEM(q.shape, q.dtype),
            pltpu.VMEM((128, head_dim), jnp.float32),
            pltpu.VMEM(new_kv.shape, new_kv.dtype),
            pltpu.SMEM(page_slot.shape, jnp.int32),
            pltpu.SMEM(page_owner.shape, jnp.int32),
            pltpu.SMEM(context_len.shape, jnp.int32),
            pltpu.VMEM(pool.shape, pool.dtype),
            pltpu.SemaphoreType.DMA((5,)),
            pltpu.SemaphoreType.DMA,
            pltpu.SemaphoreType.DMA((n_req - 1,)),
        ],
        compiler_params=pltpu.CompilerParams(vmem_limit_bytes=16 * MIB),
        cost_estimate=pl.CostEstimate(
            flops=4 * own_pages * page_len * heads * head_dim,
            bytes_accessed=page_bytes * (slots + n_req - 1) * 2,
            transcendentals=0,
        ),
        name="own_attention",
    )(*(in_hbm(x) for x in (q, new_kv, page_slot, page_owner, context_len, pool)))


def stat_rows_of(n_req):
    return round_up(2 * n_req, 8)


def other_kernel(n_req, n_tp, *refs):
    q_refs = refs[: n_req - 1]
    acc_ref, log_ref, limit_ref, pages_ref = refs[n_req - 1 : n_req + 3]
    out_refs = refs[n_req + 3 : n_req + 3 + n_tp]
    results, logs, stats, q_heads = refs[n_req + 3 + n_tp :]
    kv_heads, width = pages_ref.shape[1], pages_ref.shape[3]
    head_dim = width // 2
    heads = results.shape[1]
    chunk = heads // n_tp
    my_tp = lax.axis_index("tp")
    scale = 1.0 / math.sqrt(head_dim)
    others = n_req - 1
    pairs = round_up(others, 2) // 2
    results[0] = acc_ref[...]
    logs[0:1] = log_ref[0:1]
    scores, members = [], []
    for p in range(pairs):
        a, b = 2 * p, min(2 * p + 1, others - 1)
        members.append((a, b))
        lay_rows(q_heads.at[p], 0, q_refs[a])
        lay_rows(q_heads.at[p], 64, q_refs[b])
        tiles = query_tiles(q_heads[p], kv_heads)
        scores.append(pair_scores(pages_ref.at[a], pages_ref.at[b], tiles, head_dim) * scale)
    sums, inverse, log_rows = [], [], []
    for p in range(pairs):
        a, b = members[p]
        top, total, weights = pair_softmax(scores[p], limit_ref[p : p + 1])
        sums.append(pair_values(weights, pages_ref.at[a], pages_ref.at[b], head_dim))
        total = jnp.where(total > 0.0, total, 1.0)
        inverse.append(1.0 / total)
        log_rows.append(top + jnp.log(total))
    columns = to_columns(inverse)
    for p in range(pairs):
        result = sums[p] * columns[:, p : p + 1]
        results[2 * p + 1] = result[:64]
        logs[2 * p + 1 : 2 * p + 2] = log_rows[p]
        if 2 * p + 1 < others:
            results[2 * p + 2] = result[64:]
            logs[2 * p + 2 : 2 * p + 3] = halves(log_rows[p])
    lane = lax.broadcasted_iota(jnp.int32, (n_req, 128), 1)
    value = logs[0:n_req]
    high = value.astype(jnp.bfloat16).astype(jnp.float32)
    rest = value - high
    middle = rest.astype(jnp.bfloat16).astype(jnp.float32)
    stats[...] = jnp.zeros_like(stats)
    stats[0:n_req] = jnp.where(lane < 64, high, halves(middle))
    stats[n_req : 2 * n_req] = jnp.where(lane < 64, rest - middle, 0.0)
    tail = stats[...].astype(jnp.bfloat16)
    rows = n_req * chunk
    for d in range(n_tp):
        at = pl.ds(pl.multiple_of((my_tp ^ d) * chunk, chunk), chunk)
        for k in range(n_req):
            out_refs[d][k * chunk : (k + 1) * chunk] = results[k, at].astype(jnp.bfloat16)
        out_refs[d][rows:] = tail


def other_attention(q_list, own, n_req, n_tp):
    heads, head_dim = own[0].shape
    chunk = heads // n_tp
    rows = n_req * chunk + stat_rows_of(n_req)
    vmem = pl.BlockSpec(memory_space=pltpu.VMEM)
    return pl.pallas_call(
        functools.partial(other_kernel, n_req, n_tp),
        out_shape=[jax.ShapeDtypeStruct((rows, head_dim), jnp.bfloat16)] * n_tp,
        in_specs=[vmem] * (n_req + 3),
        out_specs=[vmem] * n_tp,
        scratch_shapes=[
            pltpu.VMEM((n_req, heads, head_dim), jnp.float32),
            pltpu.VMEM((round_up(n_req, 8), 128), jnp.float32),
            pltpu.VMEM((stat_rows_of(n_req), 128), jnp.float32),
            pltpu.VMEM((round_up(n_req - 1, 2) // 2, 128, head_dim), jnp.float32),
        ],
        compiler_params=pltpu.CompilerParams(vmem_limit_bytes=16 * MIB),
        cost_estimate=pl.CostEstimate(flops=2 * own[3].size * 16, bytes_accessed=own[3].size * 2, transcendentals=0),
        name="other_attention",
    )(*q_list, *own)


def load_kernel(first, after_ref, weight_hbm, out_ref, sems):
    parts = sems.shape[0]
    step = out_ref.shape[0] // parts
    copies = [
        pltpu.make_async_copy(
            weight_hbm.at[pl.ds(first + i * step, step)], out_ref.at[pl.ds(i * step, step)], sems.at[i]
        )
        for i in range(parts)
    ]
    for copy in copies:
        copy.start()
    for copy in copies:
        copy.wait()


def load_weight(after, out_weight, first, rows):
    columns = out_weight.shape[1]
    return pl.pallas_call(
        functools.partial(load_kernel, first),
        out_shape=jax.ShapeDtypeStruct((rows, columns), out_weight.dtype),
        in_specs=[pl.BlockSpec(memory_space=pl.ANY), pl.BlockSpec(memory_space=pltpu.HBM)],
        out_specs=pl.BlockSpec(memory_space=pltpu.VMEM),
        scratch_shapes=[pltpu.SemaphoreType.DMA((4,))],
        compiler_params=pltpu.CompilerParams(vmem_limit_bytes=20 * MIB),
        cost_estimate=pl.CostEstimate(flops=0, bytes_accessed=rows * columns * 4, transcendentals=0),
        name="load_weight",
    )(after, in_hbm(out_weight))


def project_kernel(n_req, n_tp, chunk, *refs):
    part_refs = refs[:n_req]
    weight_refs = refs[n_req : n_req + 2]
    out_refs = refs[n_req + 2 : n_req + 2 + n_tp]
    wide, logs, attention, sums = refs[n_req + 2 + n_tp :]
    rows = n_req * chunk
    total_rows = n_tp * n_req
    split = weight_refs[0].shape[0]
    columns = weight_refs[0].shape[1]
    my_tp = lax.axis_index("tp")
    me = lax.axis_index("req")
    for r in range(n_req):
        for c in range(n_tp):
            col = my_tp ^ c
            block = part_refs[r][c, :rows].astype(jnp.float32)
            tail = part_refs[r][c, rows:].astype(jnp.float32)
            value = (tail[:n_req] + halves(tail[:n_req])) + tail[n_req : 2 * n_req]
            for k in range(n_req):
                row = col * n_req + (me ^ r ^ k)
                wide[r, pl.ds(pl.multiple_of(row * chunk, chunk), chunk)] = block[k * chunk : (k + 1) * chunk]
                logs[r, pl.ds(row, 1)] = value[k : k + 1]
    shift = (128 - my_tp * chunk) % 128
    values = [pltpu.roll(logs[r], shift, 1) for r in range(n_req)]
    top = functools.reduce(jnp.maximum, values)
    factors = [jnp.exp(v - top) for v in values]
    total = functools.reduce(jnp.add, factors)
    factors = [f / total for f in factors]
    for h in range(chunk):
        block = None
        for r in range(n_req):
            term = wide[r, pl.ds(h, total_rows, stride=chunk)] * factors[r][:, h : h + 1]
            block = term if block is None else block + term
        attention[:, h * 128 : (h + 1) * 128] = block.astype(jnp.bfloat16)
    tile = min(columns, 512)

    @pl.loop(0, columns // tile)
    def _(t):
        at = pl.ds(pl.multiple_of(t * tile, tile), tile)
        product = jnp.dot(attention[:, :split], weight_refs[0][:, at], preferred_element_type=jnp.float32)
        product += jnp.dot(attention[:, split:], weight_refs[1][:, at], preferred_element_type=jnp.float32)
        for c in range(n_tp):
            sums[c, :, at] = product[c * n_req : (c + 1) * n_req]

    for d in range(n_tp):
        out_refs[d][...] = sums[my_tp ^ d].astype(out_refs[d].dtype)


def project(parts, weights, n_req, n_tp, chunk):
    depth = sum(w.shape[0] for w in weights)
    columns = weights[0].shape[1]
    rows = n_req * chunk
    vmem = pl.BlockSpec(memory_space=pltpu.VMEM)
    own = jax.ShapeDtypeStruct((n_req, columns), jnp.float32)
    sent = jax.ShapeDtypeStruct((n_req, columns), jnp.bfloat16)
    total_rows = n_tp * n_req
    return pl.pallas_call(
        functools.partial(project_kernel, n_req, n_tp, chunk),
        out_shape=[own] + [sent] * (n_tp - 1),
        in_specs=[vmem] * (n_req + 2),
        out_specs=[vmem] * n_tp,
        scratch_shapes=[
            pltpu.VMEM((n_req, n_tp * rows, 128), jnp.float32),
            pltpu.VMEM((n_req, total_rows, 128), jnp.float32),
            pltpu.VMEM((total_rows, depth), jnp.bfloat16),
            pltpu.VMEM((n_tp, n_req, columns), jnp.float32),
        ],
        compiler_params=pltpu.CompilerParams(vmem_limit_bytes=24 * MIB),
        cost_estimate=pl.CostEstimate(
            flops=2 * total_rows * depth * columns, bytes_accessed=depth * columns * 2, transcendentals=0
        ),
        name="project",
    )(*parts, *weights)


def on_device(queries, new_kv, cache_pool, page_slot, page_owner, context_len, out_weight):
    n_req = lax.axis_size("req")
    n_tp = lax.axis_size("tp")
    pool = cache_pool[0, 0]
    head_dim = pool.shape[3] // 2
    chunk = queries.shape[1] // head_dim // n_tp
    q_list = [swap(queries, "req", d) for d in range(1, n_req)]
    own = own_attention(queries, new_kv, page_slot, page_owner, context_len, pool, n_req)
    pieces = other_attention(q_list, own, n_req, n_tp)
    depth = out_weight.shape[0]
    early = depth * 3 // 8
    first = load_weight(pieces[0], out_weight, 0, early)
    arrived = jnp.stack([pieces[0]] + [swap(pieces[d], "tp", d) for d in range(1, n_tp)])
    parts = [arrived] + [swap(arrived, "req", d) for d in range(1, n_req)]
    second = load_weight(arrived, out_weight, early, depth - early)
    sums = project(parts, (first, second), n_req, n_tp, chunk)
    total = sums[0]
    for d in range(1, n_tp):
        total = total + swap(sums[d], "tp", d).astype(jnp.float32)
    return total.astype(jnp.bfloat16)


def solution(mesh):
    placed = (
        P(("groups", "tp", "req"), None),
        P(("groups", "tp", "req"), None),
        P(("groups", "tp"), "req", None, None, None, None),
        P(("groups", "tp"), None, None),
        P(("groups", "tp"), None, None),
        P(("groups", "tp"), None),
        P("tp", "req"),
    )
    return jax.shard_map(
        on_device, mesh=mesh, in_specs=placed, out_specs=P(("groups", "tp"), "req"), check_vma=False
    )
```

```python
import functools
import math

import jax
import jax.numpy as jnp
from jax import lax
from jax.experimental import pallas as pl
from jax.experimental.pallas import tpu as pltpu
from jax.sharding import PartitionSpec as P

very_negative = -1e30
MIB = 1 << 20


def swap(x, axis, offset):
    count = lax.axis_size(axis)
    return lax.ppermute(x, axis, [(i, i ^ offset) for i in range(count)])


def in_hbm(x):
    return pltpu.with_memory_space_constraint(x, pltpu.HBM)


def round_up(value, step):
    return -(-value // step) * step


def halves(x):
    return pltpu.roll(x, 64, 1)


def lay_rows(target, start, q_ref):
    head_dim = target.shape[1]
    for h in range(64):
        target[start + h : start + h + 1] = q_ref[0:1, h * head_dim : (h + 1) * head_dim].astype(jnp.float32)


def query_tiles(stacked, kv_heads):
    turned = stacked.T
    lane = lax.broadcasted_iota(jnp.int32, turned.shape, 1)
    group = 64 // kv_heads
    return [
        [
            jnp.where((lane >= a * 64 + h * group) & (lane < a * 64 + (h + 1) * group), turned, 0.0).astype(jnp.bfloat16)
            for a in range(2)
        ]
        for h in range(kv_heads)
    ]


def pair_scores(page_a, page_b, tiles, head_dim):
    total = None
    for h in range(len(tiles)):
        for a, page in enumerate((page_a, page_b)):
            part = jnp.dot(page[h, :, :head_dim], tiles[h][a], preferred_element_type=jnp.float32)
            total = part if total is None else total + part
    return total


def pair_softmax(scores, limit):
    token = lax.broadcasted_iota(jnp.int32, scores.shape, 0)
    mask = token < limit
    masked = jnp.where(mask, scores, very_negative)
    top = jnp.max(masked, axis=0, keepdims=True)
    weights = jnp.where(mask, jnp.exp(masked - top), 0.0)
    return top, jnp.sum(weights, axis=0, keepdims=True), weights


def pair_values(weights, page_a, page_b, head_dim):
    turned = weights.T.astype(jnp.bfloat16)
    kv_heads = page_a.shape[0]
    group = 64 // kv_heads
    blocks = []
    for a, page in enumerate((page_a, page_b)):
        for h in range(kv_heads):
            at = a * 64 + h * group
            blocks.append(
                jnp.dot(turned[at : at + group], page[h, :, head_dim:], preferred_element_type=jnp.float32)
            )
    return jnp.concatenate(blocks, axis=0)


def to_columns(rows):
    stacked = jnp.concatenate(rows + [jnp.zeros((128 - len(rows), 128), jnp.float32)], axis=0)
    return stacked.T


def own_kernel(n_req, own_pages, *refs):
    (q_hbm, kv_hbm, slot_hbm, owner_hbm, len_hbm, pool_hbm) = refs[:6]
    acc_ref, log_ref, limit_ref, pages_ref = refs[6:10]
    q_row, q_heads, kv, slots, owners, lens, pool, small_sem, pool_sem, page_sem = refs[10:]
    slot_count, kv_heads, page_len, width = pool_hbm.shape
    head_dim = width // 2
    entries = slot_hbm.shape[2]
    me = lax.axis_index("req")
    scale = 1.0 / math.sqrt(head_dim)
    small = [
        pltpu.make_async_copy(src, dst, small_sem.at[i])
        for i, (src, dst) in enumerate(
            ((slot_hbm, slots), (owner_hbm, owners), (len_hbm, lens), (kv_hbm, kv), (q_hbm, q_row))
        )
    ]
    for copy in small:
        copy.start()
    whole = pltpu.make_async_copy(pool_hbm, pool, pool_sem)
    whole.start()
    for copy in small:
        copy.wait()

    fetched = []
    lane = lax.broadcasted_iota(jnp.int32, (1, 128), 1)
    limits = []
    for d in range(1, n_req):
        n = me ^ d
        length = lens[0, n]
        slot = jnp.int32(0)
        limit = jnp.int32(0)
        for j in range(entries):
            held = (owners[0, n, j] == me) & (j * page_len < length)
            slot = jnp.where(held, slots[0, n, j], slot)
            limit = jnp.where(held, length - j * page_len, limit)
        copy = pltpu.make_async_copy(pool_hbm.at[slot], pages_ref.at[d - 1], page_sem.at[d - 1])
        copy.start()
        fetched.append(copy)
        limits.append(limit)
    if len(limits) % 2:
        limits.append(jnp.int32(0))
    for p in range(len(limits) // 2):
        limit_ref[p : p + 1] = jnp.where(lane < 64, limits[2 * p], limits[2 * p + 1])

    lay_rows(q_heads, 0, q_row)
    q_heads[64:] = q_heads[:64]
    tiles = query_tiles(q_heads[...], kv_heads)
    my_length = lens[0, me]
    pages, valid = [], []
    for i in range(own_pages):
        held = (owners[0, me, i] == me) & (i * page_len < my_length)
        pages.append(pool.at[jnp.where(held, slots[0, me, i], 0)])
        valid.append(jnp.where(held, my_length - i * page_len, 0))
    if own_pages % 2:
        pages.append(pages[0])
        valid.append(jnp.int32(0))
    pairs = len(pages) // 2

    base = kv_heads * head_dim
    new_k = [kv[0:1, h * head_dim : (h + 1) * head_dim] for h in range(kv_heads)]
    self_score = None
    for h in range(kv_heads):
        both = tiles[h][0] + tiles[h][1]
        part = jnp.dot(jnp.broadcast_to(new_k[h], (16, head_dim)), both, preferred_element_type=jnp.float32)
        self_score = part if self_score is None else self_score + part
    self_score = self_score[0:1] * scale

    whole.wait()
    scores = [pair_scores(pages[2 * p], pages[2 * p + 1], tiles, head_dim) * scale for p in range(pairs)]
    tops, totals, sums = [], [], []
    for p in range(pairs):
        limit = jnp.where(lane < 64, valid[2 * p], valid[2 * p + 1])
        top, total, weights = pair_softmax(scores[p], limit)
        tops.append(top)
        totals.append(total)
        sums.append(pair_values(weights, pages[2 * p], pages[2 * p + 1], head_dim))
    top = functools.reduce(jnp.maximum, tops)
    top = jnp.maximum(jnp.maximum(top, halves(top)), self_score)
    factors = [jnp.exp(t - top) for t in tops]
    own_factor = jnp.exp(self_score - top)
    total = functools.reduce(jnp.add, [f * t for f, t in zip(factors, totals)])
    total = total + halves(total) + own_factor
    columns = to_columns([f / total for f in factors] + [own_factor / total])
    result = None
    for p in range(pairs):
        term = sums[p] * columns[:, p : p + 1]
        result = term if result is None else result + term
    group = 64 // kv_heads
    new_v = jnp.concatenate(
        [
            jnp.broadcast_to(kv[0:1, base + h * head_dim : base + (h + 1) * head_dim].astype(jnp.float32), (group, head_dim))
            for h in range(kv_heads)
        ],
        axis=0,
    )
    acc_ref[...] = result[:64] + result[64:] + columns[:64, pairs : pairs + 1] * new_v
    log_ref[...] = jnp.broadcast_to(top + jnp.log(total), log_ref.shape)
    for copy in fetched:
        copy.wait()


def own_attention(q, new_kv, page_slot, page_owner, context_len, pool, n_req):
    slots, kv_heads, page_len, width = pool.shape
    head_dim = width // 2
    heads = q.shape[1] // head_dim
    own_pages = min(slots, page_slot.shape[2])
    hbm = pl.BlockSpec(memory_space=pltpu.HBM)
    vmem = pl.BlockSpec(memory_space=pltpu.VMEM)
    pair_count = round_up(n_req - 1, 2) // 2
    page_bytes = pool.size * 2 // slots
    return pl.pallas_call(
        functools.partial(own_kernel, n_req, own_pages),
        out_shape=[
            jax.ShapeDtypeStruct((heads, head_dim), jnp.float32),
            jax.ShapeDtypeStruct((8, 128), jnp.float32),
            jax.ShapeDtypeStruct((round_up(pair_count, 8), 128), jnp.int32),
            jax.ShapeDtypeStruct((n_req - 1, kv_heads, page_len, width), pool.dtype),
        ],
        in_specs=[hbm] * 6,
        out_specs=[vmem] * 4,
        scratch_shapes=[
            pltpu.VMEM(q.shape, q.dtype),
            pltpu.VMEM((128, head_dim), jnp.float32),
            pltpu.VMEM(new_kv.shape, new_kv.dtype),
            pltpu.SMEM(page_slot.shape, jnp.int32),
            pltpu.SMEM(page_owner.shape, jnp.int32),
            pltpu.SMEM(context_len.shape, jnp.int32),
            pltpu.VMEM(pool.shape, pool.dtype),
            pltpu.SemaphoreType.DMA((5,)),
            pltpu.SemaphoreType.DMA,
            pltpu.SemaphoreType.DMA((n_req - 1,)),
        ],
        compiler_params=pltpu.CompilerParams(vmem_limit_bytes=16 * MIB),
        cost_estimate=pl.CostEstimate(
            flops=4 * own_pages * page_len * heads * head_dim,
            bytes_accessed=page_bytes * (slots + n_req - 1) * 2,
            transcendentals=0,
        ),
        name="own_attention",
    )(*(in_hbm(x) for x in (q, new_kv, page_slot, page_owner, context_len, pool)))


def stat_rows_of(n_req):
    return round_up(2 * n_req, 8)


def other_kernel(n_req, n_tp, *refs):
    q_refs = refs[: n_req - 1]
    acc_ref, log_ref, limit_ref, pages_ref = refs[n_req - 1 : n_req + 3]
    out_refs = refs[n_req + 3 : n_req + 5]
    results, logs, stats, q_heads = refs[n_req + 5 :]
    kv_heads, width = pages_ref.shape[1], pages_ref.shape[3]
    head_dim = width // 2
    heads = results.shape[1]
    chunk = heads // n_tp
    my_tp = lax.axis_index("tp")
    scale = 1.0 / math.sqrt(head_dim)
    others = n_req - 1
    pairs = round_up(others, 2) // 2
    results[0] = acc_ref[...]
    logs[0:1] = log_ref[0:1]
    scores, members = [], []
    for p in range(pairs):
        a, b = 2 * p, min(2 * p + 1, others - 1)
        members.append((a, b))
        lay_rows(q_heads.at[p], 0, q_refs[a])
        lay_rows(q_heads.at[p], 64, q_refs[b])
        tiles = query_tiles(q_heads[p], kv_heads)
        scores.append(pair_scores(pages_ref.at[a], pages_ref.at[b], tiles, head_dim) * scale)
    sums, inverse, log_rows = [], [], []
    for p in range(pairs):
        a, b = members[p]
        top, total, weights = pair_softmax(scores[p], limit_ref[p : p + 1])
        sums.append(pair_values(weights, pages_ref.at[a], pages_ref.at[b], head_dim))
        total = jnp.where(total > 0.0, total, 1.0)
        inverse.append(1.0 / total)
        log_rows.append(top + jnp.log(total))
    columns = to_columns(inverse)
    for p in range(pairs):
        result = sums[p] * columns[:, p : p + 1]
        results[2 * p + 1] = result[:64]
        logs[2 * p + 1 : 2 * p + 2] = log_rows[p]
        if 2 * p + 1 < others:
            results[2 * p + 2] = result[64:]
            logs[2 * p + 2 : 2 * p + 3] = halves(log_rows[p])
    lane = lax.broadcasted_iota(jnp.int32, (n_req, 128), 1)
    value = logs[0:n_req]
    high = value.astype(jnp.bfloat16).astype(jnp.float32)
    rest = value - high
    middle = rest.astype(jnp.bfloat16).astype(jnp.float32)
    stats[...] = jnp.zeros_like(stats)
    stats[0:n_req] = jnp.where(lane < 64, high, halves(middle))
    stats[n_req : 2 * n_req] = jnp.where(lane < 64, rest - middle, 0.0)
    tail = stats[...].astype(jnp.bfloat16)
    rows = n_req * chunk
    for d in range(n_tp):
        at = pl.ds(pl.multiple_of((my_tp ^ d) * chunk, chunk), chunk)
        for k in range(n_req):
            out_refs[d % 2][d // 2, k * chunk : (k + 1) * chunk] = results[k, at].astype(jnp.bfloat16)
        out_refs[d % 2][d // 2, rows:] = tail


def other_attention(q_list, own, n_req, n_tp):
    heads, head_dim = own[0].shape
    chunk = heads // n_tp
    rows = n_req * chunk + stat_rows_of(n_req)
    vmem = pl.BlockSpec(memory_space=pltpu.VMEM)
    return pl.pallas_call(
        functools.partial(other_kernel, n_req, n_tp),
        out_shape=[jax.ShapeDtypeStruct((n_tp // 2, rows, head_dim), jnp.bfloat16)] * 2,
        in_specs=[vmem] * (n_req + 3),
        out_specs=[vmem] * 2,
        scratch_shapes=[
            pltpu.VMEM((n_req, heads, head_dim), jnp.float32),
            pltpu.VMEM((round_up(n_req, 8), 128), jnp.float32),
            pltpu.VMEM((stat_rows_of(n_req), 128), jnp.float32),
            pltpu.VMEM((round_up(n_req - 1, 2) // 2, 128, head_dim), jnp.float32),
        ],
        compiler_params=pltpu.CompilerParams(vmem_limit_bytes=16 * MIB),
        cost_estimate=pl.CostEstimate(flops=2 * own[3].size * 16, bytes_accessed=own[3].size * 2, transcendentals=0),
        name="other_attention",
    )(*q_list, *own)


def row_copies(source, first, target, sems):
    parts = sems.shape[0]
    step = target.shape[0] // parts
    return [
        pltpu.make_async_copy(
            source.at[pl.ds(first + i * step, step)], target.at[pl.ds(i * step, step)], sems.at[i]
        )
        for i in range(parts)
    ]


def load_kernel(after_ref, weight_hbm, out_ref, sems):
    copies = row_copies(weight_hbm, 0, out_ref, sems)
    for copy in copies:
        copy.start()
    for copy in copies:
        copy.wait()


def load_weight(after, out_weight, rows):
    columns = out_weight.shape[1]
    return pl.pallas_call(
        load_kernel,
        out_shape=jax.ShapeDtypeStruct((rows, columns), out_weight.dtype),
        in_specs=[pl.BlockSpec(memory_space=pl.ANY), pl.BlockSpec(memory_space=pltpu.HBM)],
        out_specs=pl.BlockSpec(memory_space=pltpu.VMEM),
        scratch_shapes=[pltpu.SemaphoreType.DMA((4,))],
        compiler_params=pltpu.CompilerParams(vmem_limit_bytes=20 * MIB),
        cost_estimate=pl.CostEstimate(flops=0, bytes_accessed=rows * columns * 4, transcendentals=0),
        name="load_weight",
    )(after, in_hbm(out_weight))


def project_kernel(n_req, n_tp, chunk, *refs):
    part_refs = refs[:n_req]
    first_ref, weight_hbm = refs[n_req : n_req + 2]
    kept_ref, sent_ref = refs[n_req + 2 : n_req + 4]
    wide, logs, attention, second, sums, sems = refs[n_req + 4 :]
    rows = n_req * chunk
    total_rows = n_tp * n_req
    early, columns = first_ref.shape
    my_tp = lax.axis_index("tp")
    me = lax.axis_index("req")
    copies = row_copies(weight_hbm, early, second, sems)
    for copy in copies:
        copy.start()
    for r in range(n_req):
        for c in range(n_tp):
            col = my_tp ^ c
            block = part_refs[r][c, :rows].astype(jnp.float32)
            tail = part_refs[r][c, rows:].astype(jnp.float32)
            value = (tail[:n_req] + halves(tail[:n_req])) + tail[n_req : 2 * n_req]
            for k in range(n_req):
                row = col * n_req + (me ^ r ^ k)
                wide[r, pl.ds(pl.multiple_of(row * chunk, chunk), chunk)] = block[k * chunk : (k + 1) * chunk]
                logs[r, pl.ds(row, 1)] = value[k : k + 1]
    shift = (128 - my_tp * chunk) % 128
    values = [pltpu.roll(logs[r], shift, 1) for r in range(n_req)]
    top = functools.reduce(jnp.maximum, values)
    factors = [jnp.exp(v - top) for v in values]
    total = functools.reduce(jnp.add, factors)
    factors = [f / total for f in factors]
    for h in range(chunk):
        block = None
        for r in range(n_req):
            term = wide[r, pl.ds(h, total_rows, stride=chunk)] * factors[r][:, h : h + 1]
            block = term if block is None else block + term
        attention[:, h * 128 : (h + 1) * 128] = block.astype(jnp.bfloat16)
    tile = min(columns, 512)

    @pl.loop(0, columns // tile)
    def _(t):
        at = pl.ds(pl.multiple_of(t * tile, tile), tile)
        product = jnp.dot(attention[:, :early], first_ref[:, at], preferred_element_type=jnp.float32)
        for c in range(n_tp):
            sums[c, :, at] = product[c * n_req : (c + 1) * n_req]

    for copy in copies:
        copy.wait()

    @pl.loop(0, columns // tile)
    def _(t):
        at = pl.ds(pl.multiple_of(t * tile, tile), tile)
        product = jnp.dot(attention[:, early:], second[:, at], preferred_element_type=jnp.float32)
        for c in range(n_tp):
            sums[c, :, at] += product[c * n_req : (c + 1) * n_req]

    for d in range(n_tp):
        target = (kept_ref, sent_ref)[d % 2]
        target[d // 2] = sums[my_tp ^ d].astype(target.dtype)


def project(parts, first, out_weight, n_req, n_tp, chunk):
    depth, columns = out_weight.shape
    rows = n_req * chunk
    vmem = pl.BlockSpec(memory_space=pltpu.VMEM)
    total_rows = n_tp * n_req
    return pl.pallas_call(
        functools.partial(project_kernel, n_req, n_tp, chunk),
        out_shape=[
            jax.ShapeDtypeStruct((n_tp // 2, n_req, columns), jnp.float32),
            jax.ShapeDtypeStruct((n_tp // 2, n_req, columns), jnp.bfloat16),
        ],
        in_specs=[vmem] * (n_req + 1) + [pl.BlockSpec(memory_space=pltpu.HBM)],
        out_specs=[vmem] * 2,
        scratch_shapes=[
            pltpu.VMEM((n_req, n_tp * rows, 128), jnp.float32),
            pltpu.VMEM((n_req, total_rows, 128), jnp.float32),
            pltpu.VMEM((total_rows, depth), jnp.bfloat16),
            pltpu.VMEM((depth - first.shape[0], columns), jnp.bfloat16),
            pltpu.VMEM((n_tp, n_req, columns), jnp.float32),
            pltpu.SemaphoreType.DMA((4,)),
        ],
        compiler_params=pltpu.CompilerParams(vmem_limit_bytes=24 * MIB),
        cost_estimate=pl.CostEstimate(
            flops=2 * total_rows * depth * columns, bytes_accessed=depth * columns * 2, transcendentals=0
        ),
        name="project",
    )(*parts, first, in_hbm(out_weight))


def on_device(queries, new_kv, cache_pool, page_slot, page_owner, context_len, out_weight):
    n_req = lax.axis_size("req")
    n_tp = lax.axis_size("tp")
    pool = cache_pool[0, 0]
    head_dim = pool.shape[3] // 2
    chunk = queries.shape[1] // head_dim // n_tp
    q_list = [swap(queries, "req", d) for d in range(1, n_req)]
    own = own_attention(queries, new_kv, page_slot, page_owner, context_len, pool, n_req)
    even, odd = other_attention(q_list, own, n_req, n_tp)
    beside = swap(odd, "tp", 1)
    arrived = [even[0], beside[0]]
    for e in range(1, n_tp // 2):
        pair = swap(jnp.stack([even[e], beside[e]]), "tp", 2 * e)
        arrived += [pair[0], pair[1]]
    arrived = jnp.stack(arrived)
    parts = [arrived] + [swap(arrived, "req", d) for d in range(1, n_req)]
    depth = out_weight.shape[0]
    first = load_weight(arrived, out_weight, depth * 5 // 8)
    kept, sent = project(parts, first, out_weight, n_req, n_tp, chunk)
    both = kept + swap(sent, "tp", 1).astype(jnp.float32)
    total = both[0]
    for e in range(1, n_tp // 2):
        total = total + swap(both[e].astype(jnp.bfloat16), "tp", 2 * e).astype(jnp.float32)
    return total.astype(jnp.bfloat16)


def solution(mesh):
    placed = (
        P(("groups", "tp", "req"), None),
        P(("groups", "tp", "req"), None),
        P(("groups", "tp"), "req", None, None, None, None),
        P(("groups", "tp"), None, None),
        P(("groups", "tp"), None, None),
        P(("groups", "tp"), None),
        P("tp", "req"),
    )
    return jax.shard_map(
        on_device, mesh=mesh, in_specs=placed, out_specs=P(("groups", "tp"), "req"), check_vma=False
    )
```

```python
import functools
import math

import jax
import jax.numpy as jnp
from jax import lax
from jax.experimental import pallas as pl
from jax.experimental.pallas import tpu as pltpu
from jax.sharding import PartitionSpec as P

very_negative = -1e30
MIB = 1 << 20


def swap(x, axis, offset):
    count = lax.axis_size(axis)
    return lax.ppermute(x, axis, [(i, i ^ offset) for i in range(count)])


def in_hbm(x):
    return pltpu.with_memory_space_constraint(x, pltpu.HBM)


def round_up(value, step):
    return -(-value // step) * step


def halves(x):
    return pltpu.roll(x, 64, 1)


def lay_rows(places, q_ref):
    head_dim = places[0][0].shape[1]
    for h in range(64):
        block = q_ref[:, h * head_dim : (h + 1) * head_dim].astype(jnp.float32)
        for i, (target, start) in enumerate(places):
            target[start + h : start + h + 1] = block[i : i + 1]


def query_tiles(stacked, kv_heads):
    turned = stacked.T
    lane = lax.broadcasted_iota(jnp.int32, turned.shape, 1)
    group = 64 // kv_heads
    return [
        [
            jnp.where((lane >= a * 64 + h * group) & (lane < a * 64 + (h + 1) * group), turned, 0.0).astype(jnp.bfloat16)
            for a in range(2)
        ]
        for h in range(kv_heads)
    ]


def pair_scores(page_a, page_b, tiles, head_dim):
    total = None
    for h in range(len(tiles)):
        for a, page in enumerate((page_a, page_b)):
            part = jnp.dot(page[h, :, :head_dim], tiles[h][a], preferred_element_type=jnp.float32)
            total = part if total is None else total + part
    return total


def pair_softmax(scores, limit):
    token = lax.broadcasted_iota(jnp.int32, scores.shape, 0)
    mask = token < limit
    masked = jnp.where(mask, scores, very_negative)
    top = jnp.max(masked, axis=0, keepdims=True)
    weights = jnp.where(mask, jnp.exp(masked - top), 0.0)
    return top, jnp.sum(weights, axis=0, keepdims=True), weights


def pair_values(weights, page_a, page_b, head_dim):
    turned = weights.T.astype(jnp.bfloat16)
    kv_heads = page_a.shape[0]
    group = 64 // kv_heads
    blocks = []
    for a, page in enumerate((page_a, page_b)):
        for h in range(kv_heads):
            at = a * 64 + h * group
            blocks.append(
                jnp.dot(turned[at : at + group], page[h, :, head_dim:], preferred_element_type=jnp.float32)
            )
    return jnp.concatenate(blocks, axis=0)


def to_columns(rows):
    stacked = jnp.concatenate(rows + [jnp.zeros((128 - len(rows), 128), jnp.float32)], axis=0)
    return stacked.T


def own_kernel(n_req, own_pages, *refs):
    (q_hbm, kv_hbm, slot_hbm, owner_hbm, len_hbm, pool_hbm) = refs[:6]
    acc_ref, log_ref, limit_ref, pages_ref = refs[7:11]
    q_row, q_heads, kv, slots, owners, lens, pool, small_sem, pool_sem, page_sem = refs[11:]
    slot_count, kv_heads, page_len, width = pool_hbm.shape
    head_dim = width // 2
    entries = slot_hbm.shape[2]
    me = lax.axis_index("req")
    scale = 1.0 / math.sqrt(head_dim)
    small = [
        pltpu.make_async_copy(src, dst, small_sem.at[i])
        for i, (src, dst) in enumerate(
            ((slot_hbm, slots), (owner_hbm, owners), (len_hbm, lens), (kv_hbm, kv), (q_hbm, q_row))
        )
    ]
    for copy in small:
        copy.start()
    whole = pltpu.make_async_copy(pool_hbm, pool, pool_sem)
    whole.start()
    for copy in small:
        copy.wait()

    fetched = []
    lane = lax.broadcasted_iota(jnp.int32, (1, 128), 1)
    limits = []
    for d in range(1, n_req):
        n = me ^ d
        length = lens[0, n]
        slot = jnp.int32(0)
        limit = jnp.int32(0)
        for j in range(entries):
            held = (owners[0, n, j] == me) & (j * page_len < length)
            slot = jnp.where(held, slots[0, n, j], slot)
            limit = jnp.where(held, length - j * page_len, limit)
        copy = pltpu.make_async_copy(pool_hbm.at[slot], pages_ref.at[d - 1], page_sem.at[d - 1])
        copy.start()
        fetched.append(copy)
        limits.append(limit)
    if len(limits) % 2:
        limits.append(jnp.int32(0))
    for p in range(len(limits) // 2):
        limit_ref[p : p + 1] = jnp.where(lane < 64, limits[2 * p], limits[2 * p + 1])

    lay_rows([(q_heads, 0)], q_row)
    q_heads[64:] = q_heads[:64]
    tiles = query_tiles(q_heads[...], kv_heads)
    my_length = lens[0, me]
    pages, valid = [], []
    for i in range(own_pages):
        held = (owners[0, me, i] == me) & (i * page_len < my_length)
        pages.append(pool.at[jnp.where(held, slots[0, me, i], 0)])
        valid.append(jnp.where(held, my_length - i * page_len, 0))
    if own_pages % 2:
        pages.append(pages[0])
        valid.append(jnp.int32(0))
    pairs = len(pages) // 2

    base = kv_heads * head_dim
    new_k = [kv[0:1, h * head_dim : (h + 1) * head_dim] for h in range(kv_heads)]
    self_score = None
    for h in range(kv_heads):
        both = tiles[h][0] + tiles[h][1]
        part = jnp.dot(jnp.broadcast_to(new_k[h], (16, head_dim)), both, preferred_element_type=jnp.float32)
        self_score = part if self_score is None else self_score + part
    self_score = self_score[0:1] * scale

    whole.wait()
    scores = [pair_scores(pages[2 * p], pages[2 * p + 1], tiles, head_dim) * scale for p in range(pairs)]
    tops, totals, sums = [], [], []
    for p in range(pairs):
        limit = jnp.where(lane < 64, valid[2 * p], valid[2 * p + 1])
        top, total, weights = pair_softmax(scores[p], limit)
        tops.append(top)
        totals.append(total)
        sums.append(pair_values(weights, pages[2 * p], pages[2 * p + 1], head_dim))
    top = functools.reduce(jnp.maximum, tops)
    top = jnp.maximum(jnp.maximum(top, halves(top)), self_score)
    factors = [jnp.exp(t - top) for t in tops]
    own_factor = jnp.exp(self_score - top)
    total = functools.reduce(jnp.add, [f * t for f, t in zip(factors, totals)])
    total = total + halves(total) + own_factor
    columns = to_columns([f / total for f in factors] + [own_factor / total])
    result = None
    for p in range(pairs):
        term = sums[p] * columns[:, p : p + 1]
        result = term if result is None else result + term
    group = 64 // kv_heads
    new_v = jnp.concatenate(
        [
            jnp.broadcast_to(kv[0:1, base + h * head_dim : base + (h + 1) * head_dim].astype(jnp.float32), (group, head_dim))
            for h in range(kv_heads)
        ],
        axis=0,
    )
    acc_ref[...] = result[:64] + result[64:] + columns[:64, pairs : pairs + 1] * new_v
    log_ref[...] = jnp.broadcast_to(top + jnp.log(total), log_ref.shape)
    for copy in fetched:
        copy.wait()


def own_attention(q, new_kv, page_slot, page_owner, context_len, pool, after, n_req):
    slots, kv_heads, page_len, width = pool.shape
    head_dim = width // 2
    heads = q.shape[1] // head_dim
    own_pages = min(slots, page_slot.shape[2])
    hbm = pl.BlockSpec(memory_space=pltpu.HBM)
    vmem = pl.BlockSpec(memory_space=pltpu.VMEM)
    pair_count = round_up(n_req - 1, 2) // 2
    page_bytes = pool.size * 2 // slots
    return pl.pallas_call(
        functools.partial(own_kernel, n_req, own_pages),
        out_shape=[
            jax.ShapeDtypeStruct((heads, head_dim), jnp.float32),
            jax.ShapeDtypeStruct((8, 128), jnp.float32),
            jax.ShapeDtypeStruct((round_up(pair_count, 8), 128), jnp.int32),
            jax.ShapeDtypeStruct((n_req - 1, kv_heads, page_len, width), pool.dtype),
        ],
        in_specs=[hbm] * 6 + [pl.BlockSpec(memory_space=pl.ANY)],
        out_specs=[vmem] * 4,
        scratch_shapes=[
            pltpu.VMEM(q.shape, q.dtype),
            pltpu.VMEM((128, head_dim), jnp.float32),
            pltpu.VMEM(new_kv.shape, new_kv.dtype),
            pltpu.SMEM(page_slot.shape, jnp.int32),
            pltpu.SMEM(page_owner.shape, jnp.int32),
            pltpu.SMEM(context_len.shape, jnp.int32),
            pltpu.VMEM(pool.shape, pool.dtype),
            pltpu.SemaphoreType.DMA((5,)),
            pltpu.SemaphoreType.DMA,
            pltpu.SemaphoreType.DMA((n_req - 1,)),
        ],
        compiler_params=pltpu.CompilerParams(vmem_limit_bytes=16 * MIB),
        cost_estimate=pl.CostEstimate(
            flops=4 * own_pages * page_len * heads * head_dim,
            bytes_accessed=page_bytes * (slots + n_req - 1) * 2,
            transcendentals=0,
        ),
        name="own_attention",
    )(*(in_hbm(x) for x in (q, new_kv, page_slot, page_owner, context_len, pool)), after)


def stat_rows_of(n_req):
    return round_up(2 * n_req, 8)


def other_kernel(n_req, n_tp, *refs):
    count = n_req.bit_length() - 1
    acc_ref, log_ref, limit_ref, pages_ref = refs[count : count + 4]
    out_refs = refs[count + 4 : count + 4 + n_tp]
    results, logs, stats, q_heads = refs[count + 4 + n_tp :]
    kv_heads, width = pages_ref.shape[1], pages_ref.shape[3]
    head_dim = width // 2
    heads = results.shape[1]
    chunk = heads // n_tp
    my_tp = lax.axis_index("tp")
    scale = 1.0 / math.sqrt(head_dim)
    others = n_req - 1
    pairs = round_up(others, 2) // 2
    results[0] = acc_ref[...]
    logs[0:1] = log_ref[0:1]
    for k in range(count):
        lay_rows([(q_heads.at[(d - 1) // 2], (d - 1) % 2 * 64) for d in range(1 << k, 2 << k)], refs[k])
    if others % 2:
        q_heads[pairs - 1, 64:] = q_heads[pairs - 1, :64]
    scores, members = [], []
    for p in range(pairs):
        a, b = 2 * p, min(2 * p + 1, others - 1)
        members.append((a, b))
        tiles = query_tiles(q_heads[p], kv_heads)
        scores.append(pair_scores(pages_ref.at[a], pages_ref.at[b], tiles, head_dim) * scale)
    sums, inverse, log_rows = [], [], []
    for p in range(pairs):
        a, b = members[p]
        top, total, weights = pair_softmax(scores[p], limit_ref[p : p + 1])
        sums.append(pair_values(weights, pages_ref.at[a], pages_ref.at[b], head_dim))
        total = jnp.where(total > 0.0, total, 1.0)
        inverse.append(1.0 / total)
        log_rows.append(top + jnp.log(total))
    columns = to_columns(inverse)
    for p in range(pairs):
        result = sums[p] * columns[:, p : p + 1]
        results[2 * p + 1] = result[:64]
        logs[2 * p + 1 : 2 * p + 2] = log_rows[p]
        if 2 * p + 1 < others:
            results[2 * p + 2] = result[64:]
            logs[2 * p + 2 : 2 * p + 3] = halves(log_rows[p])
    lane = lax.broadcasted_iota(jnp.int32, (n_req, 128), 1)
    value = logs[0:n_req]
    high = value.astype(jnp.bfloat16).astype(jnp.float32)
    rest = value - high
    middle = rest.astype(jnp.bfloat16).astype(jnp.float32)
    stats[...] = jnp.zeros_like(stats)
    stats[0:n_req] = jnp.where(lane < 64, high, halves(middle))
    stats[n_req : 2 * n_req] = jnp.where(lane < 64, rest - middle, 0.0)
    tail = stats[...].astype(jnp.bfloat16)
    rows = n_req * chunk
    for d in range(n_tp):
        at = pl.ds(pl.multiple_of((my_tp ^ d) * chunk, chunk), chunk)
        for k in range(n_req):
            out_refs[d][k * chunk : (k + 1) * chunk] = results[k, at].astype(jnp.bfloat16)
        out_refs[d][rows:] = tail


def other_attention(q_list, own, n_req, n_tp):
    heads, head_dim = own[0].shape
    chunk = heads // n_tp
    rows = n_req * chunk + stat_rows_of(n_req)
    vmem = pl.BlockSpec(memory_space=pltpu.VMEM)
    return pl.pallas_call(
        functools.partial(other_kernel, n_req, n_tp),
        out_shape=[jax.ShapeDtypeStruct((rows, head_dim), jnp.bfloat16)] * n_tp,
        in_specs=[vmem] * (len(q_list) + 4),
        out_specs=[vmem] * n_tp,
        scratch_shapes=[
            pltpu.VMEM((n_req, heads, head_dim), jnp.float32),
            pltpu.VMEM((round_up(n_req, 8), 128), jnp.float32),
            pltpu.VMEM((stat_rows_of(n_req), 128), jnp.float32),
            pltpu.VMEM((round_up(n_req - 1, 2) // 2, 128, head_dim), jnp.float32),
        ],
        compiler_params=pltpu.CompilerParams(vmem_limit_bytes=16 * MIB),
        cost_estimate=pl.CostEstimate(flops=2 * own[3].size * 16, bytes_accessed=own[3].size * 2, transcendentals=0),
        name="other_attention",
    )(*q_list, *own)


def row_copies(source, first, target, sems):
    parts = sems.shape[0]
    step = target.shape[0] // parts
    return [
        pltpu.make_async_copy(
            source.at[pl.ds(first + i * step, step)], target.at[pl.ds(i * step, step)], sems.at[i]
        )
        for i in range(parts)
    ]


def load_kernel(first, piece_ref, weight_hbm, out_ref, same_ref, sems):
    copies = row_copies(weight_hbm, first, out_ref, sems)
    for copy in copies:
        copy.start()
    same_ref[...] = piece_ref[...]
    for copy in copies:
        copy.wait()


def load_weight(piece, out_weight, first, rows):
    columns = out_weight.shape[1]
    vmem = pl.BlockSpec(memory_space=pltpu.VMEM)
    return pl.pallas_call(
        functools.partial(load_kernel, first),
        out_shape=[
            jax.ShapeDtypeStruct((rows, columns), out_weight.dtype),
            jax.ShapeDtypeStruct(piece.shape, piece.dtype),
        ],
        in_specs=[vmem, pl.BlockSpec(memory_space=pltpu.HBM)],
        out_specs=[vmem] * 2,
        scratch_shapes=[pltpu.SemaphoreType.DMA((4,))],
        compiler_params=pltpu.CompilerParams(vmem_limit_bytes=20 * MIB),
        cost_estimate=pl.CostEstimate(flops=0, bytes_accessed=rows * columns * 4, transcendentals=0),
        name="load_weight",
    )(piece, in_hbm(out_weight))


def project_kernel(n_req, n_tp, chunk, *refs):
    part_refs = refs[:n_req]
    weight_refs = refs[n_req : n_req + 2]
    out_refs = refs[n_req + 2 : n_req + 2 + n_tp]
    wide, logs, attention, sums = refs[n_req + 2 + n_tp :]
    rows = n_req * chunk
    total_rows = n_tp * n_req
    split, columns = weight_refs[0].shape
    my_tp = lax.axis_index("tp")
    me = lax.axis_index("req")
    for r in range(n_req):
        for c in range(n_tp):
            col = my_tp ^ c
            block = part_refs[r][c, :rows].astype(jnp.float32)
            tail = part_refs[r][c, rows:].astype(jnp.float32)
            value = (tail[:n_req] + halves(tail[:n_req])) + tail[n_req : 2 * n_req]
            for k in range(n_req):
                row = col * n_req + (me ^ r ^ k)
                wide[r, pl.ds(pl.multiple_of(row * chunk, chunk), chunk)] = block[k * chunk : (k + 1) * chunk]
                logs[r, pl.ds(row, 1)] = value[k : k + 1]
    shift = (128 - my_tp * chunk) % 128
    values = [pltpu.roll(logs[r], shift, 1) for r in range(n_req)]
    top = functools.reduce(jnp.maximum, values)
    factors = [jnp.exp(v - top) for v in values]
    total = functools.reduce(jnp.add, factors)
    factors = [f / total for f in factors]
    for h in range(chunk):
        block = None
        for r in range(n_req):
            term = wide[r, pl.ds(h, total_rows, stride=chunk)] * factors[r][:, h : h + 1]
            block = term if block is None else block + term
        attention[:, h * 128 : (h + 1) * 128] = block.astype(jnp.bfloat16)
    tile = min(columns, 512)

    @pl.loop(0, columns // tile)
    def _(t):
        at = pl.ds(pl.multiple_of(t * tile, tile), tile)
        product = jnp.dot(attention[:, :split], weight_refs[0][:, at], preferred_element_type=jnp.float32)
        product += jnp.dot(attention[:, split:], weight_refs[1][:, at], preferred_element_type=jnp.float32)
        for c in range(n_tp):
            sums[c, :, at] = product[c * n_req : (c + 1) * n_req]

    for d in range(n_tp):
        out_refs[d][...] = sums[my_tp ^ d].astype(out_refs[d].dtype)


def project(parts, weights, n_req, n_tp, chunk):
    depth = sum(w.shape[0] for w in weights)
    columns = weights[0].shape[1]
    rows = n_req * chunk
    vmem = pl.BlockSpec(memory_space=pltpu.VMEM)
    own = jax.ShapeDtypeStruct((n_req, columns), jnp.float32)
    sent = jax.ShapeDtypeStruct((n_req, columns), jnp.bfloat16)
    total_rows = n_tp * n_req
    return pl.pallas_call(
        functools.partial(project_kernel, n_req, n_tp, chunk),
        out_shape=[own] + [sent] * (n_tp - 1),
        in_specs=[vmem] * (n_req + 2),
        out_specs=[vmem] * n_tp,
        scratch_shapes=[
            pltpu.VMEM((n_req, n_tp * rows, 128), jnp.float32),
            pltpu.VMEM((n_req, total_rows, 128), jnp.float32),
            pltpu.VMEM((total_rows, depth), jnp.bfloat16),
            pltpu.VMEM((n_tp, n_req, columns), jnp.float32),
        ],
        compiler_params=pltpu.CompilerParams(vmem_limit_bytes=24 * MIB),
        cost_estimate=pl.CostEstimate(
            flops=2 * total_rows * depth * columns, bytes_accessed=depth * columns * 2, transcendentals=0
        ),
        name="project",
    )(*parts, *weights)


def on_device(queries, new_kv, cache_pool, page_slot, page_owner, context_len, out_weight):
    n_req = lax.axis_size("req")
    n_tp = lax.axis_size("tp")
    pool = cache_pool[0, 0]
    head_dim = pool.shape[3] // 2
    chunk = queries.shape[1] // head_dim // n_tp
    held, q_list = queries, []
    for k in range(n_req.bit_length() - 1):
        q_list.append(swap(held, "req", 1 << k))
        held = jnp.concatenate([held, q_list[-1]], axis=0)
    own = own_attention(queries, new_kv, page_slot, page_owner, context_len, pool, q_list[0], n_req)
    pieces = other_attention(q_list, own, n_req, n_tp)
    depth = out_weight.shape[0]
    early = depth * 5 // 16
    swapped = [swap(pieces[d], "tp", d) for d in range(1, n_tp)]
    first, mine = load_weight(pieces[0], out_weight, 0, early)
    arrived = jnp.stack([mine] + swapped)
    parts = [swap(arrived, "req", d) for d in range(1, n_req)]
    second, mine = load_weight(arrived, out_weight, early, depth - early)
    sums = project([mine] + parts, (first, second), n_req, n_tp, chunk)
    total = sums[0]
    for d in range(1, n_tp):
        total = total + swap(sums[d], "tp", d).astype(jnp.float32)
    return total.astype(jnp.bfloat16)


def solution(mesh):
    placed = (
        P(("groups", "tp", "req"), None),
        P(("groups", "tp", "req"), None),
        P(("groups", "tp"), "req", None, None, None, None),
        P(("groups", "tp"), None, None),
        P(("groups", "tp"), None, None),
        P(("groups", "tp"), None),
        P("tp", "req"),
    )
    return jax.shard_map(
        on_device, mesh=mesh, in_specs=placed, out_specs=P(("groups", "tp"), "req"), check_vma=False
    )
```

```python
import functools
import math

import jax
import jax.numpy as jnp
from jax import lax
from jax.experimental import pallas as pl
from jax.experimental.pallas import tpu as pltpu
from jax.sharding import PartitionSpec as P

very_negative = -1e30
MIB = 1 << 20


def swap(x, axis, offset):
    count = lax.axis_size(axis)
    return lax.ppermute(x, axis, [(i, i ^ offset) for i in range(count)])


def in_hbm(x):
    return pltpu.with_memory_space_constraint(x, pltpu.HBM)


def round_up(value, step):
    return -(-value // step) * step


def halves(x):
    return pltpu.roll(x, 64, 1)


def query_tiles(stacked, kv_heads):
    turned = stacked.astype(jnp.float32).T
    lane = lax.broadcasted_iota(jnp.int32, turned.shape, 1)
    group = 64 // kv_heads
    return [
        [
            jnp.where((lane >= a * 64 + h * group) & (lane < a * 64 + (h + 1) * group), turned, 0.0).astype(jnp.bfloat16)
            for a in range(2)
        ]
        for h in range(kv_heads)
    ]


def pair_scores(page_a, page_b, tiles, head_dim):
    total = None
    for h in range(len(tiles)):
        for a, page in enumerate((page_a, page_b)):
            part = jnp.dot(page[h, :, :head_dim], tiles[h][a], preferred_element_type=jnp.float32)
            total = part if total is None else total + part
    return total


def pair_softmax(scores, limit):
    token = lax.broadcasted_iota(jnp.int32, scores.shape, 0)
    mask = token < limit
    masked = jnp.where(mask, scores, very_negative)
    top = jnp.max(masked, axis=0, keepdims=True)
    weights = jnp.where(mask, jnp.exp(masked - top), 0.0)
    return top, jnp.sum(weights, axis=0, keepdims=True), weights


def pair_values(weights, page_a, page_b, head_dim):
    turned = weights.T.astype(jnp.bfloat16)
    kv_heads = page_a.shape[0]
    group = 64 // kv_heads
    blocks = []
    for a, page in enumerate((page_a, page_b)):
        for h in range(kv_heads):
            at = a * 64 + h * group
            blocks.append(
                jnp.dot(turned[at : at + group], page[h, :, head_dim:], preferred_element_type=jnp.float32)
            )
    return jnp.concatenate(blocks, axis=0)


def to_columns(rows):
    stacked = jnp.concatenate(rows + [jnp.zeros((128 - len(rows), 128), jnp.float32)], axis=0)
    return stacked.T


def own_kernel(n_req, own_pages, *refs):
    q_ref, kv_hbm, slot_hbm, owner_hbm, len_hbm, pool_hbm = refs[:6]
    acc_ref, log_ref, limit_ref, pages_ref = refs[6:10]
    kv, slots, owners, lens, pool, small_sem, pool_sem, page_sem = refs[10:]
    slot_count, kv_heads, page_len, width = pool_hbm.shape
    head_dim = width // 2
    entries = slot_hbm.shape[2]
    me = lax.axis_index("req")
    scale = 1.0 / math.sqrt(head_dim)
    small = [
        pltpu.make_async_copy(src, dst, small_sem.at[i])
        for i, (src, dst) in enumerate(
            ((slot_hbm, slots), (owner_hbm, owners), (len_hbm, lens), (kv_hbm, kv))
        )
    ]
    for copy in small:
        copy.start()
    whole = pltpu.make_async_copy(pool_hbm, pool, pool_sem)
    whole.start()
    tiles = query_tiles(jnp.concatenate([q_ref[...], q_ref[...]], axis=0), kv_heads)
    for copy in small:
        copy.wait()

    fetched = []
    lane = lax.broadcasted_iota(jnp.int32, (1, 128), 1)
    limits = []
    for d in range(1, n_req):
        n = me ^ d
        length = lens[0, n]
        slot = jnp.int32(0)
        limit = jnp.int32(0)
        for j in range(entries):
            held = (owners[0, n, j] == me) & (j * page_len < length)
            slot = jnp.where(held, slots[0, n, j], slot)
            limit = jnp.where(held, length - j * page_len, limit)
        copy = pltpu.make_async_copy(pool_hbm.at[slot], pages_ref.at[d - 1], page_sem.at[d - 1])
        copy.start()
        fetched.append(copy)
        limits.append(limit)
    if len(limits) % 2:
        limits.append(jnp.int32(0))
    for p in range(len(limits) // 2):
        limit_ref[p : p + 1] = jnp.where(lane < 64, limits[2 * p], limits[2 * p + 1])

    my_length = lens[0, me]
    pages, valid = [], []
    for i in range(own_pages):
        held = (owners[0, me, i] == me) & (i * page_len < my_length)
        pages.append(pool.at[jnp.where(held, slots[0, me, i], 0)])
        valid.append(jnp.where(held, my_length - i * page_len, 0))
    if own_pages % 2:
        pages.append(pages[0])
        valid.append(jnp.int32(0))
    pairs = len(pages) // 2

    base = kv_heads * head_dim
    new_k = [kv[0:1, h * head_dim : (h + 1) * head_dim] for h in range(kv_heads)]
    self_score = None
    for h in range(kv_heads):
        both = tiles[h][0] + tiles[h][1]
        part = jnp.dot(jnp.broadcast_to(new_k[h], (16, head_dim)), both, preferred_element_type=jnp.float32)
        self_score = part if self_score is None else self_score + part
    self_score = self_score[0:1] * scale

    whole.wait()
    scores = [pair_scores(pages[2 * p], pages[2 * p + 1], tiles, head_dim) * scale for p in range(pairs)]
    tops, totals, sums = [], [], []
    for p in range(pairs):
        limit = jnp.where(lane < 64, valid[2 * p], valid[2 * p + 1])
        top, total, weights = pair_softmax(scores[p], limit)
        tops.append(top)
        totals.append(total)
        sums.append(pair_values(weights, pages[2 * p], pages[2 * p + 1], head_dim))
    top = functools.reduce(jnp.maximum, tops)
    top = jnp.maximum(jnp.maximum(top, halves(top)), self_score)
    factors = [jnp.exp(t - top) for t in tops]
    own_factor = jnp.exp(self_score - top)
    total = functools.reduce(jnp.add, [f * t for f, t in zip(factors, totals)])
    total = total + halves(total) + own_factor
    columns = to_columns([f / total for f in factors] + [own_factor / total])
    result = None
    for p in range(pairs):
        term = sums[p] * columns[:, p : p + 1]
        result = term if result is None else result + term
    group = 64 // kv_heads
    new_v = jnp.concatenate(
        [
            jnp.broadcast_to(kv[0:1, base + h * head_dim : base + (h + 1) * head_dim].astype(jnp.float32), (group, head_dim))
            for h in range(kv_heads)
        ],
        axis=0,
    )
    acc_ref[...] = result[:64] + result[64:] + columns[:64, pairs : pairs + 1] * new_v
    log_ref[...] = jnp.broadcast_to(top + jnp.log(total), log_ref.shape)
    for copy in fetched:
        copy.wait()


def own_attention(q, new_kv, page_slot, page_owner, context_len, pool, n_req):
    slots, kv_heads, page_len, width = pool.shape
    head_dim = width // 2
    heads = q.shape[0]
    own_pages = min(slots, page_slot.shape[2])
    hbm = pl.BlockSpec(memory_space=pltpu.HBM)
    vmem = pl.BlockSpec(memory_space=pltpu.VMEM)
    pair_count = round_up(n_req - 1, 2) // 2
    page_bytes = pool.size * 2 // slots
    return pl.pallas_call(
        functools.partial(own_kernel, n_req, own_pages),
        out_shape=[
            jax.ShapeDtypeStruct((heads, head_dim), jnp.float32),
            jax.ShapeDtypeStruct((8, 128), jnp.float32),
            jax.ShapeDtypeStruct((round_up(pair_count, 8), 128), jnp.int32),
            jax.ShapeDtypeStruct((n_req - 1, kv_heads, page_len, width), pool.dtype),
        ],
        in_specs=[vmem] + [hbm] * 5,
        out_specs=[vmem] * 4,
        scratch_shapes=[
            pltpu.VMEM(new_kv.shape, new_kv.dtype),
            pltpu.SMEM(page_slot.shape, jnp.int32),
            pltpu.SMEM(page_owner.shape, jnp.int32),
            pltpu.SMEM(context_len.shape, jnp.int32),
            pltpu.VMEM(pool.shape, pool.dtype),
            pltpu.SemaphoreType.DMA((4,)),
            pltpu.SemaphoreType.DMA,
            pltpu.SemaphoreType.DMA((n_req - 1,)),
        ],
        compiler_params=pltpu.CompilerParams(vmem_limit_bytes=16 * MIB),
        cost_estimate=pl.CostEstimate(
            flops=4 * own_pages * page_len * heads * head_dim,
            bytes_accessed=page_bytes * (slots + n_req - 1) * 2,
            transcendentals=0,
        ),
        name="own_attention",
    )(q, *(in_hbm(x) for x in (new_kv, page_slot, page_owner, context_len, pool)))


def other_kernel(n_req, n_tp, *refs):
    q_refs = refs[: n_req - 1]
    acc_ref, log_ref, limit_ref, pages_ref = refs[n_req - 1 : n_req + 3]
    out_refs = refs[n_req + 3 : n_req + 3 + n_tp]
    results, logs = refs[n_req + 3 + n_tp :]
    kv_heads, width = pages_ref.shape[1], pages_ref.shape[3]
    head_dim = width // 2
    chunk = 64 // n_tp
    my_tp = lax.axis_index("tp")
    me = lax.axis_index("req")
    scale = 1.0 / math.sqrt(head_dim)
    others = n_req - 1
    pairs = round_up(others, 2) // 2

    def keep(d, result, log_row):
        n = me ^ d
        results[pl.ds(pl.multiple_of(n * 64, 64), 64)] = result
        logs[pl.ds(n, 1)] = log_row

    logs[...] = jnp.zeros_like(logs)
    scores, members = [], []
    for p in range(pairs):
        a, b = 2 * p, min(2 * p + 1, others - 1)
        members.append((a, b))
        tiles = query_tiles(jnp.concatenate([q_refs[a][...], q_refs[b][...]], axis=0), kv_heads)
        scores.append(pair_scores(pages_ref.at[a], pages_ref.at[b], tiles, head_dim) * scale)
    sums, inverse, log_rows = [], [], []
    for p in range(pairs):
        a, b = members[p]
        top, total, weights = pair_softmax(scores[p], limit_ref[p : p + 1])
        sums.append(pair_values(weights, pages_ref.at[a], pages_ref.at[b], head_dim))
        total = jnp.where(total > 0.0, total, 1.0)
        inverse.append(1.0 / total)
        log_rows.append(top + jnp.log(total))
    columns = to_columns(inverse)
    keep(0, acc_ref[...], log_ref[0:1])
    for p in range(pairs):
        result = sums[p] * columns[:, p : p + 1]
        keep(2 * p + 1, result[:64], log_rows[p])
        if 2 * p + 1 < others:
            keep(2 * p + 2, result[64:], halves(log_rows[p]))

    value = logs[...]
    lane = lax.broadcasted_iota(jnp.int32, value.shape, 1)
    high = value.astype(jnp.bfloat16).astype(jnp.float32)
    rest = value - high
    middle = rest.astype(jnp.bfloat16).astype(jnp.float32)
    low = rest - middle
    for d in range(n_tp):
        first = (my_tp ^ d) * chunk
        for h in range(chunk):
            rows = results[pl.ds(first + h, n_req, stride=64)]
            out_refs[d][:, h * head_dim : (h + 1) * head_dim] = rows.astype(jnp.bfloat16)
        shift = 128 - first
        stats = jnp.where(lane < chunk, pltpu.roll(high, shift % 128, 1), 0.0)
        stats = jnp.where((lane >= chunk) & (lane < 2 * chunk), pltpu.roll(middle, (shift + chunk) % 128, 1), stats)
        stats = jnp.where((lane >= 2 * chunk) & (lane < 3 * chunk), pltpu.roll(low, (shift + 2 * chunk) % 128, 1), stats)
        out_refs[d][:, chunk * head_dim :] = stats[:n_req].astype(jnp.bfloat16)


def other_attention(q_list, own, n_req, n_tp):
    heads, head_dim = own[0].shape
    chunk = heads // n_tp
    vmem = pl.BlockSpec(memory_space=pltpu.VMEM)
    return pl.pallas_call(
        functools.partial(other_kernel, n_req, n_tp),
        out_shape=[jax.ShapeDtypeStruct((n_req, chunk * head_dim + 128), jnp.bfloat16)] * n_tp,
        in_specs=[vmem] * (n_req + 3),
        out_specs=[vmem] * n_tp,
        scratch_shapes=[
            pltpu.VMEM((n_req * heads, head_dim), jnp.float32),
            pltpu.VMEM((round_up(n_req, 8), 128), jnp.float32),
        ],
        compiler_params=pltpu.CompilerParams(vmem_limit_bytes=16 * MIB),
        cost_estimate=pl.CostEstimate(flops=2 * own[3].size * 16, bytes_accessed=own[3].size * 2, transcendentals=0),
        name="other_attention",
    )(*q_list, *own)


def row_copies(source, first, target, sems):
    parts = sems.shape[0]
    step = target.shape[0] // parts
    return [
        pltpu.make_async_copy(
            source.at[pl.ds(first + i * step, step)], target.at[pl.ds(i * step, step)], sems.at[i]
        )
        for i in range(parts)
    ]


def load_kernel(first, piece_ref, weight_hbm, out_ref, same_ref, sems):
    copies = row_copies(weight_hbm, first, out_ref, sems)
    for copy in copies:
        copy.start()
    same_ref[...] = piece_ref[...]
    for copy in copies:
        copy.wait()


def load_weight(piece, out_weight, first, rows):
    columns = out_weight.shape[1]
    vmem = pl.BlockSpec(memory_space=pltpu.VMEM)
    return pl.pallas_call(
        functools.partial(load_kernel, first),
        out_shape=[
            jax.ShapeDtypeStruct((rows, columns), out_weight.dtype),
            jax.ShapeDtypeStruct(piece.shape, piece.dtype),
        ],
        in_specs=[vmem, pl.BlockSpec(memory_space=pltpu.HBM)],
        out_specs=[vmem] * 2,
        scratch_shapes=[pltpu.SemaphoreType.DMA((4,))],
        compiler_params=pltpu.CompilerParams(vmem_limit_bytes=20 * MIB),
        cost_estimate=pl.CostEstimate(flops=0, bytes_accessed=rows * columns * 4, transcendentals=0),
        name="load_weight",
    )(piece, in_hbm(out_weight))


def project_kernel(n_req, n_tp, *refs):
    part_refs = refs[:n_req]
    weight_refs = refs[n_req : n_req + 2]
    out_refs = refs[n_req + 2 : n_req + 2 + n_tp]
    attention = refs[n_req + 2 + n_tp]
    split, columns = weight_refs[0].shape
    depth = attention.shape[1]
    chunk = depth // 128
    values = []
    for part in part_refs:
        stats = part[:, depth:].astype(jnp.float32)
        values.append(stats + pltpu.roll(stats, 128 - chunk, 1) + pltpu.roll(stats, 128 - 2 * chunk, 1))
    top = functools.reduce(jnp.maximum, values)
    factors = [jnp.exp(v - top) for v in values]
    total = functools.reduce(jnp.add, factors)
    factors = [f / total for f in factors]
    for h in range(chunk):
        at = slice(h * 128, (h + 1) * 128)
        terms = [part[:, at].astype(jnp.float32) * f[:, h : h + 1] for part, f in zip(part_refs, factors)]
        attention[:, at] = functools.reduce(jnp.add, terms).astype(jnp.bfloat16)
    tile = min(columns, 1024)

    @pl.loop(0, columns // tile)
    def _(t):
        at = pl.ds(pl.multiple_of(t * tile, tile), tile)
        product = jnp.dot(attention[:, :split], weight_refs[0][:, at], preferred_element_type=jnp.float32)
        product += jnp.dot(attention[:, split:], weight_refs[1][:, at], preferred_element_type=jnp.float32)
        for d in range(n_tp):
            out_refs[d][:, at] = product[d * n_req : (d + 1) * n_req].astype(out_refs[d].dtype)


def project(parts, weights, n_req, n_tp):
    depth = sum(w.shape[0] for w in weights)
    columns = weights[0].shape[1]
    vmem = pl.BlockSpec(memory_space=pltpu.VMEM)
    own = jax.ShapeDtypeStruct((n_req, columns), jnp.float32)
    sent = jax.ShapeDtypeStruct((n_req, columns), jnp.bfloat16)
    rows = n_tp * n_req
    return pl.pallas_call(
        functools.partial(project_kernel, n_req, n_tp),
        out_shape=[own] + [sent] * (n_tp - 1),
        in_specs=[vmem] * (n_req + 2),
        out_specs=[vmem] * n_tp,
        scratch_shapes=[pltpu.VMEM((rows, depth), jnp.bfloat16)],
        compiler_params=pltpu.CompilerParams(vmem_limit_bytes=16 * MIB),
        cost_estimate=pl.CostEstimate(
            flops=2 * rows * depth * columns, bytes_accessed=depth * columns * 2, transcendentals=0
        ),
        name="project",
    )(*parts, *weights)


def on_device(queries, new_kv, cache_pool, page_slot, page_owner, context_len, out_weight):
    n_req = lax.axis_size("req")
    n_tp = lax.axis_size("tp")
    pool = cache_pool[0, 0]
    head_dim = pool.shape[3] // 2
    q = queries.reshape(-1, head_dim)
    q_list = [swap(q, "req", d) for d in range(1, n_req)]
    own = own_attention(q, new_kv, page_slot, page_owner, context_len, pool, n_req)
    pieces = other_attention(q_list, own, n_req, n_tp)
    depth = out_weight.shape[0]
    early = depth * 5 // 16
    swapped = [swap(pieces[d], "tp", d) for d in range(1, n_tp)]
    first, mine = load_weight(pieces[0], out_weight, 0, early)
    arrived = jnp.concatenate([mine] + swapped, axis=0)
    parts = [swap(arrived, "req", d) for d in range(1, n_req)]
    second, mine = load_weight(arrived, out_weight, early, depth - early)
    sums = project([mine] + parts, (first, second), n_req, n_tp)
    total = sums[0]
    for d in range(1, n_tp):
        total = total + swap(sums[d], "tp", d).astype(jnp.float32)
    return total.astype(jnp.bfloat16)


def solution(mesh):
    placed = (
        P(("groups", "tp", "req"), None),
        P(("groups", "tp", "req"), None),
        P(("groups", "tp"), "req", None, None, None, None),
        P(("groups", "tp"), None, None),
        P(("groups", "tp"), None, None),
        P(("groups", "tp"), None),
        P("tp", "req"),
    )
    return jax.shard_map(
        on_device, mesh=mesh, in_specs=placed, out_specs=P(("groups", "tp"), "req"), check_vma=False
    )
```

```python
import functools
import math

import jax
import jax.numpy as jnp
from jax import lax
from jax.experimental import pallas as pl
from jax.experimental.pallas import tpu as pltpu
from jax.sharding import PartitionSpec as P

very_negative = -1e30
MIB = 1 << 20


def swap(x, axis, offset):
    count = lax.axis_size(axis)
    return lax.ppermute(x, axis, [(i, i ^ offset) for i in range(count)])


def near_last(count):
    return list(range(2, count)) + [1]


def in_hbm(x):
    return pltpu.with_memory_space_constraint(x, pltpu.HBM)


def round_up(value, step):
    return -(-value // step) * step


def halves(x):
    return pltpu.roll(x, 64, 1)


def query_tiles(stacked, kv_heads):
    turned = stacked.astype(jnp.float32).T
    lane = lax.broadcasted_iota(jnp.int32, turned.shape, 1)
    group = 64 // kv_heads
    return [
        [
            jnp.where((lane >= a * 64 + h * group) & (lane < a * 64 + (h + 1) * group), turned, 0.0).astype(jnp.bfloat16)
            for a in range(2)
        ]
        for h in range(kv_heads)
    ]


def pair_scores(page_a, page_b, tiles, head_dim):
    total = None
    for h in range(len(tiles)):
        for a, page in enumerate((page_a, page_b)):
            part = jnp.dot(page[h, :, :head_dim], tiles[h][a], preferred_element_type=jnp.float32)
            total = part if total is None else total + part
    return total


def pair_softmax(scores, limit):
    token = lax.broadcasted_iota(jnp.int32, scores.shape, 0)
    mask = token < limit
    masked = jnp.where(mask, scores, very_negative)
    top = jnp.max(masked, axis=0, keepdims=True)
    weights = jnp.where(mask, jnp.exp(masked - top), 0.0)
    return top, jnp.sum(weights, axis=0, keepdims=True), weights


def pair_values(weights, page_a, page_b, head_dim):
    turned = weights.T.astype(jnp.bfloat16)
    kv_heads = page_a.shape[0]
    group = 64 // kv_heads
    blocks = []
    for a, page in enumerate((page_a, page_b)):
        for h in range(kv_heads):
            at = a * 64 + h * group
            blocks.append(
                jnp.dot(turned[at : at + group], page[h, :, head_dim:], preferred_element_type=jnp.float32)
            )
    return jnp.concatenate(blocks, axis=0)


def to_columns(rows):
    stacked = jnp.concatenate(rows + [jnp.zeros((128 - len(rows), 128), jnp.float32)], axis=0)
    return stacked.T


def own_kernel(n_req, own_pages, *refs):
    q_ref, kv_hbm, slot_hbm, owner_hbm, len_hbm, pool_hbm = refs[:6]
    acc_ref, log_ref, limit_ref, pages_ref = refs[6:10]
    kv, slots, owners, lens, pool, small_sem, pool_sem, page_sem = refs[10:]
    slot_count, kv_heads, page_len, width = pool_hbm.shape
    head_dim = width // 2
    entries = slot_hbm.shape[2]
    me = lax.axis_index("req")
    scale = 1.0 / math.sqrt(head_dim)
    small = [
        pltpu.make_async_copy(src, dst, small_sem.at[i])
        for i, (src, dst) in enumerate(
            ((slot_hbm, slots), (owner_hbm, owners), (len_hbm, lens), (kv_hbm, kv))
        )
    ]
    for copy in small:
        copy.start()
    whole = pltpu.make_async_copy(pool_hbm, pool, pool_sem)
    whole.start()
    tiles = query_tiles(jnp.concatenate([q_ref[...], q_ref[...]], axis=0), kv_heads)
    for copy in small:
        copy.wait()

    fetched = []
    lane = lax.broadcasted_iota(jnp.int32, (1, 128), 1)
    limits = []
    for d in range(1, n_req):
        n = me ^ d
        length = lens[0, n]
        slot = jnp.int32(0)
        limit = jnp.int32(0)
        for j in range(entries):
            held = (owners[0, n, j] == me) & (j * page_len < length)
            slot = jnp.where(held, slots[0, n, j], slot)
            limit = jnp.where(held, length - j * page_len, limit)
        copy = pltpu.make_async_copy(pool_hbm.at[slot], pages_ref.at[d - 1], page_sem.at[d - 1])
        copy.start()
        fetched.append(copy)
        limits.append(limit)
    if len(limits) % 2:
        limits.append(jnp.int32(0))
    for p in range(len(limits) // 2):
        limit_ref[p : p + 1] = jnp.where(lane < 64, limits[2 * p], limits[2 * p + 1])

    my_length = lens[0, me]
    pages, valid = [], []
    for i in range(own_pages):
        held = (owners[0, me, i] == me) & (i * page_len < my_length)
        pages.append(pool.at[jnp.where(held, slots[0, me, i], 0)])
        valid.append(jnp.where(held, my_length - i * page_len, 0))
    if own_pages % 2:
        pages.append(pages[0])
        valid.append(jnp.int32(0))
    pairs = len(pages) // 2

    base = kv_heads * head_dim
    new_k = [kv[0:1, h * head_dim : (h + 1) * head_dim] for h in range(kv_heads)]
    self_score = None
    for h in range(kv_heads):
        both = tiles[h][0] + tiles[h][1]
        part = jnp.dot(jnp.broadcast_to(new_k[h], (16, head_dim)), both, preferred_element_type=jnp.float32)
        self_score = part if self_score is None else self_score + part
    self_score = self_score[0:1] * scale

    whole.wait()
    scores = [pair_scores(pages[2 * p], pages[2 * p + 1], tiles, head_dim) * scale for p in range(pairs)]
    tops, totals, sums = [], [], []
    for p in range(pairs):
        limit = jnp.where(lane < 64, valid[2 * p], valid[2 * p + 1])
        top, total, weights = pair_softmax(scores[p], limit)
        tops.append(top)
        totals.append(total)
        sums.append(pair_values(weights, pages[2 * p], pages[2 * p + 1], head_dim))
    top = functools.reduce(jnp.maximum, tops)
    top = jnp.maximum(jnp.maximum(top, halves(top)), self_score)
    factors = [jnp.exp(t - top) for t in tops]
    own_factor = jnp.exp(self_score - top)
    total = functools.reduce(jnp.add, [f * t for f, t in zip(factors, totals)])
    total = total + halves(total) + own_factor
    columns = to_columns([f / total for f in factors] + [own_factor / total])
    result = None
    for p in range(pairs):
        term = sums[p] * columns[:, p : p + 1]
        result = term if result is None else result + term
    group = 64 // kv_heads
    new_v = jnp.concatenate(
        [
            jnp.broadcast_to(kv[0:1, base + h * head_dim : base + (h + 1) * head_dim].astype(jnp.float32), (group, head_dim))
            for h in range(kv_heads)
        ],
        axis=0,
    )
    acc_ref[...] = result[:64] + result[64:] + columns[:64, pairs : pairs + 1] * new_v
    log_ref[...] = jnp.broadcast_to(top + jnp.log(total), log_ref.shape)
    for copy in fetched:
        copy.wait()


def own_attention(q, new_kv, page_slot, page_owner, context_len, pool, n_req):
    slots, kv_heads, page_len, width = pool.shape
    head_dim = width // 2
    heads = q.shape[0]
    own_pages = min(slots, page_slot.shape[2])
    hbm = pl.BlockSpec(memory_space=pltpu.HBM)
    vmem = pl.BlockSpec(memory_space=pltpu.VMEM)
    pair_count = round_up(n_req - 1, 2) // 2
    page_bytes = pool.size * 2 // slots
    return pl.pallas_call(
        functools.partial(own_kernel, n_req, own_pages),
        out_shape=[
            jax.ShapeDtypeStruct((heads, head_dim), jnp.float32),
            jax.ShapeDtypeStruct((8, 128), jnp.float32),
            jax.ShapeDtypeStruct((round_up(pair_count, 8), 128), jnp.int32),
            jax.ShapeDtypeStruct((n_req - 1, kv_heads, page_len, width), pool.dtype),
        ],
        in_specs=[vmem] + [hbm] * 5,
        out_specs=[vmem] * 4,
        scratch_shapes=[
            pltpu.VMEM(new_kv.shape, new_kv.dtype),
            pltpu.SMEM(page_slot.shape, jnp.int32),
            pltpu.SMEM(page_owner.shape, jnp.int32),
            pltpu.SMEM(context_len.shape, jnp.int32),
            pltpu.VMEM(pool.shape, pool.dtype),
            pltpu.SemaphoreType.DMA((4,)),
            pltpu.SemaphoreType.DMA,
            pltpu.SemaphoreType.DMA((n_req - 1,)),
        ],
        compiler_params=pltpu.CompilerParams(vmem_limit_bytes=16 * MIB),
        cost_estimate=pl.CostEstimate(
            flops=4 * own_pages * page_len * heads * head_dim,
            bytes_accessed=page_bytes * (slots + n_req - 1) * 2,
            transcendentals=0,
        ),
        name="own_attention",
    )(q, *(in_hbm(x) for x in (new_kv, page_slot, page_owner, context_len, pool)))


def other_kernel(n_req, n_tp, *refs):
    q_of = dict(zip(reversed(near_last(n_req)), refs[: n_req - 1]))
    q_refs = [q_of[d] for d in range(1, n_req)]
    acc_ref, log_ref, limit_ref, pages_ref = refs[n_req - 1 : n_req + 3]
    out_refs = refs[n_req + 3 : n_req + 3 + n_tp]
    results, logs = refs[n_req + 3 + n_tp :]
    kv_heads, width = pages_ref.shape[1], pages_ref.shape[3]
    head_dim = width // 2
    chunk = 64 // n_tp
    my_tp = lax.axis_index("tp")
    me = lax.axis_index("req")
    scale = 1.0 / math.sqrt(head_dim)
    others = n_req - 1
    pairs = round_up(others, 2) // 2

    def keep(d, result, log_row):
        n = me ^ d
        results[pl.ds(pl.multiple_of(n * 64, 64), 64)] = result
        logs[pl.ds(n, 1)] = log_row

    logs[...] = jnp.zeros_like(logs)
    scores, members = [], []
    for p in range(pairs):
        a, b = 2 * p, min(2 * p + 1, others - 1)
        members.append((a, b))
        tiles = query_tiles(jnp.concatenate([q_refs[a][...], q_refs[b][...]], axis=0), kv_heads)
        scores.append(pair_scores(pages_ref.at[a], pages_ref.at[b], tiles, head_dim) * scale)
    sums, inverse, log_rows = [], [], []
    for p in range(pairs):
        a, b = members[p]
        top, total, weights = pair_softmax(scores[p], limit_ref[p : p + 1])
        sums.append(pair_values(weights, pages_ref.at[a], pages_ref.at[b], head_dim))
        total = jnp.where(total > 0.0, total, 1.0)
        inverse.append(1.0 / total)
        log_rows.append(top + jnp.log(total))
    columns = to_columns(inverse)
    keep(0, acc_ref[...], log_ref[0:1])
    for p in range(pairs):
        result = sums[p] * columns[:, p : p + 1]
        keep(2 * p + 1, result[:64], log_rows[p])
        if 2 * p + 1 < others:
            keep(2 * p + 2, result[64:], halves(log_rows[p]))

    value = logs[...]
    lane = lax.broadcasted_iota(jnp.int32, value.shape, 1)
    high = value.astype(jnp.bfloat16).astype(jnp.float32)
    rest = value - high
    middle = rest.astype(jnp.bfloat16).astype(jnp.float32)
    low = rest - middle
    for d in range(n_tp):
        first = (my_tp ^ d) * chunk
        for h in range(chunk):
            rows = results[pl.ds(first + h, n_req, stride=64)]
            out_refs[d][:, h * head_dim : (h + 1) * head_dim] = rows.astype(jnp.bfloat16)
        shift = 128 - first
        stats = jnp.where(lane < chunk, pltpu.roll(high, shift % 128, 1), 0.0)
        stats = jnp.where((lane >= chunk) & (lane < 2 * chunk), pltpu.roll(middle, (shift + chunk) % 128, 1), stats)
        stats = jnp.where((lane >= 2 * chunk) & (lane < 3 * chunk), pltpu.roll(low, (shift + 2 * chunk) % 128, 1), stats)
        out_refs[d][:, chunk * head_dim :] = stats[:n_req].astype(jnp.bfloat16)


def other_attention(q_list, own, n_req, n_tp):
    heads, head_dim = own[0].shape
    chunk = heads // n_tp
    vmem = pl.BlockSpec(memory_space=pltpu.VMEM)
    return pl.pallas_call(
        functools.partial(other_kernel, n_req, n_tp),
        out_shape=[jax.ShapeDtypeStruct((n_req, chunk * head_dim + 128), jnp.bfloat16)] * n_tp,
        in_specs=[vmem] * (n_req + 3),
        out_specs=[vmem] * n_tp,
        scratch_shapes=[
            pltpu.VMEM((n_req * heads, head_dim), jnp.float32),
            pltpu.VMEM((round_up(n_req, 8), 128), jnp.float32),
        ],
        compiler_params=pltpu.CompilerParams(vmem_limit_bytes=16 * MIB),
        cost_estimate=pl.CostEstimate(flops=2 * own[3].size * 16, bytes_accessed=own[3].size * 2, transcendentals=0),
        name="other_attention",
    )(*q_list, *own)


def row_copies(source, first, target, sems):
    parts = sems.shape[0]
    step = target.shape[0] // parts
    return [
        pltpu.make_async_copy(
            source.at[pl.ds(first + i * step, step)], target.at[pl.ds(i * step, step)], sems.at[i]
        )
        for i in range(parts)
    ]


def load_kernel(first, piece_ref, weight_hbm, out_ref, same_ref, sems):
    copies = row_copies(weight_hbm, first, out_ref, sems)
    for copy in copies:
        copy.start()
    same_ref[...] = piece_ref[...]
    for copy in copies:
        copy.wait()


def load_weight(piece, out_weight, first, rows):
    columns = out_weight.shape[1]
    vmem = pl.BlockSpec(memory_space=pltpu.VMEM)
    return pl.pallas_call(
        functools.partial(load_kernel, first),
        out_shape=[
            jax.ShapeDtypeStruct((rows, columns), out_weight.dtype),
            jax.ShapeDtypeStruct(piece.shape, piece.dtype),
        ],
        in_specs=[vmem, pl.BlockSpec(memory_space=pltpu.HBM)],
        out_specs=[vmem] * 2,
        scratch_shapes=[pltpu.SemaphoreType.DMA((4,))],
        compiler_params=pltpu.CompilerParams(vmem_limit_bytes=20 * MIB),
        cost_estimate=pl.CostEstimate(flops=0, bytes_accessed=rows * columns * 4, transcendentals=0),
        name="load_weight",
    )(piece, in_hbm(out_weight))


def project_kernel(n_req, n_tp, *refs):
    part_refs = refs[:n_req]
    weight_refs = refs[n_req : n_req + 2]
    out_refs = refs[n_req + 2 : n_req + 2 + n_tp]
    attention = refs[n_req + 2 + n_tp]
    split, columns = weight_refs[0].shape
    depth = attention.shape[1]
    chunk = depth // 128
    values = []
    for part in part_refs:
        stats = part[:, depth:].astype(jnp.float32)
        values.append(stats + pltpu.roll(stats, 128 - chunk, 1) + pltpu.roll(stats, 128 - 2 * chunk, 1))
    top = functools.reduce(jnp.maximum, values)
    factors = [jnp.exp(v - top) for v in values]
    total = functools.reduce(jnp.add, factors)
    factors = [f / total for f in factors]
    for h in range(chunk):
        at = slice(h * 128, (h + 1) * 128)
        terms = [part[:, at].astype(jnp.float32) * f[:, h : h + 1] for part, f in zip(part_refs, factors)]
        attention[:, at] = functools.reduce(jnp.add, terms).astype(jnp.bfloat16)
    tile = min(columns, 2048)

    @pl.loop(0, columns // tile)
    def _(t):
        at = pl.ds(pl.multiple_of(t * tile, tile), tile)
        product = jnp.dot(attention[:, :split], weight_refs[0][:, at], preferred_element_type=jnp.float32)
        product += jnp.dot(attention[:, split:], weight_refs[1][:, at], preferred_element_type=jnp.float32)
        for i, d in enumerate([0] + near_last(n_tp)):
            out_refs[d][:, at] = product[i * n_req : (i + 1) * n_req].astype(out_refs[d].dtype)


def project(parts, weights, n_req, n_tp):
    depth = sum(w.shape[0] for w in weights)
    columns = weights[0].shape[1]
    vmem = pl.BlockSpec(memory_space=pltpu.VMEM)
    own = jax.ShapeDtypeStruct((n_req, columns), jnp.float32)
    sent = jax.ShapeDtypeStruct((n_req, columns), jnp.bfloat16)
    rows = n_tp * n_req
    return pl.pallas_call(
        functools.partial(project_kernel, n_req, n_tp),
        out_shape=[own] + [sent] * (n_tp - 1),
        in_specs=[vmem] * (n_req + 2),
        out_specs=[vmem] * n_tp,
        scratch_shapes=[pltpu.VMEM((rows, depth), jnp.bfloat16)],
        compiler_params=pltpu.CompilerParams(vmem_limit_bytes=16 * MIB),
        cost_estimate=pl.CostEstimate(
            flops=2 * rows * depth * columns, bytes_accessed=depth * columns * 2, transcendentals=0
        ),
        name="project",
    )(*parts, *weights)


def on_device(queries, new_kv, cache_pool, page_slot, page_owner, context_len, out_weight):
    n_req = lax.axis_size("req")
    n_tp = lax.axis_size("tp")
    pool = cache_pool[0, 0]
    head_dim = pool.shape[3] // 2
    q = queries.reshape(-1, head_dim)
    q_list = [swap(q, "req", d) for d in reversed(near_last(n_req))]
    own = own_attention(q, new_kv, page_slot, page_owner, context_len, pool, n_req)
    pieces = other_attention(q_list, own, n_req, n_tp)
    depth = out_weight.shape[0]
    early = depth * 5 // 16
    swapped = [swap(pieces[d], "tp", d) for d in near_last(n_tp)]
    first, mine = load_weight(pieces[0], out_weight, 0, early)
    arrived = jnp.concatenate([mine] + swapped, axis=0)
    parts = [swap(arrived, "req", d) for d in reversed(near_last(n_req))]
    second, mine = load_weight(arrived, out_weight, early, depth - early)
    sums = project([mine] + parts, (first, second), n_req, n_tp)
    total = sums[0]
    for d in near_last(n_tp):
        total = total + swap(sums[d], "tp", d).astype(jnp.float32)
    return total.astype(jnp.bfloat16)


def solution(mesh):
    placed = (
        P(("groups", "tp", "req"), None),
        P(("groups", "tp", "req"), None),
        P(("groups", "tp"), "req", None, None, None, None),
        P(("groups", "tp"), None, None),
        P(("groups", "tp"), None, None),
        P(("groups", "tp"), None),
        P("tp", "req"),
    )
    return jax.shard_map(
        on_device, mesh=mesh, in_specs=placed, out_specs=P(("groups", "tp"), "req"), check_vma=False
    )
```

```python
import functools
import math

import jax
import jax.numpy as jnp
from jax import lax
from jax.experimental import pallas as pl
from jax.experimental.pallas import tpu as pltpu
from jax.sharding import PartitionSpec as P

very_negative = -1e30
MIB = 1 << 20


def swap(x, axis, offset):
    count = lax.axis_size(axis)
    return lax.ppermute(x, axis, [(i, i ^ offset) for i in range(count)])


def near_last(count):
    return list(range(2, count)) + [1]


def in_hbm(x):
    return pltpu.with_memory_space_constraint(x, pltpu.HBM)


def round_up(value, step):
    return -(-value // step) * step


def halves(x):
    return pltpu.roll(x, 64, 1)


def lay_rows(target, start, q_ref):
    head_dim = target.shape[1]
    for h in range(64):
        target[start + h : start + h + 1] = q_ref[0:1, h * head_dim : (h + 1) * head_dim].astype(jnp.float32)


def query_tiles(stacked, kv_heads):
    turned = stacked.T
    lane = lax.broadcasted_iota(jnp.int32, turned.shape, 1)
    group = 64 // kv_heads
    return [
        [
            jnp.where((lane >= a * 64 + h * group) & (lane < a * 64 + (h + 1) * group), turned, 0.0).astype(jnp.bfloat16)
            for a in range(2)
        ]
        for h in range(kv_heads)
    ]


def pair_scores(page_a, page_b, tiles, head_dim):
    total = None
    for h in range(len(tiles)):
        for a, page in enumerate((page_a, page_b)):
            part = jnp.dot(page[h, :, :head_dim], tiles[h][a], preferred_element_type=jnp.float32)
            total = part if total is None else total + part
    return total


def pair_softmax(scores, limit):
    token = lax.broadcasted_iota(jnp.int32, scores.shape, 0)
    mask = token < limit
    masked = jnp.where(mask, scores, very_negative)
    top = jnp.max(masked, axis=0, keepdims=True)
    weights = jnp.where(mask, jnp.exp(masked - top), 0.0)
    return top, jnp.sum(weights, axis=0, keepdims=True), weights


def pair_values(weights, page_a, page_b, head_dim):
    turned = weights.T.astype(jnp.bfloat16)
    kv_heads = page_a.shape[0]
    group = 64 // kv_heads
    blocks = []
    for a, page in enumerate((page_a, page_b)):
        for h in range(kv_heads):
            at = a * 64 + h * group
            blocks.append(
                jnp.dot(turned[at : at + group], page[h, :, head_dim:], preferred_element_type=jnp.float32)
            )
    return jnp.concatenate(blocks, axis=0)


def to_columns(rows):
    stacked = jnp.concatenate(rows + [jnp.zeros((128 - len(rows), 128), jnp.float32)], axis=0)
    return stacked.T


def own_kernel(n_req, own_pages, *refs):
    q_hbm, kv_hbm, slot_hbm, owner_hbm, len_hbm, pool_hbm = refs[:6]
    acc_ref, log_ref, limit_ref, pages_ref = refs[6:10]
    q_row, q_heads, kv, slots, owners, lens, pool, small_sem, pool_sem, page_sem = refs[10:]
    slot_count, kv_heads, page_len, width = pool_hbm.shape
    head_dim = width // 2
    entries = slot_hbm.shape[2]
    me = lax.axis_index("req")
    scale = 1.0 / math.sqrt(head_dim)
    small = [
        pltpu.make_async_copy(src, dst, small_sem.at[i])
        for i, (src, dst) in enumerate(
            ((slot_hbm, slots), (owner_hbm, owners), (len_hbm, lens), (kv_hbm, kv), (q_hbm, q_row))
        )
    ]
    for copy in small:
        copy.start()
    whole = pltpu.make_async_copy(pool_hbm, pool, pool_sem)
    whole.start()
    for copy in small:
        copy.wait()

    fetched = []
    lane = lax.broadcasted_iota(jnp.int32, (1, 128), 1)
    limits = []
    for d in range(1, n_req):
        n = me ^ d
        length = lens[0, n]
        slot = jnp.int32(0)
        limit = jnp.int32(0)
        for j in range(entries):
            held = (owners[0, n, j] == me) & (j * page_len < length)
            slot = jnp.where(held, slots[0, n, j], slot)
            limit = jnp.where(held, length - j * page_len, limit)
        copy = pltpu.make_async_copy(pool_hbm.at[slot], pages_ref.at[d - 1], page_sem.at[d - 1])
        copy.start()
        fetched.append(copy)
        limits.append(limit)
    if len(limits) % 2:
        limits.append(jnp.int32(0))
    for p in range(len(limits) // 2):
        limit_ref[p : p + 1] = jnp.where(lane < 64, limits[2 * p], limits[2 * p + 1])

    lay_rows(q_heads, 0, q_row)
    q_heads[64:] = q_heads[:64]
    tiles = query_tiles(q_heads[...], kv_heads)
    my_length = lens[0, me]
    pages, valid = [], []
    for i in range(own_pages):
        held = (owners[0, me, i] == me) & (i * page_len < my_length)
        pages.append(pool.at[jnp.where(held, slots[0, me, i], 0)])
        valid.append(jnp.where(held, my_length - i * page_len, 0))
    if own_pages % 2:
        pages.append(pages[0])
        valid.append(jnp.int32(0))
    pairs = len(pages) // 2

    base = kv_heads * head_dim
    new_k = [kv[0:1, h * head_dim : (h + 1) * head_dim] for h in range(kv_heads)]
    self_score = None
    for h in range(kv_heads):
        both = tiles[h][0] + tiles[h][1]
        part = jnp.dot(jnp.broadcast_to(new_k[h], (16, head_dim)), both, preferred_element_type=jnp.float32)
        self_score = part if self_score is None else self_score + part
    self_score = self_score[0:1] * scale

    whole.wait()
    scores = [pair_scores(pages[2 * p], pages[2 * p + 1], tiles, head_dim) * scale for p in range(pairs)]
    tops, totals, sums = [], [], []
    for p in range(pairs):
        limit = jnp.where(lane < 64, valid[2 * p], valid[2 * p + 1])
        top, total, weights = pair_softmax(scores[p], limit)
        tops.append(top)
        totals.append(total)
        sums.append(pair_values(weights, pages[2 * p], pages[2 * p + 1], head_dim))
    top = functools.reduce(jnp.maximum, tops)
    top = jnp.maximum(jnp.maximum(top, halves(top)), self_score)
    factors = [jnp.exp(t - top) for t in tops]
    own_factor = jnp.exp(self_score - top)
    total = functools.reduce(jnp.add, [f * t for f, t in zip(factors, totals)])
    total = total + halves(total) + own_factor
    columns = to_columns([f / total for f in factors] + [own_factor / total])
    result = None
    for p in range(pairs):
        term = sums[p] * columns[:, p : p + 1]
        result = term if result is None else result + term
    group = 64 // kv_heads
    new_v = jnp.concatenate(
        [
            jnp.broadcast_to(kv[0:1, base + h * head_dim : base + (h + 1) * head_dim].astype(jnp.float32), (group, head_dim))
            for h in range(kv_heads)
        ],
        axis=0,
    )
    acc_ref[...] = result[:64] + result[64:] + columns[:64, pairs : pairs + 1] * new_v
    log_ref[...] = jnp.broadcast_to(top + jnp.log(total), log_ref.shape)
    for copy in fetched:
        copy.wait()


def own_attention(q, new_kv, page_slot, page_owner, context_len, pool, n_req):
    slots, kv_heads, page_len, width = pool.shape
    head_dim = width // 2
    heads = q.shape[1] // head_dim
    own_pages = min(slots, page_slot.shape[2])
    hbm = pl.BlockSpec(memory_space=pltpu.HBM)
    vmem = pl.BlockSpec(memory_space=pltpu.VMEM)
    pair_count = round_up(n_req - 1, 2) // 2
    page_bytes = pool.size * 2 // slots
    return pl.pallas_call(
        functools.partial(own_kernel, n_req, own_pages),
        out_shape=[
            jax.ShapeDtypeStruct((heads, head_dim), jnp.float32),
            jax.ShapeDtypeStruct((8, 128), jnp.float32),
            jax.ShapeDtypeStruct((round_up(pair_count, 8), 128), jnp.int32),
            jax.ShapeDtypeStruct((n_req - 1, kv_heads, page_len, width), pool.dtype),
        ],
        in_specs=[hbm] * 6,
        out_specs=[vmem] * 4,
        scratch_shapes=[
            pltpu.VMEM(q.shape, q.dtype),
            pltpu.VMEM((128, head_dim), jnp.float32),
            pltpu.VMEM(new_kv.shape, new_kv.dtype),
            pltpu.SMEM(page_slot.shape, jnp.int32),
            pltpu.SMEM(page_owner.shape, jnp.int32),
            pltpu.SMEM(context_len.shape, jnp.int32),
            pltpu.VMEM(pool.shape, pool.dtype),
            pltpu.SemaphoreType.DMA((5,)),
            pltpu.SemaphoreType.DMA,
            pltpu.SemaphoreType.DMA((n_req - 1,)),
        ],
        compiler_params=pltpu.CompilerParams(vmem_limit_bytes=16 * MIB),
        cost_estimate=pl.CostEstimate(
            flops=4 * own_pages * page_len * heads * head_dim,
            bytes_accessed=page_bytes * (slots + n_req - 1) * 2,
            transcendentals=0,
        ),
        name="own_attention",
    )(*(in_hbm(x) for x in (q, new_kv, page_slot, page_owner, context_len, pool)))


def other_kernel(n_req, n_tp, *refs):
    q_refs = refs[: n_req - 1][::-1]
    acc_ref, log_ref, limit_ref, pages_ref = refs[n_req - 1 : n_req + 3]
    out_refs = refs[n_req + 3 : n_req + 3 + n_tp]
    results, logs, q_heads = refs[n_req + 3 + n_tp :]
    kv_heads, width = pages_ref.shape[1], pages_ref.shape[3]
    head_dim = width // 2
    chunk = 64 // n_tp
    my_tp = lax.axis_index("tp")
    me = lax.axis_index("req")
    scale = 1.0 / math.sqrt(head_dim)
    others = n_req - 1
    pairs = round_up(others, 2) // 2

    def keep(d, result, log_row):
        n = me ^ d
        results[pl.ds(pl.multiple_of(n * 64, 64), 64)] = result
        logs[pl.ds(n, 1)] = log_row

    logs[...] = jnp.zeros_like(logs)
    scores, members = [], []
    for p in range(pairs):
        a, b = 2 * p, min(2 * p + 1, others - 1)
        members.append((a, b))
        lay_rows(q_heads.at[p], 0, q_refs[a])
        lay_rows(q_heads.at[p], 64, q_refs[b])
        tiles = query_tiles(q_heads[p], kv_heads)
        scores.append(pair_scores(pages_ref.at[a], pages_ref.at[b], tiles, head_dim) * scale)
    sums, inverse, log_rows = [], [], []
    for p in range(pairs):
        a, b = members[p]
        top, total, weights = pair_softmax(scores[p], limit_ref[p : p + 1])
        sums.append(pair_values(weights, pages_ref.at[a], pages_ref.at[b], head_dim))
        total = jnp.where(total > 0.0, total, 1.0)
        inverse.append(1.0 / total)
        log_rows.append(top + jnp.log(total))
    columns = to_columns(inverse)
    keep(0, acc_ref[...], log_ref[0:1])
    for p in range(pairs):
        result = sums[p] * columns[:, p : p + 1]
        keep(2 * p + 1, result[:64], log_rows[p])
        if 2 * p + 1 < others:
            keep(2 * p + 2, result[64:], halves(log_rows[p]))

    value = logs[...]
    lane = lax.broadcasted_iota(jnp.int32, value.shape, 1)
    high = value.astype(jnp.bfloat16).astype(jnp.float32)
    rest = value - high
    middle = rest.astype(jnp.bfloat16).astype(jnp.float32)
    low = rest - middle
    for d in range(n_tp):
        first = (my_tp ^ d) * chunk
        for h in range(chunk):
            rows = results[pl.ds(first + h, n_req, stride=64)]
            out_refs[d][:, h * head_dim : (h + 1) * head_dim] = rows.astype(jnp.bfloat16)
        shift = 128 - first
        stats = jnp.where(lane < chunk, pltpu.roll(high, shift % 128, 1), 0.0)
        stats = jnp.where((lane >= chunk) & (lane < 2 * chunk), pltpu.roll(middle, (shift + chunk) % 128, 1), stats)
        stats = jnp.where((lane >= 2 * chunk) & (lane < 3 * chunk), pltpu.roll(low, (shift + 2 * chunk) % 128, 1), stats)
        out_refs[d][:, chunk * head_dim :] = stats[:n_req].astype(jnp.bfloat16)


def other_attention(q_list, own, n_req, n_tp):
    heads, head_dim = own[0].shape
    chunk = heads // n_tp
    vmem = pl.BlockSpec(memory_space=pltpu.VMEM)
    return pl.pallas_call(
        functools.partial(other_kernel, n_req, n_tp),
        out_shape=[jax.ShapeDtypeStruct((n_req, chunk * head_dim + 128), jnp.bfloat16)] * n_tp,
        in_specs=[vmem] * (n_req + 3),
        out_specs=[vmem] * n_tp,
        scratch_shapes=[
            pltpu.VMEM((n_req * heads, head_dim), jnp.float32),
            pltpu.VMEM((round_up(n_req, 8), 128), jnp.float32),
            pltpu.VMEM((round_up(n_req - 1, 2) // 2, 128, head_dim), jnp.float32),
        ],
        compiler_params=pltpu.CompilerParams(vmem_limit_bytes=16 * MIB),
        cost_estimate=pl.CostEstimate(flops=2 * own[3].size * 16, bytes_accessed=own[3].size * 2, transcendentals=0),
        name="other_attention",
    )(*q_list, *own)


def row_copies(source, first, target, sems):
    parts = sems.shape[0]
    step = target.shape[0] // parts
    return [
        pltpu.make_async_copy(
            source.at[pl.ds(first + i * step, step)], target.at[pl.ds(i * step, step)], sems.at[i]
        )
        for i in range(parts)
    ]


def load_kernel(first, piece_ref, weight_hbm, out_ref, same_ref, sems):
    copies = row_copies(weight_hbm, first, out_ref, sems)
    for copy in copies:
        copy.start()
    same_ref[...] = piece_ref[...]
    for copy in copies:
        copy.wait()


def load_weight(piece, out_weight, first, rows):
    columns = out_weight.shape[1]
    vmem = pl.BlockSpec(memory_space=pltpu.VMEM)
    return pl.pallas_call(
        functools.partial(load_kernel, first),
        out_shape=[
            jax.ShapeDtypeStruct((rows, columns), out_weight.dtype),
            jax.ShapeDtypeStruct(piece.shape, piece.dtype),
        ],
        in_specs=[vmem, pl.BlockSpec(memory_space=pltpu.HBM)],
        out_specs=[vmem] * 2,
        scratch_shapes=[pltpu.SemaphoreType.DMA((4,))],
        compiler_params=pltpu.CompilerParams(vmem_limit_bytes=20 * MIB),
        cost_estimate=pl.CostEstimate(flops=0, bytes_accessed=rows * columns * 4, transcendentals=0),
        name="load_weight",
    )(piece, in_hbm(out_weight))


def project_kernel(n_req, n_tp, *refs):
    part_refs = refs[:n_req]
    weight_refs = refs[n_req : n_req + 2]
    out_refs = refs[n_req + 2 : n_req + 2 + n_tp]
    attention = refs[n_req + 2 + n_tp]
    split, columns = weight_refs[0].shape
    depth = attention.shape[1]
    chunk = depth // 128
    values = []
    for part in part_refs:
        stats = part[:, depth:].astype(jnp.float32)
        values.append(stats + pltpu.roll(stats, 128 - chunk, 1) + pltpu.roll(stats, 128 - 2 * chunk, 1))
    top = functools.reduce(jnp.maximum, values)
    factors = [jnp.exp(v - top) for v in values]
    total = functools.reduce(jnp.add, factors)
    factors = [f / total for f in factors]
    for h in range(chunk):
        at = slice(h * 128, (h + 1) * 128)
        terms = [part[:, at].astype(jnp.float32) * f[:, h : h + 1] for part, f in zip(part_refs, factors)]
        attention[:, at] = functools.reduce(jnp.add, terms).astype(jnp.bfloat16)
    tile = min(columns, 2048)

    @pl.loop(0, columns // tile)
    def _(t):
        at = pl.ds(pl.multiple_of(t * tile, tile), tile)
        product = jnp.dot(attention[:, :split], weight_refs[0][:, at], preferred_element_type=jnp.float32)
        product += jnp.dot(attention[:, split:], weight_refs[1][:, at], preferred_element_type=jnp.float32)
        for i, d in enumerate([0] + near_last(n_tp)):
            out_refs[d][:, at] = product[i * n_req : (i + 1) * n_req].astype(out_refs[d].dtype)


def project(parts, weights, n_req, n_tp):
    depth = sum(w.shape[0] for w in weights)
    columns = weights[0].shape[1]
    vmem = pl.BlockSpec(memory_space=pltpu.VMEM)
    own = jax.ShapeDtypeStruct((n_req, columns), jnp.float32)
    sent = jax.ShapeDtypeStruct((n_req, columns), jnp.bfloat16)
    rows = n_tp * n_req
    return pl.pallas_call(
        functools.partial(project_kernel, n_req, n_tp),
        out_shape=[own] + [sent] * (n_tp - 1),
        in_specs=[vmem] * (n_req + 2),
        out_specs=[vmem] * n_tp,
        scratch_shapes=[pltpu.VMEM((rows, depth), jnp.bfloat16)],
        compiler_params=pltpu.CompilerParams(vmem_limit_bytes=16 * MIB),
        cost_estimate=pl.CostEstimate(
            flops=2 * rows * depth * columns, bytes_accessed=depth * columns * 2, transcendentals=0
        ),
        name="project",
    )(*parts, *weights)


def on_device(queries, new_kv, cache_pool, page_slot, page_owner, context_len, out_weight):
    n_req = lax.axis_size("req")
    n_tp = lax.axis_size("tp")
    pool = cache_pool[0, 0]
    q_list = [swap(queries, "req", d) for d in range(n_req - 1, 0, -1)]
    own = own_attention(queries, new_kv, page_slot, page_owner, context_len, pool, n_req)
    pieces = other_attention(q_list, own, n_req, n_tp)
    depth = out_weight.shape[0]
    early = depth // 4
    swapped = [swap(pieces[d], "tp", d) for d in near_last(n_tp)]
    first, mine = load_weight(pieces[0], out_weight, 0, early)
    arrived = jnp.concatenate([mine] + swapped, axis=0)
    parts = [swap(arrived, "req", d) for d in reversed(near_last(n_req))]
    second, mine = load_weight(arrived, out_weight, early, depth - early)
    sums = project([mine] + parts, (first, second), n_req, n_tp)
    total = sums[0]
    for d in near_last(n_tp):
        total = total + swap(sums[d], "tp", d).astype(jnp.float32)
    return total.astype(jnp.bfloat16)


def solution(mesh):
    placed = (
        P(("groups", "tp", "req"), None),
        P(("groups", "tp", "req"), None),
        P(("groups", "tp"), "req", None, None, None, None),
        P(("groups", "tp"), None, None),
        P(("groups", "tp"), None, None),
        P(("groups", "tp"), None),
        P("tp", "req"),
    )
    return jax.shard_map(
        on_device, mesh=mesh, in_specs=placed, out_specs=P(("groups", "tp"), "req"), check_vma=False
    )
```

```python
import functools
import math

import jax
import jax.numpy as jnp
from jax import lax
from jax.experimental import pallas as pl
from jax.experimental.pallas import tpu as pltpu
from jax.sharding import PartitionSpec as P

very_negative = -1e30
MIB = 1 << 20


def swap(x, axis, offset):
    count = lax.axis_size(axis)
    return lax.ppermute(x, axis, [(i, i ^ offset) for i in range(count)])


def near_last(count):
    return list(range(2, count)) + [1]


def query_order(count):
    return [count - 1, 1] + list(range(2, count - 1))


def in_hbm(x):
    return pltpu.with_memory_space_constraint(x, pltpu.HBM)


def round_up(value, step):
    return -(-value // step) * step


def halves(x):
    return pltpu.roll(x, 64, 1)


def lay_rows(target, start, q_ref):
    head_dim = target.shape[1]
    for h in range(64):
        target[start + h : start + h + 1] = q_ref[0:1, h * head_dim : (h + 1) * head_dim].astype(jnp.float32)


def query_tiles(stacked, kv_heads):
    turned = stacked.T
    lane = lax.broadcasted_iota(jnp.int32, turned.shape, 1)
    group = 64 // kv_heads
    return [
        [
            jnp.where((lane >= a * 64 + h * group) & (lane < a * 64 + (h + 1) * group), turned, 0.0).astype(jnp.bfloat16)
            for a in range(2)
        ]
        for h in range(kv_heads)
    ]


def pair_scores(page_a, page_b, tiles, head_dim):
    total = None
    for h in range(len(tiles)):
        for a, page in enumerate((page_a, page_b)):
            part = jnp.dot(page[h, :, :head_dim], tiles[h][a], preferred_element_type=jnp.float32)
            total = part if total is None else total + part
    return total


def pair_softmax(scores, limit):
    token = lax.broadcasted_iota(jnp.int32, scores.shape, 0)
    mask = token < limit
    masked = jnp.where(mask, scores, very_negative)
    top = jnp.max(masked, axis=0, keepdims=True)
    weights = jnp.where(mask, jnp.exp(masked - top), 0.0)
    return top, jnp.sum(weights, axis=0, keepdims=True), weights


def pair_values(weights, page_a, page_b, head_dim):
    turned = weights.T.astype(jnp.bfloat16)
    kv_heads = page_a.shape[0]
    group = 64 // kv_heads
    blocks = []
    for a, page in enumerate((page_a, page_b)):
        for h in range(kv_heads):
            at = a * 64 + h * group
            blocks.append(
                jnp.dot(turned[at : at + group], page[h, :, head_dim:], preferred_element_type=jnp.float32)
            )
    return jnp.concatenate(blocks, axis=0)


def to_columns(rows):
    stacked = jnp.concatenate(rows + [jnp.zeros((128 - len(rows), 128), jnp.float32)], axis=0)
    return stacked.T


def own_kernel(n_req, own_pages, *refs):
    q_hbm, kv_hbm, slot_hbm, owner_hbm, len_hbm, pool_hbm = refs[:6]
    acc_ref, log_ref, limit_ref, pages_ref = refs[6:10]
    q_row, q_heads, kv, slots, owners, lens, pool, small_sem, pool_sem, page_sem = refs[10:]
    slot_count, kv_heads, page_len, width = pool_hbm.shape
    head_dim = width // 2
    entries = slot_hbm.shape[2]
    me = lax.axis_index("req")
    scale = 1.0 / math.sqrt(head_dim)
    small = [
        pltpu.make_async_copy(src, dst, small_sem.at[i])
        for i, (src, dst) in enumerate(
            ((slot_hbm, slots), (owner_hbm, owners), (len_hbm, lens), (kv_hbm, kv), (q_hbm, q_row))
        )
    ]
    for copy in small:
        copy.start()
    whole = pltpu.make_async_copy(pool_hbm, pool, pool_sem)
    whole.start()
    for copy in small:
        copy.wait()

    fetched = []
    lane = lax.broadcasted_iota(jnp.int32, (1, 128), 1)
    limits = []
    for d in range(1, n_req):
        n = me ^ d
        length = lens[0, n]
        slot = jnp.int32(0)
        limit = jnp.int32(0)
        for j in range(entries):
            held = (owners[0, n, j] == me) & (j * page_len < length)
            slot = jnp.where(held, slots[0, n, j], slot)
            limit = jnp.where(held, length - j * page_len, limit)
        copy = pltpu.make_async_copy(pool_hbm.at[slot], pages_ref.at[d - 1], page_sem.at[d - 1])
        copy.start()
        fetched.append(copy)
        limits.append(limit)
    if len(limits) % 2:
        limits.append(jnp.int32(0))
    for p in range(len(limits) // 2):
        limit_ref[p : p + 1] = jnp.where(lane < 64, limits[2 * p], limits[2 * p + 1])

    lay_rows(q_heads, 0, q_row)
    q_heads[64:] = q_heads[:64]
    tiles = query_tiles(q_heads[...], kv_heads)
    my_length = lens[0, me]
    pages, valid = [], []
    for i in range(own_pages):
        held = (owners[0, me, i] == me) & (i * page_len < my_length)
        pages.append(pool.at[jnp.where(held, slots[0, me, i], 0)])
        valid.append(jnp.where(held, my_length - i * page_len, 0))
    if own_pages % 2:
        pages.append(pages[0])
        valid.append(jnp.int32(0))
    pairs = len(pages) // 2

    base = kv_heads * head_dim
    new_k = [kv[0:1, h * head_dim : (h + 1) * head_dim] for h in range(kv_heads)]
    self_score = None
    for h in range(kv_heads):
        both = tiles[h][0] + tiles[h][1]
        part = jnp.dot(jnp.broadcast_to(new_k[h], (16, head_dim)), both, preferred_element_type=jnp.float32)
        self_score = part if self_score is None else self_score + part
    self_score = self_score[0:1] * scale

    whole.wait()
    scores = [pair_scores(pages[2 * p], pages[2 * p + 1], tiles, head_dim) * scale for p in range(pairs)]
    tops, totals, sums = [], [], []
    for p in range(pairs):
        limit = jnp.where(lane < 64, valid[2 * p], valid[2 * p + 1])
        top, total, weights = pair_softmax(scores[p], limit)
        tops.append(top)
        totals.append(total)
        sums.append(pair_values(weights, pages[2 * p], pages[2 * p + 1], head_dim))
    top = functools.reduce(jnp.maximum, tops)
    top = jnp.maximum(jnp.maximum(top, halves(top)), self_score)
    factors = [jnp.exp(t - top) for t in tops]
    own_factor = jnp.exp(self_score - top)
    total = functools.reduce(jnp.add, [f * t for f, t in zip(factors, totals)])
    total = total + halves(total) + own_factor
    columns = to_columns([f / total for f in factors] + [own_factor / total])
    result = None
    for p in range(pairs):
        term = sums[p] * columns[:, p : p + 1]
        result = term if result is None else result + term
    group = 64 // kv_heads
    new_v = jnp.concatenate(
        [
            jnp.broadcast_to(kv[0:1, base + h * head_dim : base + (h + 1) * head_dim].astype(jnp.float32), (group, head_dim))
            for h in range(kv_heads)
        ],
        axis=0,
    )
    acc_ref[...] = result[:64] + result[64:] + columns[:64, pairs : pairs + 1] * new_v
    log_ref[...] = jnp.broadcast_to(top + jnp.log(total), log_ref.shape)
    for copy in fetched:
        copy.wait()


def own_attention(q, new_kv, page_slot, page_owner, context_len, pool, n_req):
    slots, kv_heads, page_len, width = pool.shape
    head_dim = width // 2
    heads = q.shape[1] // head_dim
    own_pages = min(slots, page_slot.shape[2])
    hbm = pl.BlockSpec(memory_space=pltpu.HBM)
    vmem = pl.BlockSpec(memory_space=pltpu.VMEM)
    pair_count = round_up(n_req - 1, 2) // 2
    page_bytes = pool.size * 2 // slots
    return pl.pallas_call(
        functools.partial(own_kernel, n_req, own_pages),
        out_shape=[
            jax.ShapeDtypeStruct((heads, head_dim), jnp.float32),
            jax.ShapeDtypeStruct((8, 128), jnp.float32),
            jax.ShapeDtypeStruct((round_up(pair_count, 8), 128), jnp.int32),
            jax.ShapeDtypeStruct((n_req - 1, kv_heads, page_len, width), pool.dtype),
        ],
        in_specs=[hbm] * 6,
        out_specs=[vmem] * 4,
        scratch_shapes=[
            pltpu.VMEM(q.shape, q.dtype),
            pltpu.VMEM((128, head_dim), jnp.float32),
            pltpu.VMEM(new_kv.shape, new_kv.dtype),
            pltpu.SMEM(page_slot.shape, jnp.int32),
            pltpu.SMEM(page_owner.shape, jnp.int32),
            pltpu.SMEM(context_len.shape, jnp.int32),
            pltpu.VMEM(pool.shape, pool.dtype),
            pltpu.SemaphoreType.DMA((5,)),
            pltpu.SemaphoreType.DMA,
            pltpu.SemaphoreType.DMA((n_req - 1,)),
        ],
        compiler_params=pltpu.CompilerParams(vmem_limit_bytes=16 * MIB),
        cost_estimate=pl.CostEstimate(
            flops=4 * own_pages * page_len * heads * head_dim,
            bytes_accessed=page_bytes * (slots + n_req - 1) * 2,
            transcendentals=0,
        ),
        name="own_attention",
    )(*(in_hbm(x) for x in (q, new_kv, page_slot, page_owner, context_len, pool)))


def other_kernel(n_req, n_tp, *refs):
    q_of = dict(zip(query_order(n_req), refs[: n_req - 1]))
    q_refs = [q_of[d] for d in range(1, n_req)]
    acc_ref, log_ref, limit_ref, pages_ref = refs[n_req - 1 : n_req + 3]
    out_refs = refs[n_req + 3 : n_req + 3 + n_tp]
    results, logs, q_heads = refs[n_req + 3 + n_tp :]
    kv_heads, width = pages_ref.shape[1], pages_ref.shape[3]
    head_dim = width // 2
    chunk = 64 // n_tp
    my_tp = lax.axis_index("tp")
    me = lax.axis_index("req")
    scale = 1.0 / math.sqrt(head_dim)
    others = n_req - 1
    pairs = round_up(others, 2) // 2

    def keep(d, result, log_row):
        n = me ^ d
        results[pl.ds(pl.multiple_of(n * 64, 64), 64)] = result
        logs[pl.ds(n, 1)] = log_row

    logs[...] = jnp.zeros_like(logs)
    scores, members = [], []
    for p in range(pairs):
        a, b = 2 * p, min(2 * p + 1, others - 1)
        members.append((a, b))
        lay_rows(q_heads.at[p], 0, q_refs[a])
        lay_rows(q_heads.at[p], 64, q_refs[b])
        tiles = query_tiles(q_heads[p], kv_heads)
        scores.append(pair_scores(pages_ref.at[a], pages_ref.at[b], tiles, head_dim) * scale)
    sums, inverse, log_rows = [], [], []
    for p in range(pairs):
        a, b = members[p]
        top, total, weights = pair_softmax(scores[p], limit_ref[p : p + 1])
        sums.append(pair_values(weights, pages_ref.at[a], pages_ref.at[b], head_dim))
        total = jnp.where(total > 0.0, total, 1.0)
        inverse.append(1.0 / total)
        log_rows.append(top + jnp.log(total))
    columns = to_columns(inverse)
    keep(0, acc_ref[...], log_ref[0:1])
    for p in range(pairs):
        result = sums[p] * columns[:, p : p + 1]
        keep(2 * p + 1, result[:64], log_rows[p])
        if 2 * p + 1 < others:
            keep(2 * p + 2, result[64:], halves(log_rows[p]))

    value = logs[...]
    lane = lax.broadcasted_iota(jnp.int32, value.shape, 1)
    high = value.astype(jnp.bfloat16).astype(jnp.float32)
    rest = value - high
    middle = rest.astype(jnp.bfloat16).astype(jnp.float32)
    low = rest - middle
    for d in range(n_tp):
        first = (my_tp ^ d) * chunk
        for h in range(chunk):
            rows = results[pl.ds(first + h, n_req, stride=64)]
            out_refs[d][:, h * head_dim : (h + 1) * head_dim] = rows.astype(jnp.bfloat16)
        shift = 128 - first
        stats = jnp.where(lane < chunk, pltpu.roll(high, shift % 128, 1), 0.0)
        stats = jnp.where((lane >= chunk) & (lane < 2 * chunk), pltpu.roll(middle, (shift + chunk) % 128, 1), stats)
        stats = jnp.where((lane >= 2 * chunk) & (lane < 3 * chunk), pltpu.roll(low, (shift + 2 * chunk) % 128, 1), stats)
        out_refs[d][:, chunk * head_dim :] = stats[:n_req].astype(jnp.bfloat16)


def other_attention(q_list, own, n_req, n_tp):
    heads, head_dim = own[0].shape
    chunk = heads // n_tp
    vmem = pl.BlockSpec(memory_space=pltpu.VMEM)
    return pl.pallas_call(
        functools.partial(other_kernel, n_req, n_tp),
        out_shape=[jax.ShapeDtypeStruct((n_req, chunk * head_dim + 128), jnp.bfloat16)] * n_tp,
        in_specs=[vmem] * (n_req + 3),
        out_specs=[vmem] * n_tp,
        scratch_shapes=[
            pltpu.VMEM((n_req * heads, head_dim), jnp.float32),
            pltpu.VMEM((round_up(n_req, 8), 128), jnp.float32),
            pltpu.VMEM((round_up(n_req - 1, 2) // 2, 128, head_dim), jnp.float32),
        ],
        compiler_params=pltpu.CompilerParams(vmem_limit_bytes=16 * MIB),
        cost_estimate=pl.CostEstimate(flops=2 * own[3].size * 16, bytes_accessed=own[3].size * 2, transcendentals=0),
        name="other_attention",
    )(*q_list, *own)


def row_copies(source, first, column, target, sems):
    parts = sems.shape[0]
    step = target.shape[0] // parts
    columns = pl.ds(column, target.shape[1])
    return [
        pltpu.make_async_copy(
            source.at[pl.ds(first + i * step, step), columns], target.at[pl.ds(i * step, step)], sems.at[i]
        )
        for i in range(parts)
    ]


def load_kernel(first, piece_ref, weight_hbm, out_ref, same_ref, sems):
    copies = row_copies(weight_hbm, first, 0, out_ref, sems)
    for copy in copies:
        copy.start()
    same_ref[...] = piece_ref[...]
    for copy in copies:
        copy.wait()


def load_weight(piece, out_weight, first, rows, columns):
    vmem = pl.BlockSpec(memory_space=pltpu.VMEM)
    return pl.pallas_call(
        functools.partial(load_kernel, first),
        out_shape=[
            jax.ShapeDtypeStruct((rows, columns), out_weight.dtype),
            jax.ShapeDtypeStruct(piece.shape, piece.dtype),
        ],
        in_specs=[vmem, pl.BlockSpec(memory_space=pltpu.HBM)],
        out_specs=[vmem] * 2,
        scratch_shapes=[pltpu.SemaphoreType.DMA((4,))],
        compiler_params=pltpu.CompilerParams(vmem_limit_bytes=20 * MIB),
        cost_estimate=pl.CostEstimate(flops=0, bytes_accessed=rows * columns * 4, transcendentals=0),
        name="load_weight",
    )(piece, in_hbm(out_weight))


def project_kernel(n_req, n_tp, *refs):
    part_refs = refs[:n_req]
    upper, lower, weight_hbm = refs[n_req : n_req + 3]
    out_refs = refs[n_req + 3 : n_req + 3 + n_tp]
    attention, last, sems = refs[n_req + 3 + n_tp :]
    split, columns = upper.shape
    copies = row_copies(weight_hbm, 0, columns, last, sems)
    for copy in copies:
        copy.start()
    depth = attention.shape[1]
    chunk = depth // 128
    values = []
    for part in part_refs:
        stats = part[:, depth:].astype(jnp.float32)
        values.append(stats + pltpu.roll(stats, 128 - chunk, 1) + pltpu.roll(stats, 128 - 2 * chunk, 1))
    top = functools.reduce(jnp.maximum, values)
    factors = [jnp.exp(v - top) for v in values]
    total = functools.reduce(jnp.add, factors)
    factors = [f / total for f in factors]
    for h in range(chunk):
        at = slice(h * 128, (h + 1) * 128)
        terms = [part[:, at].astype(jnp.float32) * f[:, h : h + 1] for part, f in zip(part_refs, factors)]
        attention[:, at] = functools.reduce(jnp.add, terms).astype(jnp.bfloat16)

    def put(product, at):
        for i, d in enumerate([0] + near_last(n_tp)):
            out_refs[d][:, at] = product[i * n_req : (i + 1) * n_req].astype(out_refs[d].dtype)

    tile = columns // pl.cdiv(columns, 2048)
    for t in range(0, columns, tile):
        at = slice(t, t + tile)
        product = jnp.dot(attention[:, :split], upper[:, at], preferred_element_type=jnp.float32)
        product += jnp.dot(attention[:, split:], lower[:, at], preferred_element_type=jnp.float32)
        put(product, at)
    for copy in copies:
        copy.wait()
    product = jnp.dot(attention[...], last[...], preferred_element_type=jnp.float32)
    put(product, slice(columns, columns + last.shape[1]))


def project(parts, weights, out_weight, n_req, n_tp):
    depth, columns = out_weight.shape
    last = columns - weights[0].shape[1]
    vmem = pl.BlockSpec(memory_space=pltpu.VMEM)
    own = jax.ShapeDtypeStruct((n_req, columns), jnp.float32)
    sent = jax.ShapeDtypeStruct((n_req, columns), jnp.bfloat16)
    rows = n_tp * n_req
    return pl.pallas_call(
        functools.partial(project_kernel, n_req, n_tp),
        out_shape=[own] + [sent] * (n_tp - 1),
        in_specs=[vmem] * (n_req + 2) + [pl.BlockSpec(memory_space=pltpu.HBM)],
        out_specs=[vmem] * n_tp,
        scratch_shapes=[
            pltpu.VMEM((rows, depth), jnp.bfloat16),
            pltpu.VMEM((depth, last), jnp.bfloat16),
            pltpu.SemaphoreType.DMA((2,)),
        ],
        compiler_params=pltpu.CompilerParams(vmem_limit_bytes=16 * MIB),
        cost_estimate=pl.CostEstimate(
            flops=2 * rows * depth * columns, bytes_accessed=depth * columns * 2, transcendentals=0
        ),
        name="project",
    )(*parts, *weights, in_hbm(out_weight))


def on_device(queries, new_kv, cache_pool, page_slot, page_owner, context_len, out_weight):
    n_req = lax.axis_size("req")
    n_tp = lax.axis_size("tp")
    pool = cache_pool[0, 0]
    q_list = [swap(queries, "req", d) for d in query_order(n_req)]
    own = own_attention(queries, new_kv, page_slot, page_owner, context_len, pool, n_req)
    pieces = other_attention(q_list, own, n_req, n_tp)
    depth, columns = out_weight.shape
    early = depth // 4
    columns -= min(512, columns // 2)
    swapped = [swap(pieces[d], "tp", d) for d in near_last(n_tp)]
    first, mine = load_weight(pieces[0], out_weight, 0, early, columns)
    arrived = jnp.concatenate([mine] + swapped, axis=0)
    parts = [swap(arrived, "req", d) for d in reversed(near_last(n_req))]
    second, mine = load_weight(arrived, out_weight, early, depth - early, columns)
    sums = project([mine] + parts, (first, second), out_weight, n_req, n_tp)
    total = sums[0]
    for d in near_last(n_tp):
        total = total + swap(sums[d], "tp", d).astype(jnp.float32)
    return total.astype(jnp.bfloat16)


def solution(mesh):
    placed = (
        P(("groups", "tp", "req"), None),
        P(("groups", "tp", "req"), None),
        P(("groups", "tp"), "req", None, None, None, None),
        P(("groups", "tp"), None, None),
        P(("groups", "tp"), None, None),
        P(("groups", "tp"), None),
        P("tp", "req"),
    )
    return jax.shard_map(
        on_device, mesh=mesh, in_specs=placed, out_specs=P(("groups", "tp"), "req"), check_vma=False
    )
```

```python
import functools
import math

import jax
import jax.numpy as jnp
from jax import lax
from jax.experimental import pallas as pl
from jax.experimental.pallas import tpu as pltpu
from jax.sharding import PartitionSpec as P

very_negative = -1e30
MIB = 1 << 20


def swap(x, axis, offset):
    count = lax.axis_size(axis)
    return lax.ppermute(x, axis, [(i, i ^ offset) for i in range(count)])


def near_last(count):
    return list(range(2, count)) + [1]


def far_first(count):
    return list(range(count - 1, 0, -1))


def in_hbm(x):
    return pltpu.with_memory_space_constraint(x, pltpu.HBM)


def round_up(value, step):
    return -(-value // step) * step


def halves(x):
    return pltpu.roll(x, 64, 1)


def lay_rows(target, start, q_ref):
    head_dim = target.shape[1]
    for h in range(64):
        target[start + h : start + h + 1] = q_ref[0:1, h * head_dim : (h + 1) * head_dim].astype(jnp.float32)


def query_tiles(stacked, kv_heads):
    turned = stacked.T
    lane = lax.broadcasted_iota(jnp.int32, turned.shape, 1)
    group = 64 // kv_heads
    return [
        [
            jnp.where((lane >= a * 64 + h * group) & (lane < a * 64 + (h + 1) * group), turned, 0.0).astype(jnp.bfloat16)
            for a in range(2)
        ]
        for h in range(kv_heads)
    ]


def pair_scores(page_a, page_b, tiles, head_dim):
    total = None
    for h in range(len(tiles)):
        for a, page in enumerate((page_a, page_b)):
            part = jnp.dot(page[h, :, :head_dim], tiles[h][a], preferred_element_type=jnp.float32)
            total = part if total is None else total + part
    return total


def pair_softmax(scores, limit):
    token = lax.broadcasted_iota(jnp.int32, scores.shape, 0)
    mask = token < limit
    masked = jnp.where(mask, scores, very_negative)
    top = jnp.max(masked, axis=0, keepdims=True)
    weights = jnp.where(mask, jnp.exp(masked - top), 0.0)
    return top, jnp.sum(weights, axis=0, keepdims=True), weights


def pair_values(weights, page_a, page_b, head_dim):
    turned = weights.T.astype(jnp.bfloat16)
    kv_heads = page_a.shape[0]
    group = 64 // kv_heads
    blocks = []
    for a, page in enumerate((page_a, page_b)):
        for h in range(kv_heads):
            at = a * 64 + h * group
            blocks.append(
                jnp.dot(turned[at : at + group], page[h, :, head_dim:], preferred_element_type=jnp.float32)
            )
    return jnp.concatenate(blocks, axis=0)


def to_columns(rows):
    stacked = jnp.concatenate(rows + [jnp.zeros((128 - len(rows), 128), jnp.float32)], axis=0)
    return stacked.T


def own_kernel(n_req, own_pages, *refs):
    q_hbm, kv_hbm, slot_hbm, owner_hbm, len_hbm, pool_hbm = refs[:6]
    acc_ref, log_ref, limit_ref, pages_ref = refs[6:10]
    q_row, q_heads, kv, slots, owners, lens, pool, small_sem, pool_sem, page_sem = refs[10:]
    slot_count, kv_heads, page_len, width = pool_hbm.shape
    head_dim = width // 2
    entries = slot_hbm.shape[2]
    me = lax.axis_index("req")
    scale = 1.0 / math.sqrt(head_dim)
    small = [
        pltpu.make_async_copy(src, dst, small_sem.at[i])
        for i, (src, dst) in enumerate(
            ((slot_hbm, slots), (owner_hbm, owners), (len_hbm, lens), (kv_hbm, kv), (q_hbm, q_row))
        )
    ]
    for copy in small:
        copy.start()
    whole = pltpu.make_async_copy(pool_hbm, pool, pool_sem)
    whole.start()
    for copy in small:
        copy.wait()

    fetched = []
    lane = lax.broadcasted_iota(jnp.int32, (1, 128), 1)
    limits = []
    for d in range(1, n_req):
        n = me ^ d
        length = lens[0, n]
        slot = jnp.int32(0)
        limit = jnp.int32(0)
        for j in range(entries):
            held = (owners[0, n, j] == me) & (j * page_len < length)
            slot = jnp.where(held, slots[0, n, j], slot)
            limit = jnp.where(held, length - j * page_len, limit)
        copy = pltpu.make_async_copy(pool_hbm.at[slot], pages_ref.at[d - 1], page_sem.at[d - 1])
        copy.start()
        fetched.append(copy)
        limits.append(limit)
    if len(limits) % 2:
        limits.append(jnp.int32(0))
    for p in range(len(limits) // 2):
        limit_ref[p : p + 1] = jnp.where(lane < 64, limits[2 * p], limits[2 * p + 1])

    lay_rows(q_heads, 0, q_row)
    q_heads[64:] = q_heads[:64]
    tiles = query_tiles(q_heads[...], kv_heads)
    my_length = lens[0, me]
    pages, valid = [], []
    for i in range(own_pages):
        held = (owners[0, me, i] == me) & (i * page_len < my_length)
        pages.append(pool.at[jnp.where(held, slots[0, me, i], 0)])
        valid.append(jnp.where(held, my_length - i * page_len, 0))
    if own_pages % 2:
        pages.append(pages[0])
        valid.append(jnp.int32(0))
    pairs = len(pages) // 2

    base = kv_heads * head_dim
    new_k = [kv[0:1, h * head_dim : (h + 1) * head_dim] for h in range(kv_heads)]
    self_score = None
    for h in range(kv_heads):
        both = tiles[h][0] + tiles[h][1]
        part = jnp.dot(jnp.broadcast_to(new_k[h], (16, head_dim)), both, preferred_element_type=jnp.float32)
        self_score = part if self_score is None else self_score + part
    self_score = self_score[0:1] * scale

    whole.wait()
    scores = [pair_scores(pages[2 * p], pages[2 * p + 1], tiles, head_dim) * scale for p in range(pairs)]
    tops, totals, sums = [], [], []
    for p in range(pairs):
        limit = jnp.where(lane < 64, valid[2 * p], valid[2 * p + 1])
        top, total, weights = pair_softmax(scores[p], limit)
        tops.append(top)
        totals.append(total)
        sums.append(pair_values(weights, pages[2 * p], pages[2 * p + 1], head_dim))
    top = functools.reduce(jnp.maximum, tops)
    top = jnp.maximum(jnp.maximum(top, halves(top)), self_score)
    factors = [jnp.exp(t - top) for t in tops]
    own_factor = jnp.exp(self_score - top)
    total = functools.reduce(jnp.add, [f * t for f, t in zip(factors, totals)])
    total = total + halves(total) + own_factor
    columns = to_columns([f / total for f in factors] + [own_factor / total])
    result = None
    for p in range(pairs):
        term = sums[p] * columns[:, p : p + 1]
        result = term if result is None else result + term
    group = 64 // kv_heads
    new_v = jnp.concatenate(
        [
            jnp.broadcast_to(kv[0:1, base + h * head_dim : base + (h + 1) * head_dim].astype(jnp.float32), (group, head_dim))
            for h in range(kv_heads)
        ],
        axis=0,
    )
    acc_ref[...] = result[:64] + result[64:] + columns[:64, pairs : pairs + 1] * new_v
    log_ref[...] = jnp.broadcast_to(top + jnp.log(total), log_ref.shape)
    for copy in fetched:
        copy.wait()


def own_attention(q, new_kv, page_slot, page_owner, context_len, pool, n_req):
    slots, kv_heads, page_len, width = pool.shape
    head_dim = width // 2
    heads = q.shape[1] // head_dim
    own_pages = min(slots, page_slot.shape[2])
    hbm = pl.BlockSpec(memory_space=pltpu.HBM)
    vmem = pl.BlockSpec(memory_space=pltpu.VMEM)
    pair_count = round_up(n_req - 1, 2) // 2
    page_bytes = pool.size * 2 // slots
    return pl.pallas_call(
        functools.partial(own_kernel, n_req, own_pages),
        out_shape=[
            jax.ShapeDtypeStruct((heads, head_dim), jnp.float32),
            jax.ShapeDtypeStruct((8, 128), jnp.float32),
            jax.ShapeDtypeStruct((round_up(pair_count, 8), 128), jnp.int32),
            jax.ShapeDtypeStruct((n_req - 1, kv_heads, page_len, width), pool.dtype),
        ],
        in_specs=[hbm] * 6,
        out_specs=[vmem] * 4,
        scratch_shapes=[
            pltpu.VMEM(q.shape, q.dtype),
            pltpu.VMEM((128, head_dim), jnp.float32),
            pltpu.VMEM(new_kv.shape, new_kv.dtype),
            pltpu.SMEM(page_slot.shape, jnp.int32),
            pltpu.SMEM(page_owner.shape, jnp.int32),
            pltpu.SMEM(context_len.shape, jnp.int32),
            pltpu.VMEM(pool.shape, pool.dtype),
            pltpu.SemaphoreType.DMA((5,)),
            pltpu.SemaphoreType.DMA,
            pltpu.SemaphoreType.DMA((n_req - 1,)),
        ],
        compiler_params=pltpu.CompilerParams(vmem_limit_bytes=16 * MIB),
        cost_estimate=pl.CostEstimate(
            flops=4 * own_pages * page_len * heads * head_dim,
            bytes_accessed=page_bytes * (slots + n_req - 1) * 2,
            transcendentals=0,
        ),
        name="own_attention",
    )(*(in_hbm(x) for x in (q, new_kv, page_slot, page_owner, context_len, pool)))


def other_kernel(n_req, n_tp, *refs):
    q_of = dict(zip(far_first(n_req), refs[: n_req - 1]))
    q_refs = [q_of[d] for d in range(1, n_req)]
    acc_ref, log_ref, limit_ref, pages_ref = refs[n_req - 1 : n_req + 3]
    out_refs = refs[n_req + 3 : n_req + 3 + n_tp]
    results, logs, q_heads = refs[n_req + 3 + n_tp :]
    kv_heads, width = pages_ref.shape[1], pages_ref.shape[3]
    head_dim = width // 2
    chunk = 64 // n_tp
    my_tp = lax.axis_index("tp")
    me = lax.axis_index("req")
    scale = 1.0 / math.sqrt(head_dim)
    others = n_req - 1
    pairs = round_up(others, 2) // 2

    def keep(d, result, log_row):
        n = me ^ d
        results[pl.ds(pl.multiple_of(n * 64, 64), 64)] = result
        logs[pl.ds(n, 1)] = log_row

    logs[...] = jnp.zeros_like(logs)
    scores, members = [], []
    for p in range(pairs):
        a, b = 2 * p, min(2 * p + 1, others - 1)
        members.append((a, b))
        lay_rows(q_heads.at[p], 0, q_refs[a])
        lay_rows(q_heads.at[p], 64, q_refs[b])
        tiles = query_tiles(q_heads[p], kv_heads)
        scores.append(pair_scores(pages_ref.at[a], pages_ref.at[b], tiles, head_dim) * scale)
    sums, inverse, log_rows = [], [], []
    for p in range(pairs):
        a, b = members[p]
        top, total, weights = pair_softmax(scores[p], limit_ref[p : p + 1])
        sums.append(pair_values(weights, pages_ref.at[a], pages_ref.at[b], head_dim))
        total = jnp.where(total > 0.0, total, 1.0)
        inverse.append(1.0 / total)
        log_rows.append(top + jnp.log(total))
    columns = to_columns(inverse)
    keep(0, acc_ref[...], log_ref[0:1])
    for p in range(pairs):
        result = sums[p] * columns[:, p : p + 1]
        keep(2 * p + 1, result[:64], log_rows[p])
        if 2 * p + 1 < others:
            keep(2 * p + 2, result[64:], halves(log_rows[p]))

    value = logs[...]
    lane = lax.broadcasted_iota(jnp.int32, value.shape, 1)
    high = value.astype(jnp.bfloat16).astype(jnp.float32)
    rest = value - high
    middle = rest.astype(jnp.bfloat16).astype(jnp.float32)
    low = rest - middle
    for d in range(n_tp):
        first = (my_tp ^ d) * chunk
        for h in range(chunk):
            rows = results[pl.ds(first + h, n_req, stride=64)]
            out_refs[d][:, h * head_dim : (h + 1) * head_dim] = rows.astype(jnp.bfloat16)
        shift = 128 - first
        stats = jnp.where(lane < chunk, pltpu.roll(high, shift % 128, 1), 0.0)
        stats = jnp.where((lane >= chunk) & (lane < 2 * chunk), pltpu.roll(middle, (shift + chunk) % 128, 1), stats)
        stats = jnp.where((lane >= 2 * chunk) & (lane < 3 * chunk), pltpu.roll(low, (shift + 2 * chunk) % 128, 1), stats)
        out_refs[d][:, chunk * head_dim :] = stats[:n_req].astype(jnp.bfloat16)


def other_attention(q_list, own, n_req, n_tp):
    heads, head_dim = own[0].shape
    chunk = heads // n_tp
    vmem = pl.BlockSpec(memory_space=pltpu.VMEM)
    return pl.pallas_call(
        functools.partial(other_kernel, n_req, n_tp),
        out_shape=[jax.ShapeDtypeStruct((n_req, chunk * head_dim + 128), jnp.bfloat16)] * n_tp,
        in_specs=[vmem] * (n_req + 3),
        out_specs=[vmem] * n_tp,
        scratch_shapes=[
            pltpu.VMEM((n_req * heads, head_dim), jnp.float32),
            pltpu.VMEM((round_up(n_req, 8), 128), jnp.float32),
            pltpu.VMEM((round_up(n_req - 1, 2) // 2, 128, head_dim), jnp.float32),
        ],
        compiler_params=pltpu.CompilerParams(vmem_limit_bytes=16 * MIB),
        cost_estimate=pl.CostEstimate(flops=2 * own[3].size * 16, bytes_accessed=own[3].size * 2, transcendentals=0),
        name="other_attention",
    )(*q_list, *own)


def row_copies(source, first, column, target, sems):
    parts = sems.shape[0]
    step = target.shape[0] // parts
    columns = pl.ds(column, target.shape[1])
    return [
        pltpu.make_async_copy(
            source.at[pl.ds(first + i * step, step), columns], target.at[pl.ds(i * step, step)], sems.at[i]
        )
        for i in range(parts)
    ]


def load_kernel(first, piece_ref, weight_hbm, out_ref, same_ref, sems):
    copies = row_copies(weight_hbm, first, 0, out_ref, sems)
    for copy in copies:
        copy.start()
    same_ref[...] = piece_ref[...]
    for copy in copies:
        copy.wait()


def load_weight(piece, out_weight, first, rows, columns):
    vmem = pl.BlockSpec(memory_space=pltpu.VMEM)
    return pl.pallas_call(
        functools.partial(load_kernel, first),
        out_shape=[
            jax.ShapeDtypeStruct((rows, columns), out_weight.dtype),
            jax.ShapeDtypeStruct(piece.shape, piece.dtype),
        ],
        in_specs=[vmem, pl.BlockSpec(memory_space=pltpu.HBM)],
        out_specs=[vmem] * 2,
        scratch_shapes=[pltpu.SemaphoreType.DMA((4,))],
        compiler_params=pltpu.CompilerParams(vmem_limit_bytes=20 * MIB),
        cost_estimate=pl.CostEstimate(flops=0, bytes_accessed=rows * columns * 4, transcendentals=0),
        name="load_weight",
    )(piece, in_hbm(out_weight))


def project_kernel(n_req, n_tp, *refs):
    part_refs = refs[:n_req]
    upper, lower, weight_hbm = refs[n_req : n_req + 3]
    out_refs = refs[n_req + 3 : n_req + 3 + n_tp]
    attention, last, sems = refs[n_req + 3 + n_tp :]
    split, columns = upper.shape
    copies = row_copies(weight_hbm, 0, columns, last, sems)
    for copy in copies:
        copy.start()
    depth = attention.shape[1]
    chunk = depth // 128
    values = []
    for part in part_refs:
        stats = part[:, depth:].astype(jnp.float32)
        values.append(stats + pltpu.roll(stats, 128 - chunk, 1) + pltpu.roll(stats, 128 - 2 * chunk, 1))
    top = functools.reduce(jnp.maximum, values)
    factors = [jnp.exp(v - top) for v in values]
    total = functools.reduce(jnp.add, factors)
    factors = [f / total for f in factors]
    for h in range(chunk):
        at = slice(h * 128, (h + 1) * 128)
        terms = [part[:, at].astype(jnp.float32) * f[:, h : h + 1] for part, f in zip(part_refs, factors)]
        attention[:, at] = functools.reduce(jnp.add, terms).astype(jnp.bfloat16)

    def put(product, at):
        for i, d in enumerate([0] + far_first(n_tp)):
            out_refs[d][:, at] = product[i * n_req : (i + 1) * n_req].astype(out_refs[d].dtype)

    tile = columns // pl.cdiv(columns, 2048)
    for t in range(0, columns, tile):
        at = slice(t, t + tile)
        product = jnp.dot(attention[:, :split], upper[:, at], preferred_element_type=jnp.float32)
        product += jnp.dot(attention[:, split:], lower[:, at], preferred_element_type=jnp.float32)
        put(product, at)
    for copy in copies:
        copy.wait()
    product = jnp.dot(attention[...], last[...], preferred_element_type=jnp.float32)
    put(product, slice(columns, columns + last.shape[1]))


def project(parts, weights, out_weight, n_req, n_tp):
    depth, columns = out_weight.shape
    last = columns - weights[0].shape[1]
    vmem = pl.BlockSpec(memory_space=pltpu.VMEM)
    own = jax.ShapeDtypeStruct((n_req, columns), jnp.float32)
    sent = jax.ShapeDtypeStruct((n_req, columns), jnp.bfloat16)
    rows = n_tp * n_req
    return pl.pallas_call(
        functools.partial(project_kernel, n_req, n_tp),
        out_shape=[own] + [sent] * (n_tp - 1),
        in_specs=[vmem] * (n_req + 2) + [pl.BlockSpec(memory_space=pltpu.HBM)],
        out_specs=[vmem] * n_tp,
        scratch_shapes=[
            pltpu.VMEM((rows, depth), jnp.bfloat16),
            pltpu.VMEM((depth, last), jnp.bfloat16),
            pltpu.SemaphoreType.DMA((2,)),
        ],
        compiler_params=pltpu.CompilerParams(vmem_limit_bytes=16 * MIB),
        cost_estimate=pl.CostEstimate(
            flops=2 * rows * depth * columns, bytes_accessed=depth * columns * 2, transcendentals=0
        ),
        name="project",
    )(*parts, *weights, in_hbm(out_weight))


def on_device(queries, new_kv, cache_pool, page_slot, page_owner, context_len, out_weight):
    n_req = lax.axis_size("req")
    n_tp = lax.axis_size("tp")
    pool = cache_pool[0, 0]
    q_list = [swap(queries, "req", d) for d in far_first(n_req)]
    own = own_attention(queries, new_kv, page_slot, page_owner, context_len, pool, n_req)
    pieces = other_attention(q_list, own, n_req, n_tp)
    depth, columns = out_weight.shape
    early = depth // 4
    columns -= min(512, columns // 2)
    swapped = [swap(pieces[d], "tp", d) for d in far_first(n_tp)]
    first, mine = load_weight(pieces[0], out_weight, 0, early, columns)
    arrived = jnp.concatenate([mine] + swapped, axis=0)
    parts = [swap(arrived, "req", d) for d in reversed(near_last(n_req))]
    second, mine = load_weight(arrived, out_weight, early, depth - early, columns)
    sums = project([mine] + parts, (first, second), out_weight, n_req, n_tp)
    total = sums[0]
    for d in far_first(n_tp):
        total = total + swap(sums[d], "tp", d).astype(jnp.float32)
    return total.astype(jnp.bfloat16)


def solution(mesh):
    placed = (
        P(("groups", "tp", "req"), None),
        P(("groups", "tp", "req"), None),
        P(("groups", "tp"), "req", None, None, None, None),
        P(("groups", "tp"), None, None),
        P(("groups", "tp"), None, None),
        P(("groups", "tp"), None),
        P("tp", "req"),
    )
    return jax.shard_map(
        on_device, mesh=mesh, in_specs=placed, out_specs=P(("groups", "tp"), "req"), check_vma=False
    )
```

```python
import functools
import math

import jax
import jax.numpy as jnp
from jax import lax
from jax.experimental import pallas as pl
from jax.experimental.pallas import tpu as pltpu
from jax.sharding import PartitionSpec as P

very_negative = -1e30
MIB = 1 << 20


def swap(x, axis, offset):
    count = lax.axis_size(axis)
    return lax.ppermute(x, axis, [(i, i ^ offset) for i in range(count)])


def near_last(count):
    return list(range(2, count)) + [1]


def far_first(count):
    return list(range(count - 1, 0, -1))


def in_hbm(x):
    return pltpu.with_memory_space_constraint(x, pltpu.HBM)


def round_up(value, step):
    return -(-value // step) * step


def halves(x):
    return pltpu.roll(x, 64, 1)


def lay_rows(target, start, q_ref):
    head_dim = target.shape[1]
    for h in range(64):
        target[start + h : start + h + 1] = q_ref[0:1, h * head_dim : (h + 1) * head_dim].astype(jnp.float32)


def query_tiles(stacked, kv_heads):
    turned = stacked.T
    lane = lax.broadcasted_iota(jnp.int32, turned.shape, 1)
    group = 64 // kv_heads
    return [
        [
            jnp.where((lane >= a * 64 + h * group) & (lane < a * 64 + (h + 1) * group), turned, 0.0).astype(jnp.bfloat16)
            for a in range(2)
        ]
        for h in range(kv_heads)
    ]


def pair_scores(page_a, page_b, tiles, head_dim):
    total = None
    for h in range(len(tiles)):
        for a, page in enumerate((page_a, page_b)):
            if page is None:
                continue
            part = jnp.dot(page[h, :, :head_dim], tiles[h][a], preferred_element_type=jnp.float32)
            total = part if total is None else total + part
    return total


def pair_softmax(scores, limit):
    token = lax.broadcasted_iota(jnp.int32, scores.shape, 0)
    mask = token < limit
    masked = jnp.where(mask, scores, very_negative)
    top = jnp.max(masked, axis=0, keepdims=True)
    weights = jnp.where(mask, jnp.exp(masked - top), 0.0)
    return top, jnp.sum(weights, axis=0, keepdims=True), weights


def pair_values(weights, page_a, page_b, head_dim):
    turned = weights.T.astype(jnp.bfloat16)
    kv_heads = page_a.shape[0]
    group = 64 // kv_heads
    blocks = []
    for a, page in enumerate((page_a, page_b)):
        if page is None:
            blocks.append(jnp.zeros((64, head_dim), jnp.float32))
            continue
        for h in range(kv_heads):
            at = a * 64 + h * group
            blocks.append(
                jnp.dot(turned[at : at + group], page[h, :, head_dim:], preferred_element_type=jnp.float32)
            )
    return jnp.concatenate(blocks, axis=0)


def to_columns(rows):
    stacked = jnp.concatenate(rows + [jnp.zeros((128 - len(rows), 128), jnp.float32)], axis=0)
    return stacked.T


def own_kernel(n_req, own_pages, *refs):
    q_hbm, kv_hbm, slot_hbm, owner_hbm, len_hbm, pool_hbm = refs[:6]
    acc_ref, log_ref, limit_ref, pages_ref = refs[6:10]
    q_row, q_heads, kv, slots, owners, lens, pool, small_sem, pool_sem, page_sem = refs[10:]
    slot_count, kv_heads, page_len, width = pool_hbm.shape
    head_dim = width // 2
    entries = slot_hbm.shape[2]
    me = lax.axis_index("req")
    scale = 1.0 / math.sqrt(head_dim)
    small = [
        pltpu.make_async_copy(src, dst, small_sem.at[i])
        for i, (src, dst) in enumerate(
            ((slot_hbm, slots), (owner_hbm, owners), (len_hbm, lens), (kv_hbm, kv), (q_hbm, q_row))
        )
    ]
    for copy in small:
        copy.start()
    whole = pltpu.make_async_copy(pool_hbm, pool, pool_sem)
    whole.start()
    for copy in small:
        copy.wait()

    fetched = []
    lane = lax.broadcasted_iota(jnp.int32, (1, 128), 1)
    limits = []
    for d in range(1, n_req):
        n = me ^ d
        length = lens[0, n]
        slot = jnp.int32(0)
        limit = jnp.int32(0)
        for j in range(entries):
            held = (owners[0, n, j] == me) & (j * page_len < length)
            slot = jnp.where(held, slots[0, n, j], slot)
            limit = jnp.where(held, length - j * page_len, limit)
        copy = pltpu.make_async_copy(pool_hbm.at[slot], pages_ref.at[d - 1], page_sem.at[d - 1])
        copy.start()
        fetched.append(copy)
        limits.append(limit)
    if len(limits) % 2:
        limits.append(jnp.int32(0))
    for p in range(len(limits) // 2):
        limit_ref[p : p + 1] = jnp.where(lane < 64, limits[2 * p], limits[2 * p + 1])

    lay_rows(q_heads, 0, q_row)
    q_heads[64:] = q_heads[:64]
    tiles = query_tiles(q_heads[...], kv_heads)
    my_length = lens[0, me]
    pages, valid = [], []
    for i in range(own_pages):
        held = (owners[0, me, i] == me) & (i * page_len < my_length)
        pages.append(pool.at[jnp.where(held, slots[0, me, i], 0)])
        valid.append(jnp.where(held, my_length - i * page_len, 0))
    if own_pages % 2:
        pages.append(pages[0])
        valid.append(jnp.int32(0))
    pairs = len(pages) // 2

    base = kv_heads * head_dim
    new_k = [kv[0:1, h * head_dim : (h + 1) * head_dim] for h in range(kv_heads)]
    self_score = None
    for h in range(kv_heads):
        both = tiles[h][0] + tiles[h][1]
        part = jnp.dot(jnp.broadcast_to(new_k[h], (16, head_dim)), both, preferred_element_type=jnp.float32)
        self_score = part if self_score is None else self_score + part
    self_score = self_score[0:1] * scale

    whole.wait()
    scores = [pair_scores(pages[2 * p], pages[2 * p + 1], tiles, head_dim) * scale for p in range(pairs)]
    tops, totals, sums = [], [], []
    for p in range(pairs):
        limit = jnp.where(lane < 64, valid[2 * p], valid[2 * p + 1])
        top, total, weights = pair_softmax(scores[p], limit)
        tops.append(top)
        totals.append(total)
        sums.append(pair_values(weights, pages[2 * p], pages[2 * p + 1], head_dim))
    top = functools.reduce(jnp.maximum, tops)
    top = jnp.maximum(jnp.maximum(top, halves(top)), self_score)
    factors = [jnp.exp(t - top) for t in tops]
    own_factor = jnp.exp(self_score - top)
    total = functools.reduce(jnp.add, [f * t for f, t in zip(factors, totals)])
    total = total + halves(total) + own_factor
    columns = to_columns([f / total for f in factors] + [own_factor / total])
    result = None
    for p in range(pairs):
        term = sums[p] * columns[:, p : p + 1]
        result = term if result is None else result + term
    group = 64 // kv_heads
    new_v = jnp.concatenate(
        [
            jnp.broadcast_to(kv[0:1, base + h * head_dim : base + (h + 1) * head_dim].astype(jnp.float32), (group, head_dim))
            for h in range(kv_heads)
        ],
        axis=0,
    )
    acc_ref[...] = result[:64] + result[64:] + columns[:64, pairs : pairs + 1] * new_v
    log_ref[...] = jnp.broadcast_to(top + jnp.log(total), log_ref.shape)
    for copy in fetched:
        copy.wait()


def own_attention(q, new_kv, page_slot, page_owner, context_len, pool, n_req):
    slots, kv_heads, page_len, width = pool.shape
    head_dim = width // 2
    heads = q.shape[1] // head_dim
    own_pages = min(slots, page_slot.shape[2])
    hbm = pl.BlockSpec(memory_space=pltpu.HBM)
    vmem = pl.BlockSpec(memory_space=pltpu.VMEM)
    pair_count = round_up(n_req - 1, 2) // 2
    page_bytes = pool.size * 2 // slots
    return pl.pallas_call(
        functools.partial(own_kernel, n_req, own_pages),
        out_shape=[
            jax.ShapeDtypeStruct((heads, head_dim), jnp.float32),
            jax.ShapeDtypeStruct((8, 128), jnp.float32),
            jax.ShapeDtypeStruct((round_up(pair_count, 8), 128), jnp.int32),
            jax.ShapeDtypeStruct((n_req - 1, kv_heads, page_len, width), pool.dtype),
        ],
        in_specs=[hbm] * 6,
        out_specs=[vmem] * 4,
        scratch_shapes=[
            pltpu.VMEM(q.shape, q.dtype),
            pltpu.VMEM((128, head_dim), jnp.float32),
            pltpu.VMEM(new_kv.shape, new_kv.dtype),
            pltpu.SMEM(page_slot.shape, jnp.int32),
            pltpu.SMEM(page_owner.shape, jnp.int32),
            pltpu.SMEM(context_len.shape, jnp.int32),
            pltpu.VMEM(pool.shape, pool.dtype),
            pltpu.SemaphoreType.DMA((5,)),
            pltpu.SemaphoreType.DMA,
            pltpu.SemaphoreType.DMA((n_req - 1,)),
        ],
        compiler_params=pltpu.CompilerParams(vmem_limit_bytes=16 * MIB),
        cost_estimate=pl.CostEstimate(
            flops=4 * own_pages * page_len * heads * head_dim,
            bytes_accessed=page_bytes * (slots + n_req - 1) * 2,
            transcendentals=0,
        ),
        name="own_attention",
    )(*(in_hbm(x) for x in (q, new_kv, page_slot, page_owner, context_len, pool)))


def other_kernel(n_req, n_tp, *refs):
    q_of = dict(zip(far_first(n_req), refs[: n_req - 1]))
    q_refs = [q_of[d] for d in range(1, n_req)]
    acc_ref, log_ref, limit_ref, pages_ref = refs[n_req - 1 : n_req + 3]
    out_refs = refs[n_req + 3 : n_req + 3 + n_tp]
    results, logs, q_heads = refs[n_req + 3 + n_tp :]
    kv_heads, width = pages_ref.shape[1], pages_ref.shape[3]
    head_dim = width // 2
    chunk = 64 // n_tp
    my_tp = lax.axis_index("tp")
    me = lax.axis_index("req")
    scale = 1.0 / math.sqrt(head_dim)
    others = n_req - 1
    pairs = round_up(others, 2) // 2

    def keep(d, result, log_row):
        n = me ^ d
        results[pl.ds(pl.multiple_of(n * 64, 64), 64)] = result
        logs[pl.ds(n, 1)] = log_row

    logs[...] = jnp.zeros_like(logs)
    scores, members = [], []
    for p in range(pairs):
        a, b = 2 * p, 2 * p + 1
        lay_rows(q_heads.at[p], 0, q_refs[a])
        if b < others:
            lay_rows(q_heads.at[p], 64, q_refs[b])
        else:
            q_heads[p, 64:] = jnp.zeros_like(q_heads[p, 64:])
        members.append((pages_ref.at[a], pages_ref.at[b] if b < others else None))
        tiles = query_tiles(q_heads[p], kv_heads)
        scores.append(pair_scores(*members[p], tiles, head_dim) * scale)
    sums, inverse, log_rows = [], [], []
    for p in range(pairs):
        top, total, weights = pair_softmax(scores[p], limit_ref[p : p + 1])
        sums.append(pair_values(weights, *members[p], head_dim))
        total = jnp.where(total > 0.0, total, 1.0)
        inverse.append(1.0 / total)
        log_rows.append(top + jnp.log(total))
    columns = to_columns(inverse)
    keep(0, acc_ref[...], log_ref[0:1])
    for p in range(pairs):
        result = sums[p] * columns[:, p : p + 1]
        keep(2 * p + 1, result[:64], log_rows[p])
        if 2 * p + 1 < others:
            keep(2 * p + 2, result[64:], halves(log_rows[p]))

    value = logs[...]
    lane = lax.broadcasted_iota(jnp.int32, value.shape, 1)
    high = value.astype(jnp.bfloat16).astype(jnp.float32)
    rest = value - high
    middle = rest.astype(jnp.bfloat16).astype(jnp.float32)
    low = rest - middle
    for d in range(n_tp):
        first = (my_tp ^ d) * chunk
        for h in range(chunk):
            rows = results[pl.ds(first + h, n_req, stride=64)]
            out_refs[d][:, h * head_dim : (h + 1) * head_dim] = rows.astype(jnp.bfloat16)
        shift = 128 - first
        stats = jnp.where(lane < chunk, pltpu.roll(high, shift % 128, 1), 0.0)
        stats = jnp.where((lane >= chunk) & (lane < 2 * chunk), pltpu.roll(middle, (shift + chunk) % 128, 1), stats)
        stats = jnp.where((lane >= 2 * chunk) & (lane < 3 * chunk), pltpu.roll(low, (shift + 2 * chunk) % 128, 1), stats)
        out_refs[d][:, chunk * head_dim :] = stats[:n_req].astype(jnp.bfloat16)


def other_attention(q_list, own, n_req, n_tp):
    heads, head_dim = own[0].shape
    chunk = heads // n_tp
    vmem = pl.BlockSpec(memory_space=pltpu.VMEM)
    return pl.pallas_call(
        functools.partial(other_kernel, n_req, n_tp),
        out_shape=[jax.ShapeDtypeStruct((n_req, chunk * head_dim + 128), jnp.bfloat16)] * n_tp,
        in_specs=[vmem] * (n_req + 3),
        out_specs=[vmem] * n_tp,
        scratch_shapes=[
            pltpu.VMEM((n_req * heads, head_dim), jnp.float32),
            pltpu.VMEM((round_up(n_req, 8), 128), jnp.float32),
            pltpu.VMEM((round_up(n_req - 1, 2) // 2, 128, head_dim), jnp.float32),
        ],
        compiler_params=pltpu.CompilerParams(vmem_limit_bytes=16 * MIB),
        cost_estimate=pl.CostEstimate(flops=2 * own[3].size * 16, bytes_accessed=own[3].size * 2, transcendentals=0),
        name="other_attention",
    )(*q_list, *own)


def row_copies(source, column, target, sems):
    parts = sems.shape[0]
    step = target.shape[0] // parts
    columns = pl.ds(column, target.shape[1])
    return [
        pltpu.make_async_copy(
            source.at[pl.ds(i * step, step), columns], target.at[pl.ds(i * step, step)], sems.at[i]
        )
        for i in range(parts)
    ]


def load_kernel(piece_ref, weight_hbm, out_ref, same_ref, sems):
    copies = row_copies(weight_hbm, 0, out_ref, sems)
    for copy in copies:
        copy.start()
    same_ref[...] = piece_ref[...]
    for copy in copies:
        copy.wait()


def load_weight(piece, out_weight, columns):
    depth = out_weight.shape[0]
    vmem = pl.BlockSpec(memory_space=pltpu.VMEM)
    return pl.pallas_call(
        load_kernel,
        out_shape=[
            jax.ShapeDtypeStruct((depth, columns), out_weight.dtype),
            jax.ShapeDtypeStruct(piece.shape, piece.dtype),
        ],
        in_specs=[vmem, pl.BlockSpec(memory_space=pltpu.HBM)],
        out_specs=[vmem] * 2,
        scratch_shapes=[pltpu.SemaphoreType.DMA((4,))],
        compiler_params=pltpu.CompilerParams(vmem_limit_bytes=20 * MIB),
        cost_estimate=pl.CostEstimate(flops=0, bytes_accessed=depth * columns * 4, transcendentals=0),
        name="load_weight",
    )(piece, in_hbm(out_weight))


def project_kernel(n_req, n_tp, *refs):
    part_refs = refs[:n_req]
    weight, weight_hbm = refs[n_req : n_req + 2]
    out_refs = refs[n_req + 2 : n_req + 2 + n_tp]
    attention, last, sems = refs[n_req + 2 + n_tp :]
    columns = weight.shape[1]
    copies = row_copies(weight_hbm, columns, last, sems)
    for copy in copies:
        copy.start()
    depth = attention.shape[1]
    chunk = depth // 128
    values = []
    for part in part_refs:
        stats = part[:, depth:].astype(jnp.float32)
        values.append(stats + pltpu.roll(stats, 128 - chunk, 1) + pltpu.roll(stats, 128 - 2 * chunk, 1))
    top = functools.reduce(jnp.maximum, values)
    factors = [jnp.exp(v - top) for v in values]
    total = functools.reduce(jnp.add, factors)
    factors = [f / total for f in factors]
    for h in range(chunk):
        at = slice(h * 128, (h + 1) * 128)
        terms = [part[:, at].astype(jnp.float32) * f[:, h : h + 1] for part, f in zip(part_refs, factors)]
        attention[:, at] = functools.reduce(jnp.add, terms).astype(jnp.bfloat16)

    def put(product, at):
        for i, d in enumerate([0] + far_first(n_tp)):
            out_refs[d][:, at] = product[i * n_req : (i + 1) * n_req].astype(out_refs[d].dtype)

    tile = round_up(pl.cdiv(columns, pl.cdiv(columns, 2048)), 256)
    for t in range(0, columns, tile):
        at = slice(t, min(t + tile, columns))
        put(jnp.dot(attention[...], weight[:, at], preferred_element_type=jnp.float32), at)
    for copy in copies:
        copy.wait()
    product = jnp.dot(attention[...], last[...], preferred_element_type=jnp.float32)
    put(product, slice(columns, columns + last.shape[1]))


def project(parts, weight, out_weight, n_req, n_tp):
    depth, columns = out_weight.shape
    last = columns - weight.shape[1]
    vmem = pl.BlockSpec(memory_space=pltpu.VMEM)
    own = jax.ShapeDtypeStruct((n_req, columns), jnp.float32)
    sent = jax.ShapeDtypeStruct((n_req, columns), jnp.bfloat16)
    rows = n_tp * n_req
    return pl.pallas_call(
        functools.partial(project_kernel, n_req, n_tp),
        out_shape=[own] + [sent] * (n_tp - 1),
        in_specs=[vmem] * (n_req + 1) + [pl.BlockSpec(memory_space=pltpu.HBM)],
        out_specs=[vmem] * n_tp,
        scratch_shapes=[
            pltpu.VMEM((rows, depth), jnp.bfloat16),
            pltpu.VMEM((depth, last), jnp.bfloat16),
            pltpu.SemaphoreType.DMA((2,)),
        ],
        compiler_params=pltpu.CompilerParams(vmem_limit_bytes=16 * MIB),
        cost_estimate=pl.CostEstimate(
            flops=2 * rows * depth * columns, bytes_accessed=depth * columns * 2, transcendentals=0
        ),
        name="project",
    )(*parts, weight, in_hbm(out_weight))


def on_device(queries, new_kv, cache_pool, page_slot, page_owner, context_len, out_weight):
    n_req = lax.axis_size("req")
    n_tp = lax.axis_size("tp")
    pool = cache_pool[0, 0]
    q_list = [swap(queries, "req", d) for d in far_first(n_req)]
    own = own_attention(queries, new_kv, page_slot, page_owner, context_len, pool, n_req)
    pieces = other_attention(q_list, own, n_req, n_tp)
    columns = out_weight.shape[1]
    columns -= min(768, columns // 2)
    swapped = [swap(pieces[d], "tp", d) for d in far_first(n_tp)]
    arrived = jnp.concatenate([pieces[0]] + swapped, axis=0)
    parts = [swap(arrived, "req", d) for d in reversed(near_last(n_req))]
    weight, mine = load_weight(arrived, out_weight, columns)
    sums = project([mine] + parts, weight, out_weight, n_req, n_tp)
    total = sums[0]
    for d in far_first(n_tp):
        total = total + swap(sums[d], "tp", d).astype(jnp.float32)
    return total.astype(jnp.bfloat16)


def solution(mesh):
    placed = (
        P(("groups", "tp", "req"), None),
        P(("groups", "tp", "req"), None),
        P(("groups", "tp"), "req", None, None, None, None),
        P(("groups", "tp"), None, None),
        P(("groups", "tp"), None, None),
        P(("groups", "tp"), None),
        P("tp", "req"),
    )
    return jax.shard_map(
        on_device, mesh=mesh, in_specs=placed, out_specs=P(("groups", "tp"), "req"), check_vma=False
    )
```

```python
import functools
import math

import jax
import jax.numpy as jnp
from jax import lax
from jax.experimental import pallas as pl
from jax.experimental.pallas import tpu as pltpu
from jax.sharding import PartitionSpec as P

very_negative = -1e30
MIB = 1 << 20


def swap(x, axis, offset):
    count = lax.axis_size(axis)
    return lax.ppermute(x, axis, [(i, i ^ offset) for i in range(count)])


def far_first(count):
    return list(range(count - 1, 0, -1))


def in_hbm(x):
    return pltpu.with_memory_space_constraint(x, pltpu.HBM)


def round_up(value, step):
    return -(-value // step) * step


def halves(x):
    return pltpu.roll(x, 64, 1)


def lay_rows(target, start, q_ref):
    head_dim = target.shape[1]
    for h in range(64):
        target[start + h : start + h + 1] = q_ref[0:1, h * head_dim : (h + 1) * head_dim].astype(jnp.float32)


def query_tiles(stacked, kv_heads):
    turned = stacked.T
    lane = lax.broadcasted_iota(jnp.int32, turned.shape, 1)
    group = 64 // kv_heads
    return [
        [
            jnp.where((lane >= a * 64 + h * group) & (lane < a * 64 + (h + 1) * group), turned, 0.0).astype(jnp.bfloat16)
            for a in range(2)
        ]
        for h in range(kv_heads)
    ]


def pair_scores(page_a, page_b, tiles, head_dim):
    total = None
    for h in range(len(tiles)):
        for a, page in enumerate((page_a, page_b)):
            part = jnp.dot(page[h, :, :head_dim], tiles[h][a], preferred_element_type=jnp.float32)
            total = part if total is None else total + part
    return total


def pair_softmax(scores, limit):
    token = lax.broadcasted_iota(jnp.int32, scores.shape, 0)
    mask = token < limit
    masked = jnp.where(mask, scores, very_negative)
    top = jnp.max(masked, axis=0, keepdims=True)
    weights = jnp.where(mask, jnp.exp(masked - top), 0.0)
    return top, jnp.sum(weights, axis=0, keepdims=True), weights


def pair_values(weights, page_a, page_b, head_dim):
    turned = weights.T.astype(jnp.bfloat16)
    kv_heads = page_a.shape[0]
    group = 64 // kv_heads
    blocks = []
    for a, page in enumerate((page_a, page_b)):
        for h in range(kv_heads):
            at = a * 64 + h * group
            blocks.append(
                jnp.dot(turned[at : at + group], page[h, :, head_dim:], preferred_element_type=jnp.float32)
            )
    return jnp.concatenate(blocks, axis=0)


def to_columns(rows):
    stacked = jnp.concatenate(rows + [jnp.zeros((128 - len(rows), 128), jnp.float32)], axis=0)
    return stacked.T


def own_kernel(n_req, own_pages, *refs):
    q_hbm, kv_hbm, slot_hbm, owner_hbm, len_hbm, pool_hbm = refs[:6]
    acc_ref, log_ref, limit_ref, pages_ref = refs[6:10]
    q_row, q_heads, kv, slots, owners, lens, pool, small_sem, pool_sem, page_sem = refs[10:]
    slot_count, kv_heads, page_len, width = pool_hbm.shape
    head_dim = width // 2
    entries = slot_hbm.shape[2]
    me = lax.axis_index("req")
    scale = 1.0 / math.sqrt(head_dim)
    small = [
        pltpu.make_async_copy(src, dst, small_sem.at[i])
        for i, (src, dst) in enumerate(
            ((slot_hbm, slots), (owner_hbm, owners), (len_hbm, lens), (kv_hbm, kv), (q_hbm, q_row))
        )
    ]
    for copy in small:
        copy.start()
    whole = pltpu.make_async_copy(pool_hbm, pool, pool_sem)
    whole.start()
    for copy in small:
        copy.wait()

    fetched = []
    lane = lax.broadcasted_iota(jnp.int32, (1, 128), 1)
    limits = []
    for d in range(1, n_req):
        n = me ^ d
        length = lens[0, n]
        slot = jnp.int32(0)
        limit = jnp.int32(0)
        for j in range(entries):
            held = (owners[0, n, j] == me) & (j * page_len < length)
            slot = jnp.where(held, slots[0, n, j], slot)
            limit = jnp.where(held, length - j * page_len, limit)
        copy = pltpu.make_async_copy(pool_hbm.at[slot], pages_ref.at[d - 1], page_sem.at[d - 1])
        copy.start()
        fetched.append(copy)
        limits.append(limit)
    if len(limits) % 2:
        limits.append(jnp.int32(0))
    for p in range(len(limits) // 2):
        limit_ref[p : p + 1] = jnp.where(lane < 64, limits[2 * p], limits[2 * p + 1])

    lay_rows(q_heads, 0, q_row)
    q_heads[64:] = q_heads[:64]
    tiles = query_tiles(q_heads[...], kv_heads)
    my_length = lens[0, me]
    pages, valid = [], []
    for i in range(own_pages):
        held = (owners[0, me, i] == me) & (i * page_len < my_length)
        pages.append(pool.at[jnp.where(held, slots[0, me, i], 0)])
        valid.append(jnp.where(held, my_length - i * page_len, 0))
    if own_pages % 2:
        pages.append(pages[0])
        valid.append(jnp.int32(0))
    pairs = len(pages) // 2

    base = kv_heads * head_dim
    new_k = [kv[0:1, h * head_dim : (h + 1) * head_dim] for h in range(kv_heads)]
    self_score = None
    for h in range(kv_heads):
        both = tiles[h][0] + tiles[h][1]
        part = jnp.dot(jnp.broadcast_to(new_k[h], (16, head_dim)), both, preferred_element_type=jnp.float32)
        self_score = part if self_score is None else self_score + part
    self_score = self_score[0:1] * scale

    whole.wait()
    scores = [pair_scores(pages[2 * p], pages[2 * p + 1], tiles, head_dim) * scale for p in range(pairs)]
    tops, totals, sums = [], [], []
    for p in range(pairs):
        limit = jnp.where(lane < 64, valid[2 * p], valid[2 * p + 1])
        top, total, weights = pair_softmax(scores[p], limit)
        tops.append(top)
        totals.append(total)
        sums.append(pair_values(weights, pages[2 * p], pages[2 * p + 1], head_dim))
    top = functools.reduce(jnp.maximum, tops)
    top = jnp.maximum(jnp.maximum(top, halves(top)), self_score)
    factors = [jnp.exp(t - top) for t in tops]
    own_factor = jnp.exp(self_score - top)
    total = functools.reduce(jnp.add, [f * t for f, t in zip(factors, totals)])
    total = total + halves(total) + own_factor
    columns = to_columns([f / total for f in factors] + [own_factor / total])
    result = None
    for p in range(pairs):
        term = sums[p] * columns[:, p : p + 1]
        result = term if result is None else result + term
    group = 64 // kv_heads
    new_v = jnp.concatenate(
        [
            jnp.broadcast_to(kv[0:1, base + h * head_dim : base + (h + 1) * head_dim].astype(jnp.float32), (group, head_dim))
            for h in range(kv_heads)
        ],
        axis=0,
    )
    acc_ref[...] = result[:64] + result[64:] + columns[:64, pairs : pairs + 1] * new_v
    log_ref[...] = jnp.broadcast_to(top + jnp.log(total), log_ref.shape)
    for copy in fetched:
        copy.wait()


def own_attention(q, new_kv, page_slot, page_owner, context_len, pool, n_req):
    slots, kv_heads, page_len, width = pool.shape
    head_dim = width // 2
    heads = q.shape[1] // head_dim
    own_pages = min(slots, page_slot.shape[2])
    hbm = pl.BlockSpec(memory_space=pltpu.HBM)
    vmem = pl.BlockSpec(memory_space=pltpu.VMEM)
    pair_count = round_up(n_req - 1, 2) // 2
    page_bytes = pool.size * 2 // slots
    return pl.pallas_call(
        functools.partial(own_kernel, n_req, own_pages),
        out_shape=[
            jax.ShapeDtypeStruct((heads, head_dim), jnp.float32),
            jax.ShapeDtypeStruct((8, 128), jnp.float32),
            jax.ShapeDtypeStruct((round_up(pair_count, 8), 128), jnp.int32),
            jax.ShapeDtypeStruct((n_req - 1, kv_heads, page_len, width), pool.dtype),
        ],
        in_specs=[hbm] * 6,
        out_specs=[vmem] * 4,
        scratch_shapes=[
            pltpu.VMEM(q.shape, q.dtype),
            pltpu.VMEM((128, head_dim), jnp.float32),
            pltpu.VMEM(new_kv.shape, new_kv.dtype),
            pltpu.SMEM(page_slot.shape, jnp.int32),
            pltpu.SMEM(page_owner.shape, jnp.int32),
            pltpu.SMEM(context_len.shape, jnp.int32),
            pltpu.VMEM(pool.shape, pool.dtype),
            pltpu.SemaphoreType.DMA((5,)),
            pltpu.SemaphoreType.DMA,
            pltpu.SemaphoreType.DMA((n_req - 1,)),
        ],
        compiler_params=pltpu.CompilerParams(vmem_limit_bytes=16 * MIB),
        cost_estimate=pl.CostEstimate(
            flops=4 * own_pages * page_len * heads * head_dim,
            bytes_accessed=page_bytes * (slots + n_req - 1) * 2,
            transcendentals=0,
        ),
        name="own_attention",
    )(*(in_hbm(x) for x in (q, new_kv, page_slot, page_owner, context_len, pool)))


def other_kernel(n_req, n_tp, *refs):
    q_of = dict(zip(far_first(n_req), refs[: n_req - 1]))
    q_refs = [q_of[d] for d in range(1, n_req)]
    acc_ref, log_ref, limit_ref, pages_ref = refs[n_req - 1 : n_req + 3]
    out_refs = refs[n_req + 3 : n_req + 3 + n_tp]
    results, logs, q_heads = refs[n_req + 3 + n_tp :]
    kv_heads, width = pages_ref.shape[1], pages_ref.shape[3]
    head_dim = width // 2
    chunk = 64 // n_tp
    my_tp = lax.axis_index("tp")
    me = lax.axis_index("req")
    scale = 1.0 / math.sqrt(head_dim)
    others = n_req - 1
    pairs = round_up(others, 2) // 2

    def keep(d, result, log_row):
        n = me ^ d
        results[pl.ds(pl.multiple_of(n * 64, 64), 64)] = result
        logs[pl.ds(n, 1)] = log_row

    logs[...] = jnp.zeros_like(logs)
    scores, members = [], []
    for p in range(pairs):
        a, b = 2 * p, min(2 * p + 1, others - 1)
        members.append((a, b))
        lay_rows(q_heads.at[p], 0, q_refs[a])
        lay_rows(q_heads.at[p], 64, q_refs[b])
        tiles = query_tiles(q_heads[p], kv_heads)
        scores.append(pair_scores(pages_ref.at[a], pages_ref.at[b], tiles, head_dim) * scale)
    sums, inverse, log_rows = [], [], []
    for p in range(pairs):
        a, b = members[p]
        top, total, weights = pair_softmax(scores[p], limit_ref[p : p + 1])
        sums.append(pair_values(weights, pages_ref.at[a], pages_ref.at[b], head_dim))
        total = jnp.where(total > 0.0, total, 1.0)
        inverse.append(1.0 / total)
        log_rows.append(top + jnp.log(total))
    columns = to_columns(inverse)
    keep(0, acc_ref[...], log_ref[0:1])
    for p in range(pairs):
        result = sums[p] * columns[:, p : p + 1]
        keep(2 * p + 1, result[:64], log_rows[p])
        if 2 * p + 1 < others:
            keep(2 * p + 2, result[64:], halves(log_rows[p]))

    value = logs[...]
    lane = lax.broadcasted_iota(jnp.int32, value.shape, 1)
    high = value.astype(jnp.bfloat16).astype(jnp.float32)
    rest = value - high
    middle = rest.astype(jnp.bfloat16).astype(jnp.float32)
    low = rest - middle
    for d in range(n_tp):
        first = (my_tp ^ d) * chunk
        for h in range(chunk):
            rows = results[pl.ds(first + h, n_req, stride=64)]
            out_refs[d][:, h * head_dim : (h + 1) * head_dim] = rows.astype(jnp.bfloat16)
        shift = 128 - first
        stats = jnp.where(lane < chunk, pltpu.roll(high, shift % 128, 1), 0.0)
        stats = jnp.where((lane >= chunk) & (lane < 2 * chunk), pltpu.roll(middle, (shift + chunk) % 128, 1), stats)
        stats = jnp.where((lane >= 2 * chunk) & (lane < 3 * chunk), pltpu.roll(low, (shift + 2 * chunk) % 128, 1), stats)
        out_refs[d][:, chunk * head_dim :] = stats[:n_req].astype(jnp.bfloat16)


def other_attention(q_list, own, n_req, n_tp):
    heads, head_dim = own[0].shape
    chunk = heads // n_tp
    vmem = pl.BlockSpec(memory_space=pltpu.VMEM)
    return pl.pallas_call(
        functools.partial(other_kernel, n_req, n_tp),
        out_shape=[jax.ShapeDtypeStruct((n_req, chunk * head_dim + 128), jnp.bfloat16)] * n_tp,
        in_specs=[vmem] * (n_req + 3),
        out_specs=[vmem] * n_tp,
        scratch_shapes=[
            pltpu.VMEM((n_req * heads, head_dim), jnp.float32),
            pltpu.VMEM((round_up(n_req, 8), 128), jnp.float32),
            pltpu.VMEM((round_up(n_req - 1, 2) // 2, 128, head_dim), jnp.float32),
        ],
        compiler_params=pltpu.CompilerParams(vmem_limit_bytes=16 * MIB),
        cost_estimate=pl.CostEstimate(flops=2 * own[3].size * 16, bytes_accessed=own[3].size * 2, transcendentals=0),
        name="other_attention",
    )(*q_list, *own)


def row_copies(source, first, column, target, sems):
    parts = sems.shape[0]
    step = target.shape[0] // parts
    columns = pl.ds(column, target.shape[1])
    return [
        pltpu.make_async_copy(
            source.at[pl.ds(first + i * step, step), columns], target.at[pl.ds(i * step, step)], sems.at[i]
        )
        for i in range(parts)
    ]


def load_kernel(first, piece_ref, weight_hbm, out_ref, same_ref, sems):
    copies = row_copies(weight_hbm, first, 0, out_ref, sems)
    for copy in copies:
        copy.start()
    same_ref[...] = piece_ref[...]
    for copy in copies:
        copy.wait()


def load_weight(piece, out_weight, first, rows, columns):
    vmem = pl.BlockSpec(memory_space=pltpu.VMEM)
    return pl.pallas_call(
        functools.partial(load_kernel, first),
        out_shape=[
            jax.ShapeDtypeStruct((rows, columns), out_weight.dtype),
            jax.ShapeDtypeStruct(piece.shape, piece.dtype),
        ],
        in_specs=[vmem, pl.BlockSpec(memory_space=pltpu.HBM)],
        out_specs=[vmem] * 2,
        scratch_shapes=[pltpu.SemaphoreType.DMA((8,))],
        compiler_params=pltpu.CompilerParams(vmem_limit_bytes=20 * MIB),
        cost_estimate=pl.CostEstimate(flops=0, bytes_accessed=rows * columns * 4, transcendentals=0),
        name="load_weight",
    )(piece, in_hbm(out_weight))


def project_kernel(n_req, n_tp, *refs):
    part_refs = refs[:n_req]
    upper, lower, weight_hbm = refs[n_req : n_req + 3]
    out_refs = refs[n_req + 3 : n_req + 3 + n_tp]
    attention, last, sems = refs[n_req + 3 + n_tp :]
    split, columns = upper.shape
    copies = row_copies(weight_hbm, 0, columns, last, sems)
    for copy in copies:
        copy.start()
    depth = attention.shape[1]
    chunk = depth // 128
    values = []
    for part in part_refs:
        stats = part[:, depth:].astype(jnp.float32)
        values.append(stats + pltpu.roll(stats, 128 - chunk, 1) + pltpu.roll(stats, 128 - 2 * chunk, 1))
    top = functools.reduce(jnp.maximum, values)
    factors = [jnp.exp(v - top) for v in values]
    total = functools.reduce(jnp.add, factors)
    factors = [f / total for f in factors]
    for h in range(chunk):
        at = slice(h * 128, (h + 1) * 128)
        terms = [part[:, at].astype(jnp.float32) * f[:, h : h + 1] for part, f in zip(part_refs, factors)]
        attention[:, at] = functools.reduce(jnp.add, terms).astype(jnp.bfloat16)

    def put(product, at):
        for i, d in enumerate([0] + far_first(n_tp)):
            out_refs[d][:, at] = product[i * n_req : (i + 1) * n_req].astype(out_refs[d].dtype)

    tile = columns // pl.cdiv(columns, 2048)
    for t in range(0, columns, tile):
        at = slice(t, t + tile)
        product = jnp.dot(attention[:, :split], upper[:, at], preferred_element_type=jnp.float32)
        product += jnp.dot(attention[:, split:], lower[:, at], preferred_element_type=jnp.float32)
        put(product, at)
    for copy in copies:
        copy.wait()
    product = jnp.dot(attention[...], last[...], preferred_element_type=jnp.float32)
    put(product, slice(columns, columns + last.shape[1]))


def project(parts, weights, out_weight, n_req, n_tp):
    depth, columns = out_weight.shape
    last = columns - weights[0].shape[1]
    vmem = pl.BlockSpec(memory_space=pltpu.VMEM)
    own = jax.ShapeDtypeStruct((n_req, columns), jnp.float32)
    sent = jax.ShapeDtypeStruct((n_req, columns), jnp.bfloat16)
    rows = n_tp * n_req
    return pl.pallas_call(
        functools.partial(project_kernel, n_req, n_tp),
        out_shape=[own] + [sent] * (n_tp - 1),
        in_specs=[vmem] * (n_req + 2) + [pl.BlockSpec(memory_space=pltpu.HBM)],
        out_specs=[vmem] * n_tp,
        scratch_shapes=[
            pltpu.VMEM((rows, depth), jnp.bfloat16),
            pltpu.VMEM((depth, last), jnp.bfloat16),
            pltpu.SemaphoreType.DMA((8,)),
        ],
        compiler_params=pltpu.CompilerParams(vmem_limit_bytes=16 * MIB),
        cost_estimate=pl.CostEstimate(
            flops=2 * rows * depth * columns, bytes_accessed=depth * columns * 2, transcendentals=0
        ),
        name="project",
    )(*parts, *weights, in_hbm(out_weight))


def on_device(queries, new_kv, cache_pool, page_slot, page_owner, context_len, out_weight):
    n_req = lax.axis_size("req")
    n_tp = lax.axis_size("tp")
    pool = cache_pool[0, 0]
    q_list = [swap(queries, "req", d) for d in far_first(n_req)]
    own = own_attention(queries, new_kv, page_slot, page_owner, context_len, pool, n_req)
    pieces = other_attention(q_list, own, n_req, n_tp)
    depth, columns = out_weight.shape
    early = depth // 4
    columns -= min(512, columns // 2)
    swapped = [swap(pieces[d], "tp", d) for d in far_first(n_tp)]
    first, mine = load_weight(pieces[0], out_weight, 0, early, columns)
    arrived = jnp.concatenate([mine] + swapped, axis=0)
    parts = [swap(arrived, "req", d) for d in range(1, n_req)]
    second, mine = load_weight(arrived, out_weight, early, depth - early, columns)
    sums = project([mine] + parts, (first, second), out_weight, n_req, n_tp)
    total = sums[0]
    for d in far_first(n_tp):
        total = total + swap(sums[d], "tp", d).astype(jnp.float32)
    return total.astype(jnp.bfloat16)


def solution(mesh):
    placed = (
        P(("groups", "tp", "req"), None),
        P(("groups", "tp", "req"), None),
        P(("groups", "tp"), "req", None, None, None, None),
        P(("groups", "tp"), None, None),
        P(("groups", "tp"), None, None),
        P(("groups", "tp"), None),
        P("tp", "req"),
    )
    return jax.shard_map(
        on_device, mesh=mesh, in_specs=placed, out_specs=P(("groups", "tp"), "req"), check_vma=False
    )
```

```python
import functools
import math

import jax
import jax.numpy as jnp
from jax import lax
from jax.experimental import pallas as pl
from jax.experimental.pallas import tpu as pltpu
from jax.sharding import PartitionSpec as P

very_negative = -1e30
MIB = 1 << 20


def swap(x, axis, offset):
    count = lax.axis_size(axis)
    return lax.ppermute(x, axis, [(i, i ^ offset) for i in range(count)])


def near_last(count):
    return list(range(2, count)) + [1]


def far_first(count):
    return list(range(count - 1, 0, -1))


def in_hbm(x):
    return pltpu.with_memory_space_constraint(x, pltpu.HBM)


def round_up(value, step):
    return -(-value // step) * step


def halves(x):
    return pltpu.roll(x, 64, 1)


def lay_rows(target, start, q_ref):
    head_dim = target.shape[1]
    for h in range(64):
        target[start + h : start + h + 1] = q_ref[0:1, h * head_dim : (h + 1) * head_dim].astype(jnp.float32)


def query_tiles(stacked, kv_heads):
    turned = stacked.T
    lane = lax.broadcasted_iota(jnp.int32, turned.shape, 1)
    group = 64 // kv_heads
    return [
        [
            jnp.where((lane >= a * 64 + h * group) & (lane < a * 64 + (h + 1) * group), turned, 0.0).astype(jnp.bfloat16)
            for a in range(2)
        ]
        for h in range(kv_heads)
    ]


def pair_scores(page_a, page_b, tiles, head_dim):
    total = None
    for h in range(len(tiles)):
        for a, page in enumerate((page_a, page_b)):
            part = jnp.dot(page[h, :, :head_dim], tiles[h][a], preferred_element_type=jnp.float32)
            total = part if total is None else total + part
    return total


def pair_softmax(scores, limit):
    token = lax.broadcasted_iota(jnp.int32, scores.shape, 0)
    mask = token < limit
    masked = jnp.where(mask, scores, very_negative)
    top = jnp.max(masked, axis=0, keepdims=True)
    weights = jnp.where(mask, jnp.exp(masked - top), 0.0)
    return top, jnp.sum(weights, axis=0, keepdims=True), weights


def pair_values(weights, page_a, page_b, head_dim):
    turned = weights.T.astype(jnp.bfloat16)
    kv_heads = page_a.shape[0]
    group = 64 // kv_heads
    blocks = []
    for a, page in enumerate((page_a, page_b)):
        for h in range(kv_heads):
            at = a * 64 + h * group
            blocks.append(
                jnp.dot(turned[at : at + group], page[h, :, head_dim:], preferred_element_type=jnp.float32)
            )
    return jnp.concatenate(blocks, axis=0)


def to_columns(rows):
    stacked = jnp.concatenate(rows + [jnp.zeros((128 - len(rows), 128), jnp.float32)], axis=0)
    return stacked.T


def own_kernel(n_req, own_pages, *refs):
    q_hbm, kv_hbm, slot_hbm, owner_hbm, len_hbm, pool_hbm = refs[:6]
    acc_ref, log_ref, limit_ref, pages_ref = refs[6:10]
    q_row, q_heads, kv, slots, owners, lens, pool, small_sem, pool_sem, page_sem = refs[10:]
    slot_count, kv_heads, page_len, width = pool_hbm.shape
    head_dim = width // 2
    entries = slot_hbm.shape[2]
    me = lax.axis_index("req")
    scale = 1.0 / math.sqrt(head_dim)
    small = [
        pltpu.make_async_copy(src, dst, small_sem.at[i])
        for i, (src, dst) in enumerate(
            ((slot_hbm, slots), (owner_hbm, owners), (len_hbm, lens), (kv_hbm, kv), (q_hbm, q_row))
        )
    ]
    for copy in small:
        copy.start()
    whole = pltpu.make_async_copy(pool_hbm, pool, pool_sem)
    whole.start()
    for copy in small:
        copy.wait()

    fetched = []
    lane = lax.broadcasted_iota(jnp.int32, (1, 128), 1)
    limits = []
    for d in range(1, n_req):
        n = me ^ d
        length = lens[0, n]
        slot = jnp.int32(0)
        limit = jnp.int32(0)
        for j in range(entries):
            held = (owners[0, n, j] == me) & (j * page_len < length)
            slot = jnp.where(held, slots[0, n, j], slot)
            limit = jnp.where(held, length - j * page_len, limit)
        copy = pltpu.make_async_copy(pool_hbm.at[slot], pages_ref.at[d - 1], page_sem.at[d - 1])
        copy.start()
        fetched.append(copy)
        limits.append(limit)
    if len(limits) % 2:
        limits.append(jnp.int32(0))
    for p in range(len(limits) // 2):
        limit_ref[p : p + 1] = jnp.where(lane < 64, limits[2 * p], limits[2 * p + 1])

    lay_rows(q_heads, 0, q_row)
    q_heads[64:] = q_heads[:64]
    tiles = query_tiles(q_heads[...], kv_heads)
    my_length = lens[0, me]
    pages, valid = [], []
    for i in range(own_pages):
        held = (owners[0, me, i] == me) & (i * page_len < my_length)
        pages.append(pool.at[jnp.where(held, slots[0, me, i], 0)])
        valid.append(jnp.where(held, my_length - i * page_len, 0))
    if own_pages % 2:
        pages.append(pages[0])
        valid.append(jnp.int32(0))
    pairs = len(pages) // 2

    base = kv_heads * head_dim
    new_k = [kv[0:1, h * head_dim : (h + 1) * head_dim] for h in range(kv_heads)]
    self_score = None
    for h in range(kv_heads):
        both = tiles[h][0] + tiles[h][1]
        part = jnp.dot(jnp.broadcast_to(new_k[h], (16, head_dim)), both, preferred_element_type=jnp.float32)
        self_score = part if self_score is None else self_score + part
    self_score = self_score[0:1] * scale

    whole.wait()
    scores = [pair_scores(pages[2 * p], pages[2 * p + 1], tiles, head_dim) * scale for p in range(pairs)]
    tops, totals, sums = [], [], []
    for p in range(pairs):
        limit = jnp.where(lane < 64, valid[2 * p], valid[2 * p + 1])
        top, total, weights = pair_softmax(scores[p], limit)
        tops.append(top)
        totals.append(total)
        sums.append(pair_values(weights, pages[2 * p], pages[2 * p + 1], head_dim))
    top = functools.reduce(jnp.maximum, tops)
    top = jnp.maximum(jnp.maximum(top, halves(top)), self_score)
    factors = [jnp.exp(t - top) for t in tops]
    own_factor = jnp.exp(self_score - top)
    total = functools.reduce(jnp.add, [f * t for f, t in zip(factors, totals)])
    total = total + halves(total) + own_factor
    columns = to_columns([f / total for f in factors] + [own_factor / total])
    result = None
    for p in range(pairs):
        term = sums[p] * columns[:, p : p + 1]
        result = term if result is None else result + term
    group = 64 // kv_heads
    new_v = jnp.concatenate(
        [
            jnp.broadcast_to(kv[0:1, base + h * head_dim : base + (h + 1) * head_dim].astype(jnp.float32), (group, head_dim))
            for h in range(kv_heads)
        ],
        axis=0,
    )
    acc_ref[...] = result[:64] + result[64:] + columns[:64, pairs : pairs + 1] * new_v
    log_ref[...] = jnp.broadcast_to(top + jnp.log(total), log_ref.shape)
    for copy in fetched:
        copy.wait()


def own_attention(q, new_kv, page_slot, page_owner, context_len, pool, n_req):
    slots, kv_heads, page_len, width = pool.shape
    head_dim = width // 2
    heads = q.shape[1] // head_dim
    own_pages = min(slots, page_slot.shape[2])
    hbm = pl.BlockSpec(memory_space=pltpu.HBM)
    vmem = pl.BlockSpec(memory_space=pltpu.VMEM)
    pair_count = round_up(n_req - 1, 2) // 2
    page_bytes = pool.size * 2 // slots
    return pl.pallas_call(
        functools.partial(own_kernel, n_req, own_pages),
        out_shape=[
            jax.ShapeDtypeStruct((heads, head_dim), jnp.float32),
            jax.ShapeDtypeStruct((8, 128), jnp.float32),
            jax.ShapeDtypeStruct((round_up(pair_count, 8), 128), jnp.int32),
            jax.ShapeDtypeStruct((n_req - 1, kv_heads, page_len, width), pool.dtype),
        ],
        in_specs=[hbm] * 6,
        out_specs=[vmem] * 4,
        scratch_shapes=[
            pltpu.VMEM(q.shape, q.dtype),
            pltpu.VMEM((128, head_dim), jnp.float32),
            pltpu.VMEM(new_kv.shape, new_kv.dtype),
            pltpu.SMEM(page_slot.shape, jnp.int32),
            pltpu.SMEM(page_owner.shape, jnp.int32),
            pltpu.SMEM(context_len.shape, jnp.int32),
            pltpu.VMEM(pool.shape, pool.dtype),
            pltpu.SemaphoreType.DMA((5,)),
            pltpu.SemaphoreType.DMA,
            pltpu.SemaphoreType.DMA((n_req - 1,)),
        ],
        compiler_params=pltpu.CompilerParams(vmem_limit_bytes=16 * MIB),
        cost_estimate=pl.CostEstimate(
            flops=4 * own_pages * page_len * heads * head_dim,
            bytes_accessed=page_bytes * (slots + n_req - 1) * 2,
            transcendentals=0,
        ),
        name="own_attention",
    )(*(in_hbm(x) for x in (q, new_kv, page_slot, page_owner, context_len, pool)))


def other_kernel(n_req, n_tp, *refs):
    q_of = dict(zip(far_first(n_req), refs[: n_req - 1]))
    q_refs = [q_of[d] for d in range(1, n_req)]
    acc_ref, log_ref, limit_ref, pages_ref = refs[n_req - 1 : n_req + 3]
    out_refs = refs[n_req + 3 : n_req + 3 + n_tp]
    results, logs, q_heads = refs[n_req + 3 + n_tp :]
    kv_heads, width = pages_ref.shape[1], pages_ref.shape[3]
    head_dim = width // 2
    chunk = 64 // n_tp
    my_tp = lax.axis_index("tp")
    me = lax.axis_index("req")
    scale = 1.0 / math.sqrt(head_dim)
    others = n_req - 1
    pairs = round_up(others, 2) // 2

    def keep(d, result, log_row):
        n = me ^ d
        results[pl.ds(pl.multiple_of(n * 64, 64), 64)] = result
        logs[pl.ds(n, 1)] = log_row

    logs[...] = jnp.zeros_like(logs)
    scores, members = [], []
    for p in range(pairs):
        a, b = 2 * p, min(2 * p + 1, others - 1)
        members.append((a, b))
        lay_rows(q_heads.at[p], 0, q_refs[a])
        lay_rows(q_heads.at[p], 64, q_refs[b])
        tiles = query_tiles(q_heads[p], kv_heads)
        scores.append(pair_scores(pages_ref.at[a], pages_ref.at[b], tiles, head_dim) * scale)
    sums, inverse, log_rows = [], [], []
    for p in range(pairs):
        a, b = members[p]
        top, total, weights = pair_softmax(scores[p], limit_ref[p : p + 1])
        sums.append(pair_values(weights, pages_ref.at[a], pages_ref.at[b], head_dim))
        total = jnp.where(total > 0.0, total, 1.0)
        inverse.append(1.0 / total)
        log_rows.append(top + jnp.log(total))
    columns = to_columns(inverse)
    keep(0, acc_ref[...], log_ref[0:1])
    for p in range(pairs):
        result = sums[p] * columns[:, p : p + 1]
        keep(2 * p + 1, result[:64], log_rows[p])
        if 2 * p + 1 < others:
            keep(2 * p + 2, result[64:], halves(log_rows[p]))

    value = logs[...]
    lane = lax.broadcasted_iota(jnp.int32, value.shape, 1)
    high = value.astype(jnp.bfloat16).astype(jnp.float32)
    rest = value - high
    middle = rest.astype(jnp.bfloat16).astype(jnp.float32)
    low = rest - middle
    for d in range(n_tp):
        first = (my_tp ^ d) * chunk
        for h in range(chunk):
            rows = results[pl.ds(first + h, n_req, stride=64)]
            out_refs[d][:, h * head_dim : (h + 1) * head_dim] = rows.astype(jnp.bfloat16)
        shift = 128 - first
        stats = jnp.where(lane < chunk, pltpu.roll(high, shift % 128, 1), 0.0)
        stats = jnp.where((lane >= chunk) & (lane < 2 * chunk), pltpu.roll(middle, (shift + chunk) % 128, 1), stats)
        stats = jnp.where((lane >= 2 * chunk) & (lane < 3 * chunk), pltpu.roll(low, (shift + 2 * chunk) % 128, 1), stats)
        out_refs[d][:, chunk * head_dim :] = stats[:n_req].astype(jnp.bfloat16)


def other_attention(q_list, own, n_req, n_tp):
    heads, head_dim = own[0].shape
    chunk = heads // n_tp
    vmem = pl.BlockSpec(memory_space=pltpu.VMEM)
    return pl.pallas_call(
        functools.partial(other_kernel, n_req, n_tp),
        out_shape=[jax.ShapeDtypeStruct((n_req, chunk * head_dim + 128), jnp.bfloat16)] * n_tp,
        in_specs=[vmem] * (n_req + 3),
        out_specs=[vmem] * n_tp,
        scratch_shapes=[
            pltpu.VMEM((n_req * heads, head_dim), jnp.float32),
            pltpu.VMEM((round_up(n_req, 8), 128), jnp.float32),
            pltpu.VMEM((round_up(n_req - 1, 2) // 2, 128, head_dim), jnp.float32),
        ],
        compiler_params=pltpu.CompilerParams(vmem_limit_bytes=16 * MIB),
        cost_estimate=pl.CostEstimate(flops=2 * own[3].size * 16, bytes_accessed=own[3].size * 2, transcendentals=0),
        name="other_attention",
    )(*q_list, *own)


def row_copies(source, first, column, target, sems):
    parts = sems.shape[0]
    step = target.shape[0] // parts
    columns = pl.ds(column, target.shape[1])
    return [
        pltpu.make_async_copy(
            source.at[pl.ds(first + i * step, step), columns], target.at[pl.ds(i * step, step)], sems.at[i]
        )
        for i in range(parts)
    ]


def load_kernel(first, piece_ref, weight_hbm, out_ref, same_ref, sems):
    copies = row_copies(weight_hbm, first, 0, out_ref, sems)
    for copy in copies:
        copy.start()
    same_ref[...] = piece_ref[...]
    for copy in copies:
        copy.wait()


def load_weight(piece, out_weight, first, rows, columns):
    vmem = pl.BlockSpec(memory_space=pltpu.VMEM)
    return pl.pallas_call(
        functools.partial(load_kernel, first),
        out_shape=[
            jax.ShapeDtypeStruct((rows, columns), out_weight.dtype),
            jax.ShapeDtypeStruct(piece.shape, piece.dtype),
        ],
        in_specs=[vmem, pl.BlockSpec(memory_space=pltpu.HBM)],
        out_specs=[vmem] * 2,
        scratch_shapes=[pltpu.SemaphoreType.DMA((4,))],
        compiler_params=pltpu.CompilerParams(vmem_limit_bytes=20 * MIB),
        cost_estimate=pl.CostEstimate(flops=0, bytes_accessed=rows * columns * 4, transcendentals=0),
        name="load_weight",
    )(piece, in_hbm(out_weight))


def project_kernel(n_req, n_tp, *refs):
    part_refs = refs[:n_req]
    upper, lower = refs[n_req : n_req + 2]
    out_refs = refs[n_req + 2 : n_req + 2 + n_tp]
    attention = refs[n_req + 2 + n_tp]
    split, columns = upper.shape
    depth = attention.shape[1]
    chunk = depth // 128
    values = []
    for part in part_refs:
        stats = part[:, depth:].astype(jnp.float32)
        values.append(stats + pltpu.roll(stats, 128 - chunk, 1) + pltpu.roll(stats, 128 - 2 * chunk, 1))
    top = functools.reduce(jnp.maximum, values)
    factors = [jnp.exp(v - top) for v in values]
    total = functools.reduce(jnp.add, factors)
    factors = [f / total for f in factors]
    for h in range(chunk):
        at = slice(h * 128, (h + 1) * 128)
        terms = [part[:, at].astype(jnp.float32) * f[:, h : h + 1] for part, f in zip(part_refs, factors)]
        attention[:, at] = functools.reduce(jnp.add, terms).astype(jnp.bfloat16)

    def put(product, at):
        for i, d in enumerate([0] + far_first(n_tp)):
            out_refs[d][:, at] = product[i * n_req : (i + 1) * n_req].astype(out_refs[d].dtype)

    tile = columns // pl.cdiv(columns, 2048)
    for t in range(0, columns, tile):
        at = slice(t, t + tile)
        product = jnp.dot(attention[:, :split], upper[:, at], preferred_element_type=jnp.float32)
        product += jnp.dot(attention[:, split:], lower[:, at], preferred_element_type=jnp.float32)
        put(product, at)


def project(parts, weights, n_req, n_tp):
    depth = sum(w.shape[0] for w in weights)
    columns = weights[0].shape[1]
    vmem = pl.BlockSpec(memory_space=pltpu.VMEM)
    own = jax.ShapeDtypeStruct((n_req, columns), jnp.float32)
    sent = jax.ShapeDtypeStruct((n_req, columns), jnp.bfloat16)
    rows = n_tp * n_req
    return pl.pallas_call(
        functools.partial(project_kernel, n_req, n_tp),
        out_shape=[own] + [sent] * (n_tp - 1),
        in_specs=[vmem] * (n_req + 2),
        out_specs=[vmem] * n_tp,
        scratch_shapes=[pltpu.VMEM((rows, depth), jnp.bfloat16)],
        compiler_params=pltpu.CompilerParams(vmem_limit_bytes=16 * MIB),
        cost_estimate=pl.CostEstimate(
            flops=2 * rows * depth * columns, bytes_accessed=depth * columns * 2, transcendentals=0
        ),
        name="project",
    )(*parts, *weights)


def on_device(queries, new_kv, cache_pool, page_slot, page_owner, context_len, out_weight):
    n_req = lax.axis_size("req")
    n_tp = lax.axis_size("tp")
    pool = cache_pool[0, 0]
    q_list = [swap(queries, "req", d) for d in far_first(n_req)]
    own = own_attention(queries, new_kv, page_slot, page_owner, context_len, pool, n_req)
    pieces = other_attention(q_list, own, n_req, n_tp)
    depth, columns = out_weight.shape
    early = depth // 4
    swapped = [swap(pieces[d], "tp", d) for d in far_first(n_tp)]
    first, mine = load_weight(pieces[0], out_weight, 0, early, columns)
    arrived = jnp.concatenate([mine] + swapped, axis=0)
    parts = [swap(arrived, "req", d) for d in reversed(near_last(n_req))]
    second, mine = load_weight(arrived, out_weight, early, depth - early, columns)
    sums = project([mine] + parts, (first, second), n_req, n_tp)
    total = sums[0]
    for d in far_first(n_tp):
        total = total + swap(sums[d], "tp", d).astype(jnp.float32)
    return total.astype(jnp.bfloat16)


def solution(mesh):
    placed = (
        P(("groups", "tp", "req"), None),
        P(("groups", "tp", "req"), None),
        P(("groups", "tp"), "req", None, None, None, None),
        P(("groups", "tp"), None, None),
        P(("groups", "tp"), None, None),
        P(("groups", "tp"), None),
        P("tp", "req"),
    )
    return jax.shard_map(
        on_device, mesh=mesh, in_specs=placed, out_specs=P(("groups", "tp"), "req"), check_vma=False
    )
```

```python
import functools
import math

import jax
import jax.numpy as jnp
from jax import lax
from jax.experimental import pallas as pl
from jax.experimental.pallas import tpu as pltpu
from jax.sharding import PartitionSpec as P

very_negative = -1e30
MIB = 1 << 20


def swap(x, axis, offset):
    count = lax.axis_size(axis)
    return lax.ppermute(x, axis, [(i, i ^ offset) for i in range(count)])


def far_first(count):
    return list(range(count - 1, 0, -1))


def in_hbm(x):
    return pltpu.with_memory_space_constraint(x, pltpu.HBM)


def round_up(value, step):
    return -(-value // step) * step


def halves(x):
    return pltpu.roll(x, 64, 1)


def lay_rows(target, start, q_ref):
    head_dim = target.shape[1]
    for h in range(64):
        target[start + h : start + h + 1] = q_ref[0:1, h * head_dim : (h + 1) * head_dim].astype(jnp.float32)


def query_tiles(stacked, kv_heads):
    turned = stacked.T
    lane = lax.broadcasted_iota(jnp.int32, turned.shape, 1)
    group = 64 // kv_heads
    return [
        [
            jnp.where((lane >= a * 64 + h * group) & (lane < a * 64 + (h + 1) * group), turned, 0.0).astype(jnp.bfloat16)
            for a in range(2)
        ]
        for h in range(kv_heads)
    ]


def pair_scores(page_a, page_b, tiles, head_dim):
    total = None
    for h in range(len(tiles)):
        for a, page in enumerate((page_a, page_b)):
            part = jnp.dot(page[h, :, :head_dim], tiles[h][a], preferred_element_type=jnp.float32)
            total = part if total is None else total + part
    return total


def pair_softmax(scores, limit):
    token = lax.broadcasted_iota(jnp.int32, scores.shape, 0)
    mask = token < limit
    masked = jnp.where(mask, scores, very_negative)
    top = jnp.max(masked, axis=0, keepdims=True)
    weights = jnp.where(mask, jnp.exp(masked - top), 0.0)
    return top, jnp.sum(weights, axis=0, keepdims=True), weights


def pair_values(weights, page_a, page_b, head_dim):
    turned = weights.T.astype(jnp.bfloat16)
    kv_heads = page_a.shape[0]
    group = 64 // kv_heads
    blocks = []
    for a, page in enumerate((page_a, page_b)):
        for h in range(kv_heads):
            at = a * 64 + h * group
            blocks.append(
                jnp.dot(turned[at : at + group], page[h, :, head_dim:], preferred_element_type=jnp.float32)
            )
    return jnp.concatenate(blocks, axis=0)


def to_columns(rows):
    stacked = jnp.concatenate(rows + [jnp.zeros((128 - len(rows), 128), jnp.float32)], axis=0)
    return stacked.T


def own_kernel(n_req, own_pages, *refs):
    q_hbm, kv_hbm, slot_hbm, owner_hbm, len_hbm, pool_hbm = refs[:6]
    acc_ref, log_ref, limit_ref, pages_ref = refs[6:10]
    q_row, q_heads, kv, slots, owners, lens, pool, small_sem, pool_sem, page_sem = refs[10:]
    slot_count, kv_heads, page_len, width = pool_hbm.shape
    head_dim = width // 2
    entries = slot_hbm.shape[2]
    me = lax.axis_index("req")
    scale = 1.0 / math.sqrt(head_dim)
    small = [
        pltpu.make_async_copy(src, dst, small_sem.at[i])
        for i, (src, dst) in enumerate(
            ((slot_hbm, slots), (owner_hbm, owners), (len_hbm, lens), (kv_hbm, kv), (q_hbm, q_row))
        )
    ]
    for copy in small:
        copy.start()
    whole = pltpu.make_async_copy(pool_hbm, pool, pool_sem)
    whole.start()
    for copy in small:
        copy.wait()

    fetched = []
    lane = lax.broadcasted_iota(jnp.int32, (1, 128), 1)
    limits = []
    for d in range(1, n_req):
        n = me ^ d
        length = lens[0, n]
        slot = jnp.int32(0)
        limit = jnp.int32(0)
        for j in range(entries):
            held = (owners[0, n, j] == me) & (j * page_len < length)
            slot = jnp.where(held, slots[0, n, j], slot)
            limit = jnp.where(held, length - j * page_len, limit)
        copy = pltpu.make_async_copy(pool_hbm.at[slot], pages_ref.at[d - 1], page_sem.at[d - 1])
        copy.start()
        fetched.append(copy)
        limits.append(limit)
    if len(limits) % 2:
        limits.append(jnp.int32(0))
    for p in range(len(limits) // 2):
        limit_ref[p : p + 1] = jnp.where(lane < 64, limits[2 * p], limits[2 * p + 1])

    lay_rows(q_heads, 0, q_row)
    q_heads[64:] = q_heads[:64]
    tiles = query_tiles(q_heads[...], kv_heads)
    my_length = lens[0, me]
    pages, valid = [], []
    for i in range(own_pages):
        held = (owners[0, me, i] == me) & (i * page_len < my_length)
        pages.append(pool.at[jnp.where(held, slots[0, me, i], 0)])
        valid.append(jnp.where(held, my_length - i * page_len, 0))
    if own_pages % 2:
        pages.append(pages[0])
        valid.append(jnp.int32(0))
    pairs = len(pages) // 2

    base = kv_heads * head_dim
    new_k = [kv[0:1, h * head_dim : (h + 1) * head_dim] for h in range(kv_heads)]
    self_score = None
    for h in range(kv_heads):
        both = tiles[h][0] + tiles[h][1]
        part = jnp.dot(jnp.broadcast_to(new_k[h], (16, head_dim)), both, preferred_element_type=jnp.float32)
        self_score = part if self_score is None else self_score + part
    self_score = self_score[0:1] * scale

    whole.wait()
    scores = [pair_scores(pages[2 * p], pages[2 * p + 1], tiles, head_dim) * scale for p in range(pairs)]
    tops, totals, sums = [], [], []
    for p in range(pairs):
        limit = jnp.where(lane < 64, valid[2 * p], valid[2 * p + 1])
        top, total, weights = pair_softmax(scores[p], limit)
        tops.append(top)
        totals.append(total)
        sums.append(pair_values(weights, pages[2 * p], pages[2 * p + 1], head_dim))
    top = functools.reduce(jnp.maximum, tops)
    top = jnp.maximum(jnp.maximum(top, halves(top)), self_score)
    factors = [jnp.exp(t - top) for t in tops]
    own_factor = jnp.exp(self_score - top)
    total = functools.reduce(jnp.add, [f * t for f, t in zip(factors, totals)])
    total = total + halves(total) + own_factor
    columns = to_columns([f / total for f in factors] + [own_factor / total])
    result = None
    for p in range(pairs):
        term = sums[p] * columns[:, p : p + 1]
        result = term if result is None else result + term
    group = 64 // kv_heads
    new_v = jnp.concatenate(
        [
            jnp.broadcast_to(kv[0:1, base + h * head_dim : base + (h + 1) * head_dim].astype(jnp.float32), (group, head_dim))
            for h in range(kv_heads)
        ],
        axis=0,
    )
    acc_ref[...] = result[:64] + result[64:] + columns[:64, pairs : pairs + 1] * new_v
    log_ref[...] = jnp.broadcast_to(top + jnp.log(total), log_ref.shape)
    for copy in fetched:
        copy.wait()


def own_attention(q, new_kv, page_slot, page_owner, context_len, pool, n_req):
    slots, kv_heads, page_len, width = pool.shape
    head_dim = width // 2
    heads = q.shape[1] // head_dim
    own_pages = min(slots, page_slot.shape[2])
    hbm = pl.BlockSpec(memory_space=pltpu.HBM)
    vmem = pl.BlockSpec(memory_space=pltpu.VMEM)
    pair_count = round_up(n_req - 1, 2) // 2
    page_bytes = pool.size * 2 // slots
    return pl.pallas_call(
        functools.partial(own_kernel, n_req, own_pages),
        out_shape=[
            jax.ShapeDtypeStruct((heads, head_dim), jnp.float32),
            jax.ShapeDtypeStruct((8, 128), jnp.float32),
            jax.ShapeDtypeStruct((round_up(pair_count, 8), 128), jnp.int32),
            jax.ShapeDtypeStruct((n_req - 1, kv_heads, page_len, width), pool.dtype),
        ],
        in_specs=[hbm] * 6,
        out_specs=[vmem] * 4,
        scratch_shapes=[
            pltpu.VMEM(q.shape, q.dtype),
            pltpu.VMEM((128, head_dim), jnp.float32),
            pltpu.VMEM(new_kv.shape, new_kv.dtype),
            pltpu.SMEM(page_slot.shape, jnp.int32),
            pltpu.SMEM(page_owner.shape, jnp.int32),
            pltpu.SMEM(context_len.shape, jnp.int32),
            pltpu.VMEM(pool.shape, pool.dtype),
            pltpu.SemaphoreType.DMA((5,)),
            pltpu.SemaphoreType.DMA,
            pltpu.SemaphoreType.DMA((n_req - 1,)),
        ],
        compiler_params=pltpu.CompilerParams(vmem_limit_bytes=16 * MIB),
        cost_estimate=pl.CostEstimate(
            flops=4 * own_pages * page_len * heads * head_dim,
            bytes_accessed=page_bytes * (slots + n_req - 1) * 2,
            transcendentals=0,
        ),
        name="own_attention",
    )(*(in_hbm(x) for x in (q, new_kv, page_slot, page_owner, context_len, pool)))


def other_kernel(n_req, n_tp, *refs):
    q_of = dict(zip(far_first(n_req), refs[: n_req - 1]))
    q_refs = [q_of[d] for d in range(1, n_req)]
    acc_ref, log_ref, limit_ref, pages_ref = refs[n_req - 1 : n_req + 3]
    out_refs = refs[n_req + 3 : n_req + 3 + n_tp]
    results, logs, q_heads = refs[n_req + 3 + n_tp :]
    kv_heads, width = pages_ref.shape[1], pages_ref.shape[3]
    head_dim = width // 2
    chunk = 64 // n_tp
    my_tp = lax.axis_index("tp")
    me = lax.axis_index("req")
    scale = 1.0 / math.sqrt(head_dim)
    others = n_req - 1
    pairs = round_up(others, 2) // 2

    def keep(d, result, log_row):
        n = me ^ d
        results[pl.ds(pl.multiple_of(n * 64, 64), 64)] = result
        logs[pl.ds(n, 1)] = log_row

    logs[...] = jnp.zeros_like(logs)
    scores, members = [], []
    for p in range(pairs):
        a, b = 2 * p, min(2 * p + 1, others - 1)
        members.append((a, b))
        lay_rows(q_heads.at[p], 0, q_refs[a])
        lay_rows(q_heads.at[p], 64, q_refs[b])
        tiles = query_tiles(q_heads[p], kv_heads)
        scores.append(pair_scores(pages_ref.at[a], pages_ref.at[b], tiles, head_dim) * scale)
    sums, inverse, log_rows = [], [], []
    for p in range(pairs):
        a, b = members[p]
        top, total, weights = pair_softmax(scores[p], limit_ref[p : p + 1])
        sums.append(pair_values(weights, pages_ref.at[a], pages_ref.at[b], head_dim))
        total = jnp.where(total > 0.0, total, 1.0)
        inverse.append(1.0 / total)
        log_rows.append(top + jnp.log(total))
    columns = to_columns(inverse)
    keep(0, acc_ref[...], log_ref[0:1])
    for p in range(pairs):
        result = sums[p] * columns[:, p : p + 1]
        keep(2 * p + 1, result[:64], log_rows[p])
        if 2 * p + 1 < others:
            keep(2 * p + 2, result[64:], halves(log_rows[p]))

    value = logs[...]
    lane = lax.broadcasted_iota(jnp.int32, value.shape, 1)
    high = value.astype(jnp.bfloat16).astype(jnp.float32)
    rest = value - high
    middle = rest.astype(jnp.bfloat16).astype(jnp.float32)
    low = rest - middle
    for d in range(n_tp):
        first = (my_tp ^ d) * chunk
        for h in range(chunk):
            rows = results[pl.ds(first + h, n_req, stride=64)]
            out_refs[d][:, h * head_dim : (h + 1) * head_dim] = rows.astype(jnp.bfloat16)
        shift = 128 - first
        stats = jnp.where(lane < chunk, pltpu.roll(high, shift % 128, 1), 0.0)
        stats = jnp.where((lane >= chunk) & (lane < 2 * chunk), pltpu.roll(middle, (shift + chunk) % 128, 1), stats)
        stats = jnp.where((lane >= 2 * chunk) & (lane < 3 * chunk), pltpu.roll(low, (shift + 2 * chunk) % 128, 1), stats)
        out_refs[d][:, chunk * head_dim :] = stats[:n_req].astype(jnp.bfloat16)


def other_attention(q_list, own, n_req, n_tp):
    heads, head_dim = own[0].shape
    chunk = heads // n_tp
    vmem = pl.BlockSpec(memory_space=pltpu.VMEM)
    return pl.pallas_call(
        functools.partial(other_kernel, n_req, n_tp),
        out_shape=[jax.ShapeDtypeStruct((n_req, chunk * head_dim + 128), jnp.bfloat16)] * n_tp,
        in_specs=[vmem] * (n_req + 3),
        out_specs=[vmem] * n_tp,
        scratch_shapes=[
            pltpu.VMEM((n_req * heads, head_dim), jnp.float32),
            pltpu.VMEM((round_up(n_req, 8), 128), jnp.float32),
            pltpu.VMEM((round_up(n_req - 1, 2) // 2, 128, head_dim), jnp.float32),
        ],
        compiler_params=pltpu.CompilerParams(vmem_limit_bytes=16 * MIB),
        cost_estimate=pl.CostEstimate(flops=2 * own[3].size * 16, bytes_accessed=own[3].size * 2, transcendentals=0),
        name="other_attention",
    )(*q_list, *own)


def row_copies(source, first, column, target, sems):
    parts = sems.shape[0]
    step = target.shape[0] // parts
    columns = pl.ds(column, target.shape[1])
    return [
        pltpu.make_async_copy(
            source.at[pl.ds(first + i * step, step), columns], target.at[pl.ds(i * step, step)], sems.at[i]
        )
        for i in range(parts)
    ]


def load_kernel(first, piece_ref, weight_hbm, out_ref, same_ref, sems):
    copies = row_copies(weight_hbm, first, 0, out_ref, sems)
    for copy in copies:
        copy.start()
    same_ref[...] = piece_ref[...]
    for copy in copies:
        copy.wait()


def load_weight(piece, out_weight, first, rows, columns):
    vmem = pl.BlockSpec(memory_space=pltpu.VMEM)
    return pl.pallas_call(
        functools.partial(load_kernel, first),
        out_shape=[
            jax.ShapeDtypeStruct((rows, columns), out_weight.dtype),
            jax.ShapeDtypeStruct(piece.shape, piece.dtype),
        ],
        in_specs=[vmem, pl.BlockSpec(memory_space=pltpu.HBM)],
        out_specs=[vmem] * 2,
        scratch_shapes=[pltpu.SemaphoreType.DMA((4,))],
        compiler_params=pltpu.CompilerParams(vmem_limit_bytes=20 * MIB),
        cost_estimate=pl.CostEstimate(flops=0, bytes_accessed=rows * columns * 4, transcendentals=0),
        name="load_weight",
    )(piece, in_hbm(out_weight))


def project_kernel(n_req, n_tp, *refs):
    part_refs = refs[:n_req]
    upper, lower = refs[n_req : n_req + 2]
    out_refs = refs[n_req + 2 : n_req + 2 + n_tp]
    attention = refs[n_req + 2 + n_tp]
    split, columns = upper.shape
    depth = attention.shape[1]
    chunk = depth // 128
    values = []
    for part in part_refs:
        stats = part[:, depth:].astype(jnp.float32)
        values.append(stats + pltpu.roll(stats, 128 - chunk, 1) + pltpu.roll(stats, 128 - 2 * chunk, 1))
    top = functools.reduce(jnp.maximum, values)
    factors = [jnp.exp(v - top) for v in values]
    total = functools.reduce(jnp.add, factors)
    factors = [f / total for f in factors]
    for h in range(chunk):
        at = slice(h * 128, (h + 1) * 128)
        terms = [part[:, at].astype(jnp.float32) * f[:, h : h + 1] for part, f in zip(part_refs, factors)]
        attention[:, at] = functools.reduce(jnp.add, terms).astype(jnp.bfloat16)

    def put(product, at):
        for i, d in enumerate([0] + far_first(n_tp)):
            out_refs[d][:, at] = product[i * n_req : (i + 1) * n_req].astype(out_refs[d].dtype)

    tile = columns // pl.cdiv(columns, 2048)
    for t in range(0, columns, tile):
        at = slice(t, t + tile)
        product = jnp.dot(attention[:, :split], upper[:, at], preferred_element_type=jnp.float32)
        product += jnp.dot(attention[:, split:], lower[:, at], preferred_element_type=jnp.float32)
        put(product, at)


def project(parts, weights, n_req, n_tp):
    depth = sum(w.shape[0] for w in weights)
    columns = weights[0].shape[1]
    vmem = pl.BlockSpec(memory_space=pltpu.VMEM)
    own = jax.ShapeDtypeStruct((n_req, columns), jnp.float32)
    sent = jax.ShapeDtypeStruct((n_req, columns), jnp.bfloat16)
    rows = n_tp * n_req
    return pl.pallas_call(
        functools.partial(project_kernel, n_req, n_tp),
        out_shape=[own] + [sent] * (n_tp - 1),
        in_specs=[vmem] * (n_req + 2),
        out_specs=[vmem] * n_tp,
        scratch_shapes=[pltpu.VMEM((rows, depth), jnp.bfloat16)],
        compiler_params=pltpu.CompilerParams(vmem_limit_bytes=16 * MIB),
        cost_estimate=pl.CostEstimate(
            flops=2 * rows * depth * columns, bytes_accessed=depth * columns * 2, transcendentals=0
        ),
        name="project",
    )(*parts, *weights)


def on_device(queries, new_kv, cache_pool, page_slot, page_owner, context_len, out_weight):
    n_req = lax.axis_size("req")
    n_tp = lax.axis_size("tp")
    pool = cache_pool[0, 0]
    q_list = [swap(queries, "req", d) for d in far_first(n_req)]
    own = own_attention(queries, new_kv, page_slot, page_owner, context_len, pool, n_req)
    pieces = other_attention(q_list, own, n_req, n_tp)
    depth, columns = out_weight.shape
    early = depth // 8
    swapped = [swap(pieces[d], "tp", d) for d in far_first(n_tp)]
    first, mine = load_weight(pieces[0], out_weight, 0, early, columns)
    arrived = jnp.concatenate([mine] + swapped, axis=0)
    parts = [swap(arrived, "req", d) for d in range(1, n_req)]
    second, mine = load_weight(arrived, out_weight, early, depth - early, columns)
    sums = project([mine] + parts, (first, second), n_req, n_tp)
    total = sums[0]
    for d in far_first(n_tp):
        total = total + swap(sums[d], "tp", d).astype(jnp.float32)
    return total.astype(jnp.bfloat16)


def solution(mesh):
    placed = (
        P(("groups", "tp", "req"), None),
        P(("groups", "tp", "req"), None),
        P(("groups", "tp"), "req", None, None, None, None),
        P(("groups", "tp"), None, None),
        P(("groups", "tp"), None, None),
        P(("groups", "tp"), None),
        P("tp", "req"),
    )
    return jax.shard_map(
        on_device, mesh=mesh, in_specs=placed, out_specs=P(("groups", "tp"), "req"), check_vma=False
    )
```

```python
import functools
import math

import jax
import jax.numpy as jnp
from jax import lax
from jax.experimental import pallas as pl
from jax.experimental.pallas import tpu as pltpu
from jax.sharding import PartitionSpec as P

very_negative = -1e30
MIB = 1 << 20


def swap(x, axis, offset):
    count = lax.axis_size(axis)
    return lax.ppermute(x, axis, [(i, i ^ offset) for i in range(count)])


def far_first(count):
    return list(range(count - 1, 0, -1))


def in_hbm(x):
    return pltpu.with_memory_space_constraint(x, pltpu.HBM)


def round_up(value, step):
    return -(-value // step) * step


def halves(x):
    return pltpu.roll(x, 64, 1)


def lay_rows(target, start, q_ref):
    head_dim = target.shape[1]
    for h in range(64):
        target[start + h : start + h + 1] = q_ref[0:1, h * head_dim : (h + 1) * head_dim].astype(jnp.float32)


def query_tiles(stacked, kv_heads):
    turned = stacked.T
    lane = lax.broadcasted_iota(jnp.int32, turned.shape, 1)
    group = 64 // kv_heads
    return [
        [
            jnp.where((lane >= a * 64 + h * group) & (lane < a * 64 + (h + 1) * group), turned, 0.0).astype(jnp.bfloat16)
            for a in range(2)
        ]
        for h in range(kv_heads)
    ]


def pair_scores(page_a, page_b, tiles, head_dim):
    total = None
    for h in range(len(tiles)):
        for a, page in enumerate((page_a, page_b)):
            part = jnp.dot(page[h, :, :head_dim], tiles[h][a], preferred_element_type=jnp.float32)
            total = part if total is None else total + part
    return total


def pair_softmax(scores, limit):
    token = lax.broadcasted_iota(jnp.int32, scores.shape, 0)
    mask = token < limit
    masked = jnp.where(mask, scores, very_negative)
    top = jnp.max(masked, axis=0, keepdims=True)
    weights = jnp.where(mask, jnp.exp(masked - top), 0.0)
    return top, jnp.sum(weights, axis=0, keepdims=True), weights


def pair_values(weights, page_a, page_b, head_dim):
    turned = weights.T.astype(jnp.bfloat16)
    kv_heads = page_a.shape[0]
    group = 64 // kv_heads
    blocks = []
    for a, page in enumerate((page_a, page_b)):
        for h in range(kv_heads):
            at = a * 64 + h * group
            blocks.append(
                jnp.dot(turned[at : at + group], page[h, :, head_dim:], preferred_element_type=jnp.float32)
            )
    return jnp.concatenate(blocks, axis=0)


def to_columns(rows):
    stacked = jnp.concatenate(rows + [jnp.zeros((128 - len(rows), 128), jnp.float32)], axis=0)
    return stacked.T


def own_kernel(n_req, own_pages, *refs):
    q_hbm, kv_hbm, slot_hbm, owner_hbm, len_hbm, pool_hbm = refs[:6]
    acc_ref, log_ref, limit_ref, pages_ref = refs[6:10]
    q_row, q_heads, kv, slots, owners, lens, pool, small_sem, pool_sem, page_sem = refs[10:]
    slot_count, kv_heads, page_len, width = pool_hbm.shape
    head_dim = width // 2
    entries = slot_hbm.shape[2]
    me = lax.axis_index("req")
    scale = 1.0 / math.sqrt(head_dim)
    small = [
        pltpu.make_async_copy(src, dst, small_sem.at[i])
        for i, (src, dst) in enumerate(
            ((slot_hbm, slots), (owner_hbm, owners), (len_hbm, lens), (kv_hbm, kv), (q_hbm, q_row))
        )
    ]
    for copy in small:
        copy.start()
    whole = pltpu.make_async_copy(pool_hbm, pool, pool_sem)
    whole.start()
    for copy in small:
        copy.wait()

    fetched = []
    lane = lax.broadcasted_iota(jnp.int32, (1, 128), 1)
    limits = []
    for d in range(1, n_req):
        n = me ^ d
        length = lens[0, n]
        slot = jnp.int32(0)
        limit = jnp.int32(0)
        for j in range(entries):
            held = (owners[0, n, j] == me) & (j * page_len < length)
            slot = jnp.where(held, slots[0, n, j], slot)
            limit = jnp.where(held, length - j * page_len, limit)
        copy = pltpu.make_async_copy(pool_hbm.at[slot], pages_ref.at[d - 1], page_sem.at[d - 1])
        copy.start()
        fetched.append(copy)
        limits.append(limit)
    if len(limits) % 2:
        limits.append(jnp.int32(0))
    for p in range(len(limits) // 2):
        limit_ref[p : p + 1] = jnp.where(lane < 64, limits[2 * p], limits[2 * p + 1])

    lay_rows(q_heads, 0, q_row)
    q_heads[64:] = q_heads[:64]
    tiles = query_tiles(q_heads[...], kv_heads)
    my_length = lens[0, me]
    pages, valid = [], []
    for i in range(own_pages):
        held = (owners[0, me, i] == me) & (i * page_len < my_length)
        pages.append(pool.at[jnp.where(held, slots[0, me, i], 0)])
        valid.append(jnp.where(held, my_length - i * page_len, 0))
    if own_pages % 2:
        pages.append(pages[0])
        valid.append(jnp.int32(0))
    pairs = len(pages) // 2

    base = kv_heads * head_dim
    new_k = [kv[0:1, h * head_dim : (h + 1) * head_dim] for h in range(kv_heads)]
    self_score = None
    for h in range(kv_heads):
        both = tiles[h][0] + tiles[h][1]
        part = jnp.dot(jnp.broadcast_to(new_k[h], (16, head_dim)), both, preferred_element_type=jnp.float32)
        self_score = part if self_score is None else self_score + part
    self_score = self_score[0:1] * scale

    whole.wait()
    scores = [pair_scores(pages[2 * p], pages[2 * p + 1], tiles, head_dim) * scale for p in range(pairs)]
    tops, totals, sums = [], [], []
    for p in range(pairs):
        limit = jnp.where(lane < 64, valid[2 * p], valid[2 * p + 1])
        top, total, weights = pair_softmax(scores[p], limit)
        tops.append(top)
        totals.append(total)
        sums.append(pair_values(weights, pages[2 * p], pages[2 * p + 1], head_dim))
    top = functools.reduce(jnp.maximum, tops)
    top = jnp.maximum(jnp.maximum(top, halves(top)), self_score)
    factors = [jnp.exp(t - top) for t in tops]
    own_factor = jnp.exp(self_score - top)
    total = functools.reduce(jnp.add, [f * t for f, t in zip(factors, totals)])
    total = total + halves(total) + own_factor
    columns = to_columns([f / total for f in factors] + [own_factor / total])
    result = None
    for p in range(pairs):
        term = sums[p] * columns[:, p : p + 1]
        result = term if result is None else result + term
    group = 64 // kv_heads
    new_v = jnp.concatenate(
        [
            jnp.broadcast_to(kv[0:1, base + h * head_dim : base + (h + 1) * head_dim].astype(jnp.float32), (group, head_dim))
            for h in range(kv_heads)
        ],
        axis=0,
    )
    acc_ref[...] = result[:64] + result[64:] + columns[:64, pairs : pairs + 1] * new_v
    log_ref[...] = jnp.broadcast_to(top + jnp.log(total), log_ref.shape)
    for copy in fetched:
        copy.wait()


def own_attention(q, new_kv, page_slot, page_owner, context_len, pool, n_req):
    slots, kv_heads, page_len, width = pool.shape
    head_dim = width // 2
    heads = q.shape[1] // head_dim
    own_pages = min(slots, page_slot.shape[2])
    hbm = pl.BlockSpec(memory_space=pltpu.HBM)
    vmem = pl.BlockSpec(memory_space=pltpu.VMEM)
    pair_count = round_up(n_req - 1, 2) // 2
    page_bytes = pool.size * 2 // slots
    return pl.pallas_call(
        functools.partial(own_kernel, n_req, own_pages),
        out_shape=[
            jax.ShapeDtypeStruct((heads, head_dim), jnp.float32),
            jax.ShapeDtypeStruct((8, 128), jnp.float32),
            jax.ShapeDtypeStruct((round_up(pair_count, 8), 128), jnp.int32),
            jax.ShapeDtypeStruct((n_req - 1, kv_heads, page_len, width), pool.dtype),
        ],
        in_specs=[hbm] * 6,
        out_specs=[vmem] * 4,
        scratch_shapes=[
            pltpu.VMEM(q.shape, q.dtype),
            pltpu.VMEM((128, head_dim), jnp.float32),
            pltpu.VMEM(new_kv.shape, new_kv.dtype),
            pltpu.SMEM(page_slot.shape, jnp.int32),
            pltpu.SMEM(page_owner.shape, jnp.int32),
            pltpu.SMEM(context_len.shape, jnp.int32),
            pltpu.VMEM(pool.shape, pool.dtype),
            pltpu.SemaphoreType.DMA((5,)),
            pltpu.SemaphoreType.DMA,
            pltpu.SemaphoreType.DMA((n_req - 1,)),
        ],
        compiler_params=pltpu.CompilerParams(vmem_limit_bytes=16 * MIB),
        cost_estimate=pl.CostEstimate(
            flops=4 * own_pages * page_len * heads * head_dim,
            bytes_accessed=page_bytes * (slots + n_req - 1) * 2,
            transcendentals=0,
        ),
        name="own_attention",
    )(*(in_hbm(x) for x in (q, new_kv, page_slot, page_owner, context_len, pool)))


def other_kernel(n_req, n_tp, *refs):
    q_of = dict(zip(far_first(n_req), refs[: n_req - 1]))
    q_refs = [q_of[d] for d in range(1, n_req)]
    acc_ref, log_ref, limit_ref, pages_ref = refs[n_req - 1 : n_req + 3]
    out_refs = refs[n_req + 3 : n_req + 3 + n_tp]
    results, logs, q_heads = refs[n_req + 3 + n_tp :]
    kv_heads, width = pages_ref.shape[1], pages_ref.shape[3]
    head_dim = width // 2
    chunk = 64 // n_tp
    my_tp = lax.axis_index("tp")
    me = lax.axis_index("req")
    scale = 1.0 / math.sqrt(head_dim)
    others = n_req - 1
    pairs = round_up(others, 2) // 2

    def keep(d, result, log_row):
        n = me ^ d
        results[pl.ds(pl.multiple_of(n * 64, 64), 64)] = result
        logs[pl.ds(n, 1)] = log_row

    logs[...] = jnp.zeros_like(logs)
    scores, members = [], []
    for p in range(pairs):
        a, b = 2 * p, min(2 * p + 1, others - 1)
        members.append((a, b))
        lay_rows(q_heads.at[p], 0, q_refs[a])
        lay_rows(q_heads.at[p], 64, q_refs[b])
        tiles = query_tiles(q_heads[p], kv_heads)
        scores.append(pair_scores(pages_ref.at[a], pages_ref.at[b], tiles, head_dim) * scale)
    sums, inverse, log_rows = [], [], []
    for p in range(pairs):
        a, b = members[p]
        top, total, weights = pair_softmax(scores[p], limit_ref[p : p + 1])
        sums.append(pair_values(weights, pages_ref.at[a], pages_ref.at[b], head_dim))
        total = jnp.where(total > 0.0, total, 1.0)
        inverse.append(1.0 / total)
        log_rows.append(top + jnp.log(total))
    columns = to_columns(inverse)
    keep(0, acc_ref[...], log_ref[0:1])
    for p in range(pairs):
        result = sums[p] * columns[:, p : p + 1]
        keep(2 * p + 1, result[:64], log_rows[p])
        if 2 * p + 1 < others:
            keep(2 * p + 2, result[64:], halves(log_rows[p]))

    value = logs[...]
    lane = lax.broadcasted_iota(jnp.int32, value.shape, 1)
    high = value.astype(jnp.bfloat16).astype(jnp.float32)
    rest = value - high
    middle = rest.astype(jnp.bfloat16).astype(jnp.float32)
    low = rest - middle
    for d in range(n_tp):
        first = (my_tp ^ d) * chunk
        for h in range(chunk):
            rows = results[pl.ds(first + h, n_req, stride=64)]
            out_refs[d][:, h * head_dim : (h + 1) * head_dim] = rows.astype(jnp.bfloat16)
        shift = 128 - first
        stats = jnp.where(lane < chunk, pltpu.roll(high, shift % 128, 1), 0.0)
        stats = jnp.where((lane >= chunk) & (lane < 2 * chunk), pltpu.roll(middle, (shift + chunk) % 128, 1), stats)
        stats = jnp.where((lane >= 2 * chunk) & (lane < 3 * chunk), pltpu.roll(low, (shift + 2 * chunk) % 128, 1), stats)
        out_refs[d][:, chunk * head_dim :] = stats[:n_req].astype(jnp.bfloat16)


def other_attention(q_list, own, n_req, n_tp):
    heads, head_dim = own[0].shape
    chunk = heads // n_tp
    vmem = pl.BlockSpec(memory_space=pltpu.VMEM)
    return pl.pallas_call(
        functools.partial(other_kernel, n_req, n_tp),
        out_shape=[jax.ShapeDtypeStruct((n_req, chunk * head_dim + 128), jnp.bfloat16)] * n_tp,
        in_specs=[vmem] * (n_req + 3),
        out_specs=[vmem] * n_tp,
        scratch_shapes=[
            pltpu.VMEM((n_req * heads, head_dim), jnp.float32),
            pltpu.VMEM((round_up(n_req, 8), 128), jnp.float32),
            pltpu.VMEM((round_up(n_req - 1, 2) // 2, 128, head_dim), jnp.float32),
        ],
        compiler_params=pltpu.CompilerParams(vmem_limit_bytes=16 * MIB),
        cost_estimate=pl.CostEstimate(flops=2 * own[3].size * 16, bytes_accessed=own[3].size * 2, transcendentals=0),
        name="other_attention",
    )(*q_list, *own)


def row_copies(source, first, column, target, sems):
    parts = sems.shape[0]
    step = target.shape[0] // parts
    columns = pl.ds(column, target.shape[1])
    return [
        pltpu.make_async_copy(
            source.at[pl.ds(first + i * step, step), columns], target.at[pl.ds(i * step, step)], sems.at[i]
        )
        for i in range(parts)
    ]


def load_kernel(first, piece_ref, weight_hbm, out_ref, same_ref, sems):
    copies = row_copies(weight_hbm, first, 0, out_ref, sems)
    for copy in copies:
        copy.start()
    same_ref[...] = piece_ref[...]
    for copy in copies:
        copy.wait()


def load_weight(piece, out_weight, first, rows, columns):
    vmem = pl.BlockSpec(memory_space=pltpu.VMEM)
    return pl.pallas_call(
        functools.partial(load_kernel, first),
        out_shape=[
            jax.ShapeDtypeStruct((rows, columns), out_weight.dtype),
            jax.ShapeDtypeStruct(piece.shape, piece.dtype),
        ],
        in_specs=[vmem, pl.BlockSpec(memory_space=pltpu.HBM)],
        out_specs=[vmem] * 2,
        scratch_shapes=[pltpu.SemaphoreType.DMA((4,))],
        compiler_params=pltpu.CompilerParams(vmem_limit_bytes=20 * MIB),
        cost_estimate=pl.CostEstimate(flops=0, bytes_accessed=rows * columns * 4, transcendentals=0),
        name="load_weight",
    )(piece, in_hbm(out_weight))


def project_kernel(n_req, n_tp, *refs):
    part_refs = refs[:n_req]
    upper, lower = refs[n_req : n_req + 2]
    out_refs = refs[n_req + 2 : n_req + 2 + n_tp]
    attention = refs[n_req + 2 + n_tp]
    split, columns = upper.shape
    depth = attention.shape[1]
    chunk = depth // 128
    values = []
    for part in part_refs:
        stats = part[:, depth:].astype(jnp.float32)
        values.append(stats + pltpu.roll(stats, 128 - chunk, 1) + pltpu.roll(stats, 128 - 2 * chunk, 1))
    top = functools.reduce(jnp.maximum, values)
    factors = [jnp.exp(v - top) for v in values]
    total = functools.reduce(jnp.add, factors)
    factors = [f / total for f in factors]
    for h in range(chunk):
        at = slice(h * 128, (h + 1) * 128)
        terms = [part[:, at].astype(jnp.float32) * f[:, h : h + 1] for part, f in zip(part_refs, factors)]
        attention[:, at] = functools.reduce(jnp.add, terms).astype(jnp.bfloat16)

    def put(product, at):
        for i, d in enumerate([0] + far_first(n_tp)):
            out_refs[d][:, at] = product[i * n_req : (i + 1) * n_req].astype(out_refs[d].dtype)

    tile = columns // pl.cdiv(columns, 2048)
    for t in range(0, columns, tile):
        at = slice(t, t + tile)
        product = jnp.dot(attention[:, :split], upper[:, at], preferred_element_type=jnp.float32)
        product += jnp.dot(attention[:, split:], lower[:, at], preferred_element_type=jnp.float32)
        put(product, at)


def project(parts, weights, n_req, n_tp):
    depth = sum(w.shape[0] for w in weights)
    columns = weights[0].shape[1]
    vmem = pl.BlockSpec(memory_space=pltpu.VMEM)
    own = jax.ShapeDtypeStruct((n_req, columns), jnp.float32)
    sent = jax.ShapeDtypeStruct((n_req, columns), jnp.bfloat16)
    rows = n_tp * n_req
    return pl.pallas_call(
        functools.partial(project_kernel, n_req, n_tp),
        out_shape=[own] + [sent] * (n_tp - 1),
        in_specs=[vmem] * (n_req + 2),
        out_specs=[vmem] * n_tp,
        scratch_shapes=[pltpu.VMEM((rows, depth), jnp.bfloat16)],
        compiler_params=pltpu.CompilerParams(vmem_limit_bytes=16 * MIB),
        cost_estimate=pl.CostEstimate(
            flops=2 * rows * depth * columns, bytes_accessed=depth * columns * 2, transcendentals=0
        ),
        name="project",
    )(*parts, *weights)


def on_device(queries, new_kv, cache_pool, page_slot, page_owner, context_len, out_weight):
    n_req = lax.axis_size("req")
    n_tp = lax.axis_size("tp")
    pool = cache_pool[0, 0]
    q_list = [swap(queries, "req", d) for d in far_first(n_req)]
    own = own_attention(queries, new_kv, page_slot, page_owner, context_len, pool, n_req)
    pieces = other_attention(q_list, own, n_req, n_tp)
    depth, columns = out_weight.shape
    early = depth // 4
    swapped = [swap(pieces[d], "tp", d) for d in far_first(n_tp)]
    first, mine = load_weight(pieces[0], out_weight, 0, early, columns)
    arrived = jnp.concatenate([mine] + swapped, axis=0)
    parts = [swap(arrived, "req", d) for d in range(1, n_req)]
    second, mine = load_weight(arrived, out_weight, early, depth - early, columns)
    sums = project([mine] + parts, (first, second), n_req, n_tp)
    total = sums[0]
    for d in far_first(n_tp):
        total = total + swap(sums[d], "tp", d).astype(jnp.float32)
    return total.astype(jnp.bfloat16)


def solution(mesh):
    placed = (
        P(("groups", "tp", "req"), None),
        P(("groups", "tp", "req"), None),
        P(("groups", "tp"), "req", None, None, None, None),
        P(("groups", "tp"), None, None),
        P(("groups", "tp"), None, None),
        P(("groups", "tp"), None),
        P("tp", "req"),
    )
    return jax.shard_map(
        on_device, mesh=mesh, in_specs=placed, out_specs=P(("groups", "tp"), "req"), check_vma=False
    )
```
